32 devices in a mesh: gz: 2 (over x), bx: 2 (over y), by: 8 (over z, core).
Axes of the slice: x: 2, y: 2, z: 4, core: 2. Of those that a mesh axis runs over, the one named last changes fastest.
Arguments:
- observed: float32 [64, 128, 1024], P('gz', 'bx', 'by'), may hold values from 0.02 to 50.2
- psf_z: float32 [65], replicated, may hold values from 0.003 to 1.11
- psf_x: float32 [65], replicated, may hold values from 0.003 to 1.11
- psf_y: float32 [65], replicated, may hold values from 0.003 to 1.11
Outputs:
- estimate: float32 [64, 128, 1024], P('gz', 'bx', 'by')
The draws below stay inside these ranges and needn't reach their ends.
All inputs are finite; a program needn't handle non-finite values.
Results may differ from the reference program's by a relative error of at most 0.00002.
Values sent between devices are 32-bit elements; how exact they have to be, the bound alone decides.
No kernel may reach another device: no remote copies, remote signals or barrier semaphores. Data moves between devices by JAX's collectives and lax.ppermute only.
A program may use at most 64 MiB of HBM per device.

```python
import math
import jax
import jax.numpy as jnp
from jax import lax

TAPS = 65
ITERS = 2
NZ = 64
NX = 128
NY = 1024


def draw_observed(key, part):
    folded = jax.random.fold_in(key, 101)
    key_rough, key_bright, key_level = jax.random.split(folded, 3)
    shape = (NZ, NX, NY)
    rough = jnp.exp(jax.random.uniform(key_rough, shape, jnp.float32, math.log(0.02), math.log(0.2)))
    background = rough
    chance = 0.005
    level = jnp.exp(jax.random.uniform(key_level, shape, jnp.float32, 0.0, math.log(50.0)))
    bright = jax.random.bernoulli(key_bright, chance, shape)
    return (background + jnp.where(bright, level, 0.0)).astype(jnp.float32)


def psf_taps(key):
    key_width, key_floor, key_shift, key_jitter = jax.random.split(key, 4)
    spread = (TAPS - 1) / 8.0 * jax.random.uniform(key_width, (), jnp.float32, 1.0, 1.5)
    floor_level = jax.random.uniform(key_floor, (), jnp.float32, 0.003, 0.01)
    offset = jax.random.uniform(key_shift, (), jnp.float32, -0.5, 0.5)
    place = jnp.arange(TAPS, dtype=jnp.float32) - (TAPS - 1) / 2.0 - offset
    jitter = jax.random.uniform(key_jitter, (TAPS,), jnp.float32, 0.9, 1.1)
    return (jnp.exp(-place * place / (2.0 * spread * spread)) * jitter + floor_level).astype(jnp.float32)


def draw_psf_z(key, part):
    return psf_taps(jax.random.fold_in(key, 211))


def draw_psf_x(key, part):
    return psf_taps(jax.random.fold_in(key, 223))


def draw_psf_y(key, part):
    return psf_taps(jax.random.fold_in(key, 227))


def setup_inputs(seed: int = 0) -> dict:
    seeds = jax.random.split(jax.random.key(seed), 5)
    return {
        "observed": draw_observed(jax.random.fold_in(seeds[4], 71), 0),
        "psf_z": draw_psf_z(jax.random.fold_in(seeds[4], 71), 0),
        "psf_x": draw_psf_x(jax.random.fold_in(seeds[4], 71), 0),
        "psf_y": draw_psf_y(jax.random.fold_in(seeds[4], 71), 0),
    }


def pass_axis(extended, kernel, axis_dim, length):
    result = kernel[0] * lax.slice_in_dim(extended, 0, length, axis=axis_dim)
    for offset in range(1, kernel.shape[0]):
        result = result + kernel[offset] * lax.slice_in_dim(extended, offset, offset + length, axis=axis_dim)
    return result


def pad_axis(field, radius, axis_dim):
    widths = [(0, 0), (0, 0), (0, 0)]
    widths[axis_dim] = (radius, radius)
    return jnp.pad(field, widths)


def blur(field, kernel_z, kernel_x, kernel_y):
    radius = kernel_z.shape[0] // 2
    for axis_dim, kernel in ((0, kernel_z), (1, kernel_x), (2, kernel_y)):
        field = pass_axis(pad_axis(field, radius, axis_dim), kernel, axis_dim, field.shape[axis_dim])
    return field


def reference(observed, psf_z, psf_x, psf_y):
    kernel_z = psf_z / jnp.sum(psf_z)
    kernel_x = psf_x / jnp.sum(psf_x)
    kernel_y = psf_y / jnp.sum(psf_y)
    estimate = observed
    for sweep in range(ITERS):
        blurred = blur(estimate, kernel_z, kernel_x, kernel_y)
        quotient = observed / blurred
        estimate = estimate * blur(quotient, kernel_z[::-1], kernel_x[::-1], kernel_y[::-1])
    return estimate
```

```python
import functools
import jax
import jax.numpy as jnp
from jax import lax
from jax.experimental import pallas as pl
from jax.experimental.pallas import tpu as pltpu
from jax.sharding import PartitionSpec as P

ITERS = 2
LANES = 128
F32 = jnp.float32
BF16 = jnp.bfloat16
VMEM = pl.BlockSpec(memory_space=pltpu.VMEM)
SMEM = pl.BlockSpec(memory_space=pltpu.SMEM)
PARAMS = pltpu.CompilerParams(vmem_limit_bytes=40 * 1024 * 1024)


def shaped(*shape):
    return jax.ShapeDtypeStruct(shape, F32)


def split(value):
    high = value.astype(BF16)
    return high, (value - high.astype(F32)).astype(BF16)


def dot(left, right):
    return lax.dot_general(left, right, (((1,), (0,)), ((), ())), preferred_element_type=F32)


def banded(taps, rows, width, start):
    room = (width + 2 * LANES - 1) // LANES * LANES
    base = jnp.concatenate([taps, jnp.zeros((1, room - LANES), F32)], axis=1)
    base = jnp.broadcast_to(base, (rows, room))
    return pltpu.roll(base, start % room, 1, stride=1, stride_axis=0)[:, :width]


def taps_kernel(psf_ref, out_ref):
    count = psf_ref.shape[1]
    row = lax.broadcasted_iota(jnp.int32, (LANES, LANES), 0)
    lane = lax.broadcasted_iota(jnp.int32, (LANES, LANES), 1)
    out_ref[...] = jnp.zeros_like(out_ref)
    for d in range(3):
        raw = psf_ref[d : d + 1, :]
        taps = raw / jnp.sum(raw, axis=1, keepdims=True)
        taps = jnp.concatenate([taps, jnp.zeros((1, LANES - count), F32)], axis=1)
        column = jnp.transpose(jnp.broadcast_to(taps, (LANES, LANES)))
        turned = jnp.sum(jnp.where(row + lane == count - 1, column, 0.0), axis=0, keepdims=True)
        out_ref[2 * d : 2 * d + 1, :] = taps
        out_ref[2 * d + 1 : 2 * d + 2, :] = turned


def turn_kernel(radius, chunk, where_ref, block_ref, own_ref, first_ref, last_ref, *part_refs):
    length, columns = block_ref.shape
    for at in range(0, length, LANES):
        own_ref[:, at : at + LANES] = jnp.transpose(block_ref[at : at + LANES, :])
    first_ref[...] = own_ref[:radius, :]
    last_ref[...] = own_ref[columns - radius :, :]
    for slot, part_ref in enumerate(part_refs):
        place = pl.multiple_of(where_ref[slot] * chunk, chunk)
        part_ref[...] = own_ref[pl.ds(place, chunk), :]


def ordered_rows(matrix, where_ref, order_ref, chunk):
    order_ref[1] = matrix
    for slot in range(matrix.shape[0] // chunk):
        place = pl.multiple_of(where_ref[slot] * chunk, chunk)
        order_ref[0, pl.ds(slot * chunk, chunk), :] = order_ref[1, pl.ds(place, chunk), :]
    return order_ref[0]


def left_product(stacked, high_rows, value):
    high, low = split(value)
    both = dot(stacked, high)
    return both[:high_rows] + (both[high_rows:] + dot(stacked[:high_rows], low))


def stack(matrix):
    return jnp.concatenate(split(matrix), axis=0)


def first_y_kernel(chunk, where_ref, taps_ref, own_ref, low_ref, high_ref, *refs):
    part_refs, order_ref = refs[:-1], refs[-1]
    columns, length = own_ref.shape
    radius = low_ref.shape[0]
    matrix = banded(taps_ref[4:5, :], columns, columns + 2 * radius, 0)
    matrix = stack(ordered_rows(matrix, where_ref, order_ref, chunk))
    step = 2 * LANES
    for at in range(0, length, step):
        here = slice(at, at + step)
        field = jnp.concatenate([low_ref[:, here], own_ref[:, here], high_ref[:, here]], axis=0)
        result = left_product(matrix, columns, field)
        for slot, part_ref in enumerate(part_refs):
            part_ref[:, here] = result[slot * chunk : (slot + 1) * chunk]


def gather_kernel(span, chunk, where_ref, *refs):
    count = where_ref.shape[0] // 2
    part_refs, (own_ref, first_ref, last_ref) = refs[:count], refs[count:]
    columns = own_ref.shape[0]
    for slot, part_ref in enumerate(part_refs):
        place = pl.multiple_of(where_ref[count + slot] * chunk, chunk)
        own_ref[pl.ds(place, chunk), :] = part_ref[...]
    first_ref[...] = own_ref[:span, :]
    last_ref[...] = own_ref[columns - span :, :]


def middle_y_kernel(chunk, where_ref, taps_ref, own_ref, low_ref, high_ref, seen_ref, seen_low_ref, seen_high_ref,
                    estimate_ref, *refs):
    part_refs, order_ref = refs[:-1], refs[-1]
    columns, length = own_ref.shape
    radius = seen_low_ref.shape[0]
    wide = columns + 2 * radius
    back = stack(banded(taps_ref[5:6, :], wide, wide + 2 * radius, 0))
    matrix = banded(taps_ref[4:5, :], columns, wide, 0)
    matrix = stack(ordered_rows(matrix, where_ref, order_ref, chunk))
    step = 2 * LANES
    for at in range(0, length, step):
        here = slice(at, at + step)
        field = jnp.concatenate([low_ref[:, here], own_ref[:, here], high_ref[:, here]], axis=0)
        seen = jnp.concatenate([seen_low_ref[:, here], seen_ref[:, here], seen_high_ref[:, here]], axis=0)
        estimate = seen * left_product(back, wide, field)
        estimate_ref[:, here] = estimate[radius : radius + columns]
        result = left_product(matrix, columns, estimate)
        for slot, part_ref in enumerate(part_refs):
            part_ref[:, here] = result[slot * chunk : (slot + 1) * chunk]


def last_y_kernel(taps_ref, own_ref, low_ref, high_ref, estimate_ref, out_ref):
    columns, length = own_ref.shape
    radius = low_ref.shape[0]
    back = stack(banded(taps_ref[5:6, :], columns, columns + 2 * radius, 0))
    step = 2 * LANES
    for at in range(0, length, step):
        here = slice(at, at + step)
        field = jnp.concatenate([low_ref[:, here], own_ref[:, here], high_ref[:, here]], axis=0)
        estimate = estimate_ref[:, here] * left_product(back, columns, field)
        for tile in range(0, step, LANES):
            out_ref[at + tile : at + tile + LANES, :] = jnp.transpose(estimate[:, tile : tile + LANES])


def put_rows(ref, lines, value):
    for tile in range(ref.shape[0]):
        ref[tile, lines, :] = value[:, tile * LANES : (tile + 1) * LANES]


def get_rows(ref, lines):
    return jnp.concatenate([ref[tile, lines, :] for tile in range(ref.shape[0])], axis=1)


def seen_kernel(sizes, where_ref, *refs):
    groups, beside, rows = sizes
    part_refs, out_ref, held_ref = refs[:-2], refs[-2], refs[-1]
    chunk, length = part_refs[0].shape
    tiles = length // LANES
    per = LANES // rows
    fill(sizes, where_ref, part_refs, held_ref)
    for at in range(groups * tiles):
        for k in range(per):
            pieces = [held_ref[b, at * chunk : (at + 1) * chunk, k * rows : (k + 1) * rows] for b in range(beside)]
            place = (at * per + k) * chunk
            put_rows(out_ref, slice(place, place + chunk), jnp.concatenate(pieces, axis=1))


def fill(sizes, where_ref, part_refs, held_ref):
    groups, beside, rows = sizes
    chunk, length = part_refs[0].shape
    tiles = length // LANES
    for slot, part_ref in enumerate(part_refs):
        dz, dx = slot // beside, slot % beside
        source_z = lax.rem(where_ref[0] + groups - dz, groups)
        source_x = lax.rem(where_ref[1] + beside - dx, beside)
        for t in range(tiles):
            place = pl.multiple_of((source_z * tiles + t) * chunk, chunk)
            held_ref[source_x, pl.ds(place, chunk), :] = part_ref[:, t * LANES : (t + 1) * LANES]


def planes_kernel(sizes, radius, where_ref, taps_ref, seen_ref, *refs):
    groups, beside, rows = sizes
    count = groups * beside
    part_refs, out_refs = refs[:count], refs[count : 2 * count]
    held_ref, field_ref, other_ref, weight_ref = refs[2 * count :]
    chunk, length = part_refs[0].shape
    tiles = length // LANES
    per = LANES // rows
    width = beside * rows
    planes = groups * tiles * per
    fill(sizes, where_ref, part_refs, held_ref)

    forward = banded(taps_ref[3:4, :], width, width, -radius)
    blocks = []
    for b in range(beside):
        for k in range(per):
            line = [jnp.zeros((rows, width), F32)] * per
            line[k] = forward[b * rows : (b + 1) * rows]
            blocks.append(jnp.concatenate(line, axis=1))
    high, low = split(jnp.concatenate(blocks, axis=0))
    both = jnp.concatenate([high, low], axis=1)
    group = min(tiles, max(1, 256 // chunk))
    for at in range(0, groups * tiles, group):
        here = slice(at * chunk, (at + group) * chunk)
        left = jnp.concatenate([held_ref[b, here, :] for b in range(beside)], axis=1)
        left_high, left_low = split(left)
        result = dot(left_high, both)
        result = result[:, : per * width] + (result[:, per * width :] + dot(left_low, high))
        for g in range(group):
            for k in range(per):
                place = ((at + g) * per + k) * chunk
                part = result[g * chunk : (g + 1) * chunk, k * width : (k + 1) * width]
                put_rows(field_ref, slice(place, place + chunk), part)

    def doubled(matrix):
        high, low = split(matrix)
        return jnp.concatenate(
            [jnp.concatenate([high, high], axis=1), jnp.concatenate([low, jnp.zeros_like(low)], axis=1)], axis=0
        )

    ahead = doubled(banded(taps_ref[0:1, :], planes, planes, -radius))
    back = doubled(banded(taps_ref[1:2, :], planes, planes, -radius))

    def over_planes(matrix, value):
        result = dot(matrix, jnp.concatenate(split(value), axis=0))
        return result[:planes] + result[planes:]

    for y in range(0, chunk, 2):
        lines = [pl.ds(y + k, planes, stride=chunk) for k in range(2)]
        value = jnp.concatenate([get_rows(field_ref, line) for line in lines], axis=1)
        seen = jnp.concatenate([get_rows(seen_ref, line) for line in lines], axis=1)
        value = over_planes(back, seen / over_planes(ahead, value))
        for k, line in enumerate(lines):
            put_rows(other_ref, line, value[:, k * width : (k + 1) * width])

    turned = banded(taps_ref[2:3, :], width, width, -radius)
    for b in range(beside):
        blocks = []
        for k in range(per):
            line = [jnp.zeros((width, rows), F32)] * per
            line[k] = turned[:, b * rows : (b + 1) * rows]
            blocks.append(jnp.concatenate(line, axis=1))
        high, low = split(jnp.concatenate(blocks, axis=0))
        weight_ref[b] = jnp.concatenate([high, low], axis=1)
    for dz in range(groups):
        target_z = lax.rem(where_ref[0] + dz, groups)
        for at in range(0, tiles, group):
            pieces = []
            for g in range(group):
                line = []
                for k in range(per):
                    place = pl.multiple_of(((target_z * tiles + at + g) * per + k) * chunk, chunk)
                    line.append(get_rows(other_ref, pl.ds(place, chunk)))
                pieces.append(jnp.concatenate(line, axis=1))
            left_high, left_low = split(jnp.concatenate(pieces, axis=0))
            for dx in range(beside):
                target_x = lax.rem(where_ref[1] + dx, beside)
                result = dot(left_high, weight_ref[target_x])
                result = result[:, :LANES] + (result[:, LANES:] + dot(left_low, weight_ref[target_x][:, :LANES]))
                for g in range(group):
                    out_refs[dz * beside + dx][:, (at + g) * LANES : (at + g + 1) * LANES] = result[
                        g * chunk : (g + 1) * chunk
                    ]


def per_device(observed, psf_z, psf_x, psf_y):
    groups, beside = lax.axis_size("gz"), lax.axis_size("bx")
    along = lax.axis_size("by")
    count = groups * beside
    planes, rows, columns = observed.shape
    length = planes * rows
    chunk = columns // count
    radius = psf_z.shape[0] // 2
    sizes = (groups, beside, rows)
    me_z, me_x = lax.axis_index("gz"), lax.axis_index("bx")
    offsets = [(dz, dx) for dz in range(groups) for dx in range(beside)]
    place = jnp.stack([me_z, me_x]).astype(jnp.int32)
    ahead = [lax.rem(me_z + dz, groups) * beside + lax.rem(me_x + dx, beside) for dz, dx in offsets]
    behind = [
        lax.rem(me_z + groups - dz, groups) * beside + lax.rem(me_x + beside - dx, beside) for dz, dx in offsets
    ]
    where = jnp.stack(ahead + behind).astype(jnp.int32)

    def exchanged(parts):
        result = [parts[0]]
        for (dz, dx), part in list(zip(offsets, parts))[1:]:
            pairs = [
                (z * beside + x, ((z + dz) % groups) * beside + (x + dx) % beside)
                for z in range(groups)
                for x in range(beside)
            ]
            result.append(lax.ppermute(part, ("gz", "bx"), pairs))
        return result

    def from_sides(first, last):
        up = [(i, i + 1) for i in range(along - 1)]
        down = [(i + 1, i) for i in range(along - 1)]
        return lax.ppermute(last, "by", up), lax.ppermute(first, "by", down)

    part = shaped(chunk, length)
    whole = shaped(columns, length)

    def call(kernel, outs, specs, scratch=()):
        return pl.pallas_call(
            kernel,
            out_shape=outs,
            in_specs=specs,
            out_specs=jax.tree.map(lambda _: VMEM, outs),
            scratch_shapes=list(scratch),
            compiler_params=PARAMS,
        )

    seen, first, last, *parts = call(
        functools.partial(turn_kernel, radius, chunk),
        [whole, shaped(radius, length), shaped(radius, length)] + [part] * count,
        [SMEM, VMEM],
    )(where, observed.reshape(length, columns))
    seen_low, seen_high = from_sides(first, last)
    seen_parts = exchanged(parts)
    taps = call(taps_kernel, shaped(8, LANES), [VMEM])(jnp.stack([psf_z, psf_x, psf_y]))

    order = pltpu.VMEM((2, columns, columns + 2 * radius), F32)
    parts = call(
        functools.partial(first_y_kernel, chunk), [part] * count, [SMEM] + [VMEM] * 4, [order]
    )(where, taps, seen, seen_low, seen_high)
    parts = exchanged(parts)

    lines = groups * planes * chunk
    across = (beside * rows // LANES, lines, LANES)
    held = pltpu.VMEM((beside, groups * (length // LANES) * chunk, LANES), F32)
    seen_across = call(
        functools.partial(seen_kernel, sizes), shaped(*across), [SMEM] + [VMEM] * count, [held]
    )(place, *seen_parts)

    def through_planes(parts):
        return call(
            functools.partial(planes_kernel, sizes, radius),
            [part] * count,
            [SMEM] + [VMEM] * (2 + count),
            [
                held,
                pltpu.VMEM(across, F32),
                pltpu.VMEM(across, F32),
                pltpu.VMEM((beside, beside * LANES, 2 * LANES), BF16),
            ],
        )(place, taps, seen_across, *parts)

    def gathered(parts, span):
        own, first, last = call(
            functools.partial(gather_kernel, span, chunk),
            [whole, shaped(span, length), shaped(span, length)],
            [SMEM] + [VMEM] * count,
        )(where, *parts)
        return own, *from_sides(first, last)

    estimate = seen
    estimate_low, estimate_high = seen_low, seen_high
    for sweep in range(ITERS):
        parts = exchanged(through_planes(parts))
        if sweep < ITERS - 1:
            own, low, high = gathered(parts, 2 * radius)
            estimate, *parts = call(
                functools.partial(middle_y_kernel, chunk), [whole] + [part] * count, [SMEM] + [VMEM] * 7, [order]
            )(where, taps, own, low, high, estimate, estimate_low, estimate_high)
            parts = exchanged(parts)
        else:
            own, low, high = gathered(parts, radius)
            out = call(last_y_kernel, shaped(length, columns), [VMEM] * 5)(taps, own, low, high, estimate)
    return out.reshape(planes, rows, columns)


def solution(mesh):
    placed = (P("gz", "bx", "by"), P(), P(), P())
    return jax.shard_map(
        per_device, mesh=mesh, in_specs=placed, out_specs=P("gz", "bx", "by"), check_vma=False
    )
```

```python
import functools
import jax
import jax.numpy as jnp
from jax import lax
from jax.experimental import pallas as pl
from jax.experimental.pallas import tpu as pltpu
from jax.sharding import PartitionSpec as P

LANES = 128
RATE = 1150 * 1000 * 1000
STEP = 2 * LANES
F32 = jnp.float32
BF16 = jnp.bfloat16
VMEM = pl.BlockSpec(memory_space=pltpu.VMEM)
SMEM = pl.BlockSpec(memory_space=pltpu.SMEM)


def shaped(*shape):
    return jax.ShapeDtypeStruct(shape, F32)


def call(cost, kernel, outs, specs, scratch=()):
    return pl.pallas_call(
        kernel,
        out_shape=outs,
        in_specs=specs,
        out_specs=jax.tree.map(lambda _: VMEM, outs),
        scratch_shapes=list(scratch),
        compiler_params=pltpu.CompilerParams(vmem_limit_bytes=40 * 1024 * 1024),
        cost_estimate=pl.CostEstimate(flops=int(cost * RATE), bytes_accessed=0, transcendentals=0),
    )


def parts_of(columns, radius, count):
    outer = [(0, radius), (columns - radius, radius)]
    inner = [(radius, columns - 2 * radius)]
    fits = columns >= 3 * radius and count % 2 == 0
    for runs in (outer, inner):
        fits = fits and sum(size for _, size in runs) % (8 * count) == 0
    return [outer, inner] if fits else [[(0, columns)]]


def size_of(runs):
    return sum(size for _, size in runs)


def rows_of(value, runs):
    return jnp.concatenate([value[start : start + size] for start, size in runs], axis=0)


def place_of(runs, offset):
    place, before = runs[0][0] + offset, 0
    for (start, size), (after, _) in zip(runs, runs[1:]):
        before += size
        place = jnp.where(offset >= before, after - before + offset, place)
    return place


def split(value):
    high = value.astype(BF16)
    return high, (value - high.astype(F32)).astype(BF16)


def dot(left, right):
    return lax.dot_general(left, right, (((1,), (0,)), ((), ())), preferred_element_type=F32)


def banded(taps, rows, width, start):
    room = (width + 2 * LANES - 1) // LANES * LANES
    base = jnp.concatenate([taps, jnp.zeros((1, room - LANES), F32)], axis=1)
    base = jnp.broadcast_to(base, (rows, room))
    return pltpu.roll(base, start % room, 1, stride=1, stride_axis=0)[:, :width]


def stack(matrix):
    return jnp.concatenate(split(matrix), axis=0)


def left_product(stacked, value):
    rows = stacked.shape[0] // 2
    high, low = split(value)
    both = dot(stacked, high)
    return both[:rows] + (both[rows:] + dot(stacked[:rows], low))


def ordered_rows(matrix, where_ref, order_ref, runs, count):
    size = size_of(runs)
    chunk = size // count
    width = matrix.shape[1]
    order_ref[0, :size, :width] = rows_of(matrix, runs)
    for slot in range(count):
        place = pl.multiple_of(where_ref[slot] * chunk, chunk)
        order_ref[1, slot * chunk : (slot + 1) * chunk, :width] = order_ref[0, pl.ds(place, chunk), :width]
    return order_ref[1, :size, :width]


def taps_of(psf_ref):
    count = psf_ref.shape[1]
    row = lax.broadcasted_iota(jnp.int32, (LANES, LANES), 0)
    lane = lax.broadcasted_iota(jnp.int32, (LANES, LANES), 1)
    taps = psf_ref[...] / jnp.sum(psf_ref[...], axis=1, keepdims=True)
    taps = jnp.concatenate([taps, jnp.zeros((1, LANES - count), F32)], axis=1)
    column = jnp.transpose(jnp.broadcast_to(taps, (LANES, LANES)))
    return taps, jnp.sum(jnp.where(row + lane == count - 1, column, 0.0), axis=0, keepdims=True)


def weights_kernel(sizes, psf_z_ref, psf_x_ref, rows_ahead_ref, rows_back_ref, planes_ahead_ref, planes_back_ref):
    groups, beside, radius, depth, rows = sizes
    per = LANES // rows
    width = beside * rows
    taps, turned = taps_of(psf_x_ref)
    ahead = banded(turned, width, width, -radius)
    back = banded(taps, width, width, -radius)
    blocks = []
    for b in range(beside):
        for k in range(per):
            line = [jnp.zeros((rows, width), F32)] * per
            line[k] = ahead[b * rows : (b + 1) * rows]
            blocks.append(jnp.concatenate(line, axis=1))
    rows_ahead_ref[...] = jnp.concatenate(split(jnp.concatenate(blocks, axis=0)), axis=1)
    for b in range(beside):
        blocks = []
        for k in range(per):
            line = [jnp.zeros((width, rows), F32)] * per
            line[k] = back[:, b * rows : (b + 1) * rows]
            blocks.append(jnp.concatenate(line, axis=1))
        rows_back_ref[b] = jnp.concatenate(split(jnp.concatenate(blocks, axis=0)), axis=1)
    planes = groups * depth
    for ref, line in zip((planes_ahead_ref, planes_back_ref), taps_of(psf_z_ref)):
        high, low = split(banded(line, planes, planes, -radius))
        ref[...] = jnp.concatenate(
            [jnp.concatenate([high, high], axis=1), jnp.concatenate([low, jnp.zeros_like(low)], axis=1)], axis=0
        )


def send_sides(where_ref, count, value_ref, span, sibling_ref, other_ref):
    odd = where_ref[2 * count]
    room = value_ref.shape[0] - span
    sibling_ref[...] = value_ref[pl.ds(pl.multiple_of((1 - odd) * room, 8), span), :]
    other_ref[...] = value_ref[pl.ds(pl.multiple_of(odd * room, 8), span), :]


def start_kernel(parts, radius, count, where_ref, psf_ref, block_ref, *refs):
    own_ref, sibling_ref, other_ref, taps_ref = refs[:4]
    part_refs, order_ref = refs[4:-1], refs[-1]
    length, columns = block_ref.shape
    for at in range(0, length, LANES):
        own_ref[:, at : at + LANES] = jnp.transpose(block_ref[at : at + LANES, :])
    send_sides(where_ref, count, own_ref, radius, sibling_ref, other_ref)
    taps, turned = taps_of(psf_ref)
    taps_ref[...] = jnp.concatenate([taps, turned, jnp.zeros((6, LANES), F32)], axis=0)
    before = 0
    for k, runs in reversed(list(enumerate(parts))):
        chunk = size_of(runs) // count
        for slot, part_ref in enumerate(part_refs):
            place = pl.multiple_of(place_of(runs, where_ref[slot] * chunk), 8)
            part_ref[before : before + chunk, :] = own_ref[pl.ds(place, chunk), :]
        before += chunk
        if k:
            matrix = banded(taps, columns, columns, -radius)
            matrix = stack(ordered_rows(matrix, where_ref, order_ref, runs, count))
            for at in range(0, length, STEP):
                here = slice(at, at + STEP)
                result = left_product(matrix, own_ref[:, here])
                for slot, part_ref in enumerate(part_refs):
                    part_ref[before : before + chunk, here] = result[slot * chunk : (slot + 1) * chunk]
            before += chunk


def first_y_kernel(runs, radius, where_ref, taps_ref, own_ref, sibling_ref, other_ref, *refs):
    part_refs, order_ref = refs[:-1], refs[-1]
    columns, length = own_ref.shape
    count = len(part_refs)
    chunk = size_of(runs) // count
    matrix = banded(taps_ref[0:1, :], columns, columns + 2 * radius, 0)
    matrix = stack(ordered_rows(matrix, where_ref, order_ref, runs, count))
    odd = where_ref[2 * count] == 1
    for at in range(0, length, STEP):
        here = slice(at, at + STEP)
        field = assembled([[(0, columns)]], odd, [own_ref], [(sibling_ref, other_ref)], here)
        result = left_product(matrix, field)
        for slot, part_ref in enumerate(part_refs):
            part_ref[:, here] = result[slot * chunk : (slot + 1) * chunk]


def put_chunks(where_ref, count, part_refs, own_ref):
    chunk = part_refs[0].shape[0]
    for slot, part_ref in enumerate(part_refs):
        place = pl.multiple_of(where_ref[count + slot] * chunk, chunk)
        own_ref[pl.ds(place, chunk), :] = part_ref[...]


def gather_kernel(span, where_ref, *refs):
    sides = 2 if span else 0
    count = len(refs) - 2 - sides
    part_refs, own_ref = refs[:count], refs[count + 1]
    put_chunks(where_ref, count, part_refs, own_ref)
    if span:
        send_sides(where_ref, count, own_ref, span, *refs[count + 2 :])


def assembled(parts, odd, own_refs, side_refs, here):
    total = max(start + size for runs in parts for start, size in runs)
    pieces = {}
    for runs, ref in zip(parts, own_refs):
        at = 0
        for start, size in runs:
            pieces[start] = ref[at : at + size] if isinstance(ref, jax.Array) else ref[at : at + size, here]
            at += size
    own = [pieces[start] for start in sorted(pieces)]
    low, high = [], []
    for sibling_ref, other_ref in side_refs:
        sibling, other = sibling_ref[:, here], other_ref[:, here]
        low.insert(0, jnp.where(odd, sibling, other))
        high.append(jnp.where(odd, other, sibling))
    return jnp.concatenate(low + own + high, axis=0)


def middle_y_kernel(parts, radius, count, where_ref, taps_ref, *refs):
    kinds = len(parts)
    own_refs, refs = refs[:kinds], refs[kinds:]
    side_refs, refs = [refs[2 * k : 2 * k + 2] for k in range(kinds)], refs[2 * kinds :]
    seen_ref, seen_sibling_ref, seen_other_ref, estimate_ref = refs[:4]
    part_refs, order_ref = refs[4:-1], refs[-1]
    columns, length = seen_ref.shape
    wide = columns + 2 * radius
    odd = where_ref[2 * count] == 1
    back = stack(banded(taps_ref[1:2, :], wide, wide + 2 * radius, 0))
    matrix = banded(taps_ref[0:1, :], columns, wide, 0)
    rows = [ordered_rows(matrix, where_ref, order_ref, runs, count) for runs in parts]
    matrix = stack(jnp.concatenate(rows, axis=0))
    for at in range(0, length, STEP):
        here = slice(at, at + STEP)
        seen = assembled([[(0, columns)]], odd, [seen_ref], [(seen_sibling_ref, seen_other_ref)], here)
        estimate = seen * left_product(back, assembled(parts, odd, own_refs, side_refs, here))
        estimate_ref[:, here] = estimate[radius : radius + columns]
        result = left_product(matrix, estimate)
        place = 0
        for part_ref in part_refs:
            chunk = part_ref.shape[0]
            part_ref[:, here] = result[place : place + chunk]
            place += chunk


def inner_y_kernel(parts, radius, count, where_ref, taps_ref, outer_ref, estimate_ref, *refs):
    part_refs, (own_ref, out_ref) = refs[:count], refs[count:]
    put_chunks(where_ref, count, part_refs, own_ref)
    columns, length = estimate_ref.shape
    ((start, size),) = parts[1]
    back = stack(banded(taps_ref[1:2, :], size, columns, start - radius))
    for at in range(0, length, STEP):
        here = slice(at, at + STEP)
        field = assembled(parts, None, [outer_ref, own_ref], [], here)
        out_ref[:, here] = estimate_ref[start : start + size, here] * left_product(back, field)


def last_y_kernel(parts, radius, count, where_ref, taps_ref, *refs):
    kinds = len(parts)
    sibling_ref, other_ref, estimate_ref, *refs, out_ref = refs
    own_refs, ready_refs = refs[:kinds], refs[kinds:]
    columns, length = estimate_ref.shape
    odd = where_ref[2 * count] == 1
    back = stack(rows_of(banded(taps_ref[1:2, :], columns, columns + 2 * radius, 0), parts[0]))
    for at in range(0, length, STEP):
        here = slice(at, at + STEP)
        field = assembled(parts, odd, own_refs, [(sibling_ref, other_ref)], here)
        outer = rows_of(estimate_ref[:, here], parts[0]) * left_product(back, field)
        estimate = assembled(parts, None, [outer, *ready_refs], [], here)
        for tile in range(0, STEP, LANES):
            out_ref[at + tile : at + tile + LANES, :] = jnp.transpose(estimate[:, tile : tile + LANES])


def put_lines(ref, lines, value):
    for tile in range(ref.shape[0]):
        ref[tile, lines, :] = value[:, tile * LANES : (tile + 1) * LANES]


def get_lines(ref, lines):
    return jnp.concatenate([ref[tile, lines, :] for tile in range(ref.shape[0])], axis=1)


def fill(sizes, where_ref, part_refs, first, chunk, held_ref):
    groups, beside = sizes[:2]
    count = groups * beside
    tiles = part_refs[0].shape[1] // LANES
    for slot, part_ref in enumerate(part_refs):
        dz, dx = slot // beside, slot % beside
        source_z = lax.rem(where_ref[2 * count + 1] + groups - dz, groups)
        source_x = lax.rem(where_ref[2 * count + 2] + beside - dx, beside)
        for t in range(tiles):
            place = pl.multiple_of((source_z * tiles + t) * chunk, chunk)
            held_ref[source_x, pl.ds(place, chunk), :] = part_ref[first : first + chunk, t * LANES : (t + 1) * LANES]


def planes_kernel(
    sizes, first, seen_first, where_ref, rows_ahead_ref, rows_back_ref, planes_ahead_ref, planes_back_ref, *refs
):
    groups, beside, _, _, rows = sizes
    count = groups * beside
    part_refs, refs = refs[:count], refs[count:]
    begins = seen_first is not None
    if begins:
        seen_refs, refs = refs[:count], refs[count:]
        out_refs, (mark_ref, seen_ref, held_ref, field_ref, other_ref) = refs[:count], refs[count:]
    else:
        seen_ref, out_refs, (mark_ref, held_ref, field_ref, other_ref) = refs[0], refs[1 : count + 1], refs[count + 1 :]
    mark_ref[...] = jnp.zeros_like(mark_ref)
    chunk, length = out_refs[0].shape
    tiles = length // LANES
    per = LANES // rows
    width = beside * rows
    planes = groups * tiles * per
    if begins:
        fill(sizes, where_ref, seen_refs, seen_first, chunk, held_ref)
        for at in range(groups * tiles):
            for k in range(per):
                lines = slice(at * chunk, (at + 1) * chunk)
                pieces = [held_ref[b, lines, k * rows : (k + 1) * rows] for b in range(beside)]
                place = (at * per + k) * chunk
                put_lines(seen_ref, slice(place, place + chunk), jnp.concatenate(pieces, axis=1))
    fill(sizes, where_ref, part_refs, first, chunk, held_ref)

    across = per * width
    group = min(tiles, max(1, STEP // chunk))
    for at in range(0, groups * tiles, group):
        here = slice(at * chunk, (at + group) * chunk)
        high, low = split(jnp.concatenate([held_ref[b, here, :] for b in range(beside)], axis=1))
        result = dot(high, rows_ahead_ref[...])
        result = result[:, :across] + (result[:, across:] + dot(low, rows_ahead_ref[:, :across]))
        for g in range(group):
            for k in range(per):
                place = ((at + g) * per + k) * chunk
                part = result[g * chunk : (g + 1) * chunk, k * width : (k + 1) * width]
                put_lines(field_ref, slice(place, place + chunk), part)

    def over_planes(matrix_ref, value):
        result = dot(matrix_ref[...], jnp.concatenate(split(value), axis=0))
        return result[:planes] + result[planes:]

    for y in range(0, chunk, 2):
        lines = [pl.ds(y + k, planes, stride=chunk) for k in range(2)]
        value = jnp.concatenate([get_lines(field_ref, line) for line in lines], axis=1)
        seen = jnp.concatenate([get_lines(seen_ref, line) for line in lines], axis=1)
        value = over_planes(planes_back_ref, seen / over_planes(planes_ahead_ref, value))
        for k, line in enumerate(lines):
            put_lines(other_ref, line, value[:, k * width : (k + 1) * width])

    for dz in range(groups):
        target_z = lax.rem(where_ref[2 * count + 1] + dz, groups)
        for at in range(0, tiles, group):
            pieces = []
            for g in range(group):
                line = []
                for k in range(per):
                    place = pl.multiple_of(((target_z * tiles + at + g) * per + k) * chunk, chunk)
                    line.append(get_lines(other_ref, pl.ds(place, chunk)))
                pieces.append(jnp.concatenate(line, axis=1))
            high, low = split(jnp.concatenate(pieces, axis=0))
            for dx in range(beside):
                target_x = lax.rem(where_ref[2 * count + 2] + dx, beside)
                result = dot(high, rows_back_ref[target_x])
                result = result[:, :LANES] + (result[:, LANES:] + dot(low, rows_back_ref[target_x][:, :LANES]))
                for g in range(group):
                    out_refs[dz * beside + dx][:, (at + g) * LANES : (at + g + 1) * LANES] = result[
                        g * chunk : (g + 1) * chunk
                    ]


def per_device(observed, psf_z, psf_x, psf_y):
    groups, beside, along = (lax.axis_size(axis) for axis in ("gz", "bx", "by"))
    count = groups * beside
    planes, rows, columns = observed.shape
    length = planes * rows
    radius = psf_z.shape[0] // 2
    sizes = (groups, beside, radius, planes, rows)
    width = beside * rows
    parts = parts_of(columns, radius, count)
    chunks = [size_of(runs) // count for runs in parts]

    me_z, me_x = lax.axis_index("gz"), lax.axis_index("bx")
    offsets = [(dz, dx) for dz in range(groups) for dx in range(beside)]
    ahead = [lax.rem(me_z + dz, groups) * beside + lax.rem(me_x + dx, beside) for dz, dx in offsets]
    behind = [
        lax.rem(me_z + groups - dz, groups) * beside + lax.rem(me_x + beside - dx, beside) for dz, dx in offsets
    ]
    where = jnp.stack(ahead + behind + [lax.rem(lax.axis_index("by"), 2), me_z, me_x]).astype(jnp.int32)

    def exchanged(values):
        result = [values[0]]
        for (dz, dx), value in list(zip(offsets, values))[1:]:
            pairs = [
                (z * beside + x, ((z + dz) % groups) * beside + (x + dx) % beside)
                for z in range(groups)
                for x in range(beside)
            ]
            result.append(lax.ppermute(value, ("gz", "bx"), pairs))
        return result

    def from_sides(sibling, other):
        result = []
        for value, first in ((other, 1), (sibling, 0)):
            pairs = [(i, i + 1) for i in range(first, along - 1, 2)]
            result.append(lax.ppermute(value, "by", pairs + [(j, i) for i, j in pairs]))
        return result[1], result[0]

    line = (1, psf_z.shape[0])
    matrix = jax.ShapeDtypeStruct((2 * groups * planes,) * 2, BF16)
    order = pltpu.VMEM((2, columns, columns + 2 * radius), F32)
    block = sum(chunks)
    seen, sibling, other, taps, *parcels = call(
            1.3,
        functools.partial(start_kernel, parts, radius, count),
        [shaped(columns, length), shaped(radius, length), shaped(radius, length), shaped(8, LANES)]
        + [shaped(block + sum(chunks[1:]), length)] * count,
        [SMEM, VMEM, VMEM],
        [order],
    )(where, psf_y.reshape(line), observed.reshape(length, columns))
    seen_sides = from_sides(sibling, other)
    parcels = exchanged(parcels)
    weights = call(
            0.4,
        functools.partial(weights_kernel, sizes),
        [
            jax.ShapeDtypeStruct((beside * LANES, 2 * LANES // rows * width), BF16),
            jax.ShapeDtypeStruct((beside, LANES // rows * width, 2 * LANES), BF16),
            matrix,
            matrix,
        ],
        [VMEM] * 2,
    )(psf_z.reshape(line), psf_x.reshape(line))
    outer = exchanged(
        call(
            1.1,
            functools.partial(first_y_kernel, parts[0], radius),
            [shaped(chunks[0], length)] * count,
            [SMEM] + [VMEM] * 4,
            [order],
        )(where, taps, seen, *seen_sides)
    )

    def through_planes(values, first, chunk, seen_values, seen_first=None):
        lines = groups * planes * chunk
        across = (width // LANES, lines, LANES)
        begins = seen_first is not None
        result = call(
            50,
            functools.partial(planes_kernel, sizes, first, seen_first),
            [shaped(chunk, length)] * count + [shaped(8, LANES)] + [shaped(*across)] * begins,
            [SMEM] + [VMEM] * (4 + len(values) + len(seen_values)),
            [
                pltpu.VMEM((beside, groups * (length // LANES) * chunk, LANES), F32),
                pltpu.VMEM(across, F32),
                pltpu.VMEM(across, F32),
            ],
        )(where, *weights, *values, *seen_values)
        return result[:count], result[count], result[count + 1 :] if begins else seen_values

    def gathered(values, chunk, span, mark):
        own, *sides = call(
            0.6,
            functools.partial(gather_kernel, span),
            [shaped(chunk * count, length)] + [shaped(span, length)] * (2 if span else 0),
            [SMEM] + [VMEM] * count + [pl.BlockSpec(memory_space=pl.ANY)],
        )(where, *values, mark)
        return own, from_sides(*sides) if span else []

    fields, across, owns, sides = ([None] * len(parts) for _ in range(4))
    before = 0
    for k in reversed(range(len(parts))):
        values, first = (parcels, before + chunks[k]) if k else (outer, 0)
        fields[k], mark, across[k] = through_planes(values, first, chunks[k], parcels, before)
        fields[k] = exchanged(fields[k])
        before += chunks[k] * (2 if k else 1)
    for k in reversed(range(len(parts))):
        owns[k], sides[k] = gathered(fields[k], chunks[k], 2 * radius // len(parts), mark)
    estimate, *parcels = call(
            3.5,
        functools.partial(middle_y_kernel, parts, radius, count),
        [shaped(columns, length)] + [shaped(chunk, length) for chunk in chunks for _ in range(count)],
        [SMEM] + [VMEM] * (4 + 3 * len(parts)),
        [order],
    )(where, taps, *owns, *[side for pair in sides for side in pair], seen, *seen_sides)
    for k in range(len(parts)):
        fields[k] = exchanged(parcels[k * count : (k + 1) * count])
    for k in range(len(parts)):
        values, mark, _ = through_planes(fields[k], 0, chunks[k], across[k])
        fields[k] = exchanged(values)
    own, sides = gathered(fields[0], chunks[0], radius, mark)
    owns, ready = [own], []
    if len(parts) > 1:
        inner = shaped(size_of(parts[1]), length)
        inner, result = call(
            50,
            functools.partial(inner_y_kernel, parts, radius, count), [inner, inner], [SMEM] + [VMEM] * (3 + count)
        )(where, taps, own, estimate, *fields[1])
        owns, ready = [own, inner], [result]
    out = call(
            2.2,
        functools.partial(last_y_kernel, parts, radius, count),
        shaped(length, columns),
        [SMEM] + [VMEM] * (3 + 2 * len(parts)),
    )(where, taps, *sides, estimate, *owns, *ready)
    return out.reshape(planes, rows, columns)


def solution(mesh):
    placed = (P("gz", "bx", "by"), P(), P(), P())
    return jax.shard_map(
        per_device, mesh=mesh, in_specs=placed, out_specs=P("gz", "bx", "by"), check_vma=False
    )
```

```python
import functools
import jax
import jax.numpy as jnp
from jax import lax
from jax.experimental import pallas as pl
from jax.experimental.pallas import tpu as pltpu
from jax.sharding import PartitionSpec as P

LANES = 128
RATE = 1150 * 1000 * 1000
STEP = 4 * LANES
F32 = jnp.float32
BF16 = jnp.bfloat16
VMEM = pl.BlockSpec(memory_space=pltpu.VMEM)
SMEM = pl.BlockSpec(memory_space=pltpu.SMEM)
ANY = pl.BlockSpec(memory_space=pl.ANY)
HBM = pl.BlockSpec(memory_space=pltpu.HBM)


def shaped(*shape):
    return jax.ShapeDtypeStruct(shape, F32)


def stays(value):
    return pltpu.with_memory_space_constraint(value, pltpu.HBM)


def call(cost, kernel, outs, specs, scratch=(), place=VMEM):
    return pl.pallas_call(
        kernel,
        out_shape=outs,
        in_specs=specs,
        out_specs=jax.tree.map(lambda _: place, outs),
        scratch_shapes=list(scratch),
        compiler_params=pltpu.CompilerParams(vmem_limit_bytes=40 * 1024 * 1024),
        cost_estimate=pl.CostEstimate(flops=int(cost * RATE), bytes_accessed=0, transcendentals=0),
    )


def parts_of(columns, radius, count):
    outer = [(0, radius), (columns - radius, radius)]
    inner = [(radius, columns - 2 * radius)]
    fits = columns >= 3 * radius and count % 2 == 0
    for runs in (outer, inner):
        fits = fits and sum(size for _, size in runs) % (8 * count) == 0
    return [outer, inner] if fits else [[(0, columns)]]


def flat(lists):
    return [value for values in lists for value in values]


def size_of(runs):
    return sum(size for _, size in runs)


def rows_of(value, runs):
    return jnp.concatenate([value[start : start + size] for start, size in runs], axis=0)


def place_of(runs, offset):
    place, before = runs[0][0] + offset, 0
    for (start, size), (after, _) in zip(runs, runs[1:]):
        before += size
        place = jnp.where(offset >= before, after - before + offset, place)
    return place


def offsets_of(groups, beside):
    offsets = [(dz, dx) for dz in range(groups) for dx in range(beside)]
    return offsets[:1] + sorted(offsets[1:], key=lambda offset: offset.count(0))


def split(value):
    high = value.astype(BF16)
    return high, (value - high.astype(F32)).astype(BF16)


def dot(left, right):
    return lax.dot_general(left, right, (((1,), (0,)), ((), ())), preferred_element_type=F32)


def banded(taps, rows, width, start):
    room = (width + 2 * LANES - 1) // LANES * LANES
    base = jnp.concatenate([taps, jnp.zeros((1, room - LANES), F32)], axis=1)
    base = jnp.broadcast_to(base, (rows, room))
    return pltpu.roll(base, start % room, 1, stride=1, stride_axis=0)[:, :width]


def as_left(matrix):
    high, low = split(matrix)
    return jnp.concatenate([high, high, low], axis=1)


def left_product(matrix, value):
    high, low = split(value)
    return dot(matrix, jnp.concatenate([high, low, high], axis=0))


def as_right(matrix):
    high, low = split(matrix)
    return jnp.concatenate([high, high, low], axis=0)


def right_product(value, matrix):
    high, low = split(value)
    return dot(jnp.concatenate([high, low, high], axis=1), matrix)


def ordered_rows(matrix, where_ref, order_ref, runs, count):
    size = size_of(runs)
    chunk = size // count
    width = matrix.shape[1]
    order_ref[0, :size, :width] = rows_of(matrix, runs)
    for slot in range(count):
        place = pl.multiple_of(where_ref[slot] * chunk, chunk)
        order_ref[1, slot * chunk : (slot + 1) * chunk, :width] = order_ref[0, pl.ds(place, chunk), :width]
    return order_ref[1, :size, :width]


def columns_of(matrix, runs):
    return jnp.concatenate([matrix[:, start : start + size] for start, size in runs], axis=1)


def taps_of(psf_ref):
    count = psf_ref.shape[1]
    row = lax.broadcasted_iota(jnp.int32, (LANES, LANES), 0)
    lane = lax.broadcasted_iota(jnp.int32, (LANES, LANES), 1)
    taps = psf_ref[...] / jnp.sum(psf_ref[...], axis=1, keepdims=True)
    taps = jnp.concatenate([taps, jnp.zeros((1, LANES - count), F32)], axis=1)
    column = jnp.transpose(jnp.broadcast_to(taps, (LANES, LANES)))
    return taps, jnp.sum(jnp.where(row + lane == count - 1, column, 0.0), axis=0, keepdims=True)


def weights_kernel(
    sizes,
    parts,
    where_ref,
    psf_z_ref,
    psf_x_ref,
    psf_y_ref,
    first_ref,
    back_early_ref,
    back_late_ref,
    ahead_early_ref,
    ahead_late_ref,
    end_early_ref,
    end_late_ref,
    rows_ahead_ref,
    rows_back_ref,
    planes_ahead_ref,
    planes_back_ref,
    order_ref,
):
    groups, beside, radius, depth, rows, columns = sizes
    count = groups * beside
    taps, turned = taps_of(psf_y_ref)
    wide = columns + 2 * radius
    span = 2 * radius // len(parts)
    edges = [(0, 2 * radius), (wide - 2 * radius, 2 * radius)]

    ahead = banded(taps, columns, wide, 0)
    ahead = jnp.concatenate([ordered_rows(ahead, where_ref, order_ref, runs, count) for runs in parts], axis=0)
    first_ref[...] = as_left(ahead[: size_of(parts[0])])
    ahead_early_ref[...] = as_left(ahead[:, 2 * radius : columns])
    ahead_late_ref[...] = as_left(columns_of(ahead, edges))
    back = banded(turned, wide, wide + 2 * radius, 0)
    late = [(2 * radius - span, span), (columns + 2 * radius, span)]
    early = [(0, 2 * radius - span), (2 * radius, columns), (columns + 2 * radius + span, 2 * radius - span)]
    back_early_ref[...] = as_left(columns_of(back, [run for run in early if run[1]]))
    back_late_ref[...] = as_left(columns_of(rows_of(back, edges), late))
    back = banded(turned, columns, wide, 0)
    end_early_ref[...] = as_left(back[:, radius : radius + columns])
    edges = [(0, radius), (columns - radius, radius)]
    end_late_ref[...] = as_left(columns_of(rows_of(back, edges), [(0, radius), (columns + radius, radius)]))

    per = LANES // rows
    width = beside * rows
    taps, turned = taps_of(psf_x_ref)
    ahead = banded(turned, width, width, -radius)
    back = banded(taps, width, width, -radius)
    blocks = []
    for b in range(beside):
        for k in range(per):
            line = [jnp.zeros((rows, width), F32)] * per
            line[k] = ahead[b * rows : (b + 1) * rows]
            blocks.append(jnp.concatenate(line, axis=1))
    rows_ahead_ref[...] = as_right(jnp.concatenate(blocks, axis=0))
    for b in range(beside):
        blocks = []
        for k in range(per):
            line = [jnp.zeros((width, rows), F32)] * per
            line[k] = back[:, b * rows : (b + 1) * rows]
            blocks.append(jnp.concatenate(line, axis=1))
        slot = lax.rem(b + beside - where_ref[2 * count + 2], beside)
        rows_back_ref[:, pl.ds(pl.multiple_of(slot * LANES, LANES), LANES)] = as_right(jnp.concatenate(blocks, axis=0))
    planes = groups * depth
    for ref, line in zip((planes_ahead_ref, planes_back_ref), taps_of(psf_z_ref)):
        ref[...] = as_left(banded(line, planes, planes, -radius))


def send_sides(where_ref, count, value_ref, span, sibling_ref, other_ref):
    odd = where_ref[2 * count]
    room = value_ref.shape[0] - span
    sibling_ref[...] = value_ref[pl.ds(pl.multiple_of((1 - odd) * room, 8), span), :]
    other_ref[...] = value_ref[pl.ds(pl.multiple_of(odd * room, 8), span), :]


def start_kernel(parts, radius, count, where_ref, psf_hbm, block_hbm, *refs):
    own_ref, sibling_ref, other_ref = refs[:3]
    part_refs, (order_ref, psf_ref, block_ref, sems) = refs[3:-4], refs[-4:]
    length, columns = block_ref.shape
    pieces = sems.shape[0] - 1
    piece = length // pieces
    copies = [pltpu.make_async_copy(psf_hbm, psf_ref, sems.at[pieces])]
    for k in range(pieces):
        here = pl.ds(k * piece, piece)
        copies.append(pltpu.make_async_copy(block_hbm.at[here], block_ref.at[here], sems.at[k]))
    for copy in copies:
        copy.start()
    copies[0].wait()
    taps, _ = taps_of(psf_ref)
    matrices = [None]
    for runs in parts[1:]:
        matrix = banded(taps, columns, columns, -radius)
        matrices.append(as_left(ordered_rows(matrix, where_ref, order_ref, runs, count)))
    for k in range(pieces):
        copies[k + 1].wait()
        for at in range(k * piece, (k + 1) * piece, LANES):
            own_ref[:, at : at + LANES] = jnp.transpose(block_ref[at : at + LANES, :])
    send_sides(where_ref, count, own_ref, radius, sibling_ref, other_ref)
    before = 0
    for k, runs in reversed(list(enumerate(parts))):
        chunk = size_of(runs) // count
        for slot, part_ref in enumerate(part_refs):
            place = pl.multiple_of(place_of(runs, where_ref[slot] * chunk), 8)
            part_ref[before : before + chunk, :] = own_ref[pl.ds(place, chunk), :]
        before += chunk
        if k:
            for at in range(0, length, STEP):
                here = slice(at, at + STEP)
                result = left_product(matrices[k], own_ref[:, here])
                for slot, part_ref in enumerate(part_refs):
                    part_ref[before : before + chunk, here] = result[slot * chunk : (slot + 1) * chunk]
            before += chunk


def first_y_kernel(where_ref, matrix_ref, own_ref, other_ref, sibling_ref, *part_refs):
    columns, length = own_ref.shape
    count = len(part_refs)
    chunk = part_refs[0].shape[0]
    odd = where_ref[2 * count] == 1
    for at in range(0, length, STEP):
        here = slice(at, at + STEP)
        field = assembled([[(0, columns)]], odd, [own_ref], [(other_ref, sibling_ref)], here)
        result = left_product(matrix_ref[...], field)
        for slot, part_ref in enumerate(part_refs):
            part_ref[:, here] = result[slot * chunk : (slot + 1) * chunk]


def put_parts(where_ref, count, part_refs, own_refs):
    for k, own_ref in enumerate(own_refs):
        for slot, part_ref in enumerate(part_refs[k * count : (k + 1) * count]):
            chunk = part_ref.shape[0]
            place = pl.multiple_of(where_ref[count + slot] * chunk, chunk)
            own_ref[pl.ds(place, chunk), :] = part_ref[...]


def sides_kernel(count, where_ref, *refs):
    part_refs, (_, sibling_ref, other_ref) = refs[:count], refs[count:]
    span = sibling_ref.shape[0]
    chunk = part_refs[0].shape[0]
    odd = where_ref[2 * count]
    for slot, part_ref in enumerate(part_refs):
        start = where_ref[count + slot] * chunk
        for first, to_sibling in ((0, odd), (count * chunk - span, 1 - odd)):
            inside = (start >= first) & (start < first + span)

            def put(ref, start=start, first=first, part_ref=part_ref):
                ref[pl.ds(pl.multiple_of(start - first, 8), chunk), :] = part_ref[...]

            pl.when(inside & (to_sibling == 1))(functools.partial(put, sibling_ref))
            pl.when(inside & (to_sibling == 0))(functools.partial(put, other_ref))


def assembled(parts, odd, own_refs, side_refs, here):
    pieces = {}
    for runs, ref in zip(parts, own_refs):
        at = 0
        for start, size in runs:
            pieces[start] = ref[at : at + size] if isinstance(ref, jax.Array) else ref[at : at + size, here]
            at += size
    own = [pieces[start] for start in sorted(pieces)]
    low, high = [], []
    for other_ref, sibling_ref in side_refs:
        sibling, other = sibling_ref[:, here], other_ref[:, here]
        low.insert(0, jnp.where(odd, sibling, other))
        high.append(jnp.where(odd, other, sibling))
    return jnp.concatenate(low + own + high, axis=0)


def middle_early_kernel(parts, radius, count, where_ref, back_ref, ahead_ref, *refs):
    kinds = len(parts)
    own_refs, refs = refs[-kinds:], refs[:-kinds]
    put_parts(where_ref, count, refs, own_refs)
    refs = refs[kinds * count :]
    side_refs = [refs[2 * k : 2 * k + 2] for k in range(kinds - 1)]
    seen_ref, outer_ref, inner_ref, result_ref = refs[2 * kinds - 2 :]
    columns, length = seen_ref.shape
    wide = columns + 2 * radius
    edges = [(0, 2 * radius), (wide - 2 * radius, 2 * radius)]
    odd = where_ref[2 * count] == 1
    for at in range(0, length, STEP):
        here = slice(at, at + STEP)
        blurred = left_product(back_ref[...], assembled(parts, odd, own_refs, side_refs, here))
        outer_ref[:, here] = rows_of(blurred, edges)
        inner = seen_ref[radius : columns - radius, here] * blurred[2 * radius : columns]
        inner_ref[:, here] = inner
        result_ref[:, here] = left_product(ahead_ref[...], inner)


def middle_late_kernel(parts, radius, count, where_ref, back_ref, ahead_ref, *refs):
    (other_ref, sibling_ref, outer_ref, inner_ref, result_ref), refs = refs[:5], refs[5:]
    seen_ref, seen_other_ref, seen_sibling_ref, estimate_ref, *part_refs = refs
    columns, length = seen_ref.shape
    wide = columns + 2 * radius
    edges = [(0, 2 * radius), (wide - 2 * radius, 2 * radius)]
    odd = where_ref[2 * count] == 1
    for at in range(0, length, STEP):
        here = slice(at, at + STEP)
        sides = assembled([], odd, [], [(other_ref, sibling_ref)], here)
        seen = assembled([[(0, columns)]], odd, [seen_ref], [(seen_other_ref, seen_sibling_ref)], here)
        outer = rows_of(seen, edges) * (outer_ref[:, here] + left_product(back_ref[...], sides))
        estimate_ref[:, here] = jnp.concatenate(
            [outer[radius : 2 * radius], inner_ref[:, here], outer[2 * radius : 3 * radius]], axis=0
        )
        result = result_ref[:, here] + left_product(ahead_ref[...], outer)
        place = 0
        for part_ref in part_refs:
            chunk = part_ref.shape[0]
            part_ref[:, here] = result[place : place + chunk]
            place += chunk


def last_early_kernel(parts, radius, count, where_ref, back_ref, estimate_ref, *refs):
    outer_ref, inner_ref, *own_refs = refs[len(parts) * count :]
    put_parts(where_ref, count, refs, own_refs)
    columns, length = estimate_ref.shape
    edges = [(0, radius), (columns - radius, radius)]
    for at in range(0, length, STEP):
        here = slice(at, at + STEP)
        blurred = left_product(back_ref[...], assembled(parts, None, own_refs, [], here))
        outer_ref[:, here] = rows_of(blurred, edges)
        inner_ref[:, here] = estimate_ref[radius : columns - radius, here] * blurred[radius : columns - radius]


def last_late_kernel(
    radius, count, where_ref, back_ref, other_ref, sibling_ref, outer_ref, inner_ref, estimate_ref, out_hbm, out_ref, sems
):
    columns, length = estimate_ref.shape
    odd = where_ref[2 * count] == 1
    edges = [(0, radius), (columns - radius, radius)]
    pieces = sems.shape[0]
    piece = length // pieces
    copies = []
    for at in range(0, length, STEP):
        here = slice(at, at + STEP)
        sides = assembled([], odd, [], [(other_ref, sibling_ref)], here)
        outer = rows_of(estimate_ref[:, here], edges) * (outer_ref[:, here] + left_product(back_ref[...], sides))
        estimate = jnp.concatenate([outer[:radius], inner_ref[:, here], outer[radius:]], axis=0)
        for tile in range(0, STEP, LANES):
            out_ref[at + tile : at + tile + LANES, :] = jnp.transpose(estimate[:, tile : tile + LANES])
        if (at + STEP) % piece == 0:
            k = at // piece
            lines = pl.ds(k * piece, piece)
            copies.append(pltpu.make_async_copy(out_ref.at[lines], out_hbm.at[lines], sems.at[k]))
            copies[-1].start()
    for copy in copies:
        copy.wait()


def put_lines(ref, lines, value):
    for tile in range(ref.shape[0]):
        ref[tile, lines, :] = value[:, tile * LANES : (tile + 1) * LANES]


def get_lines(ref, lines):
    return jnp.concatenate([ref[tile, lines, :] for tile in range(ref.shape[0])], axis=1)


def fill(sizes, where_ref, part_refs, first, chunk, held_ref):
    groups, beside = sizes[:2]
    count = groups * beside
    tiles = part_refs[0].shape[1] // LANES
    for (dz, dx), part_ref in zip(offsets_of(groups, beside), part_refs):
        source_z = lax.rem(where_ref[2 * count + 1] + groups - dz, groups)
        source_x = lax.rem(where_ref[2 * count + 2] + beside - dx, beside)
        for t in range(tiles):
            place = pl.multiple_of((source_z * tiles + t) * chunk, chunk)
            held_ref[source_x, pl.ds(place, chunk), :] = part_ref[first : first + chunk, t * LANES : (t + 1) * LANES]


def planes_kernel(
    sizes, first, seen_first, where_ref, rows_ahead_ref, rows_back_ref, planes_ahead_ref, planes_back_ref, *refs
):
    groups, beside, _, _, rows, _ = sizes
    count = groups * beside
    part_refs, refs = refs[:count], refs[count:]
    begins = seen_first is not None
    if begins:
        seen_refs, refs = refs[:count], refs[count:]
        out_refs, (mark_ref, seen_ref, held_ref, field_ref, other_ref) = refs[:count], refs[count:]
    else:
        seen_ref, out_refs, (mark_ref, held_ref, field_ref, other_ref) = refs[0], refs[1 : count + 1], refs[count + 1 :]
    mark_ref[...] = jnp.zeros_like(mark_ref)
    chunk, length = out_refs[0].shape
    tiles = length // LANES
    per = LANES // rows
    width = beside * rows
    planes = groups * tiles * per
    if begins:
        fill(sizes, where_ref, seen_refs, seen_first, chunk, held_ref)
        for at in range(groups * tiles):
            for k in range(per):
                lines = slice(at * chunk, (at + 1) * chunk)
                pieces = [held_ref[b, lines, k * rows : (k + 1) * rows] for b in range(beside)]
                place = (at * per + k) * chunk
                put_lines(seen_ref, slice(place, place + chunk), jnp.concatenate(pieces, axis=1))
    fill(sizes, where_ref, part_refs, first, chunk, held_ref)

    group = min(tiles, max(1, 4 * LANES // chunk))
    for at in range(0, groups * tiles, group):
        here = slice(at * chunk, (at + group) * chunk)
        left = jnp.concatenate([held_ref[b, here, :] for b in range(beside)], axis=1)
        result = right_product(left, rows_ahead_ref[...])
        for g in range(group):
            for k in range(per):
                place = ((at + g) * per + k) * chunk
                part = result[g * chunk : (g + 1) * chunk, k * width : (k + 1) * width]
                put_lines(field_ref, slice(place, place + chunk), part)

    for y in range(0, chunk, 2):
        lines = [pl.ds(y + k, planes, stride=chunk) for k in range(2)]
        value = jnp.concatenate([get_lines(field_ref, line) for line in lines], axis=1)
        seen = jnp.concatenate([get_lines(seen_ref, line) for line in lines], axis=1)
        value = left_product(planes_back_ref[...], seen / left_product(planes_ahead_ref[...], value))
        for k, line in enumerate(lines):
            put_lines(other_ref, line, value[:, k * width : (k + 1) * width])

    offsets = offsets_of(groups, beside)
    for dz in range(groups):
        target_z = lax.rem(where_ref[2 * count + 1] + dz, groups)
        for at in range(0, tiles, group):
            pieces = []
            for g in range(group):
                line = []
                for k in range(per):
                    place = pl.multiple_of(((target_z * tiles + at + g) * per + k) * chunk, chunk)
                    line.append(get_lines(other_ref, pl.ds(place, chunk)))
                pieces.append(jnp.concatenate(line, axis=1))
            left = jnp.concatenate(pieces, axis=0)
            result = right_product(left, rows_back_ref[...])
            for dx in range(beside):
                for g in range(group):
                    out_refs[offsets.index((dz, dx))][:, (at + g) * LANES : (at + g + 1) * LANES] = result[
                        g * chunk : (g + 1) * chunk, dx * LANES : (dx + 1) * LANES
                    ]


def per_device(observed, psf_z, psf_x, psf_y):
    groups, beside, along = (lax.axis_size(axis) for axis in ("gz", "bx", "by"))
    count = groups * beside
    planes, rows, columns = observed.shape
    length = planes * rows
    radius = psf_z.shape[0] // 2
    sizes = (groups, beside, radius, planes, rows, columns)
    width = beside * rows
    parts = parts_of(columns, radius, count)
    chunks = [size_of(runs) // count for runs in parts]

    me_z, me_x = lax.axis_index("gz"), lax.axis_index("bx")
    offsets = offsets_of(groups, beside)
    ahead = [lax.rem(me_z + dz, groups) * beside + lax.rem(me_x + dx, beside) for dz, dx in offsets]
    behind = [
        lax.rem(me_z + groups - dz, groups) * beside + lax.rem(me_x + beside - dx, beside) for dz, dx in offsets
    ]
    where = jnp.stack(ahead + behind + [lax.rem(lax.axis_index("by"), 2), me_z, me_x]).astype(jnp.int32)

    def exchanged(values):
        result = [values[0]]
        for (dz, dx), value in list(zip(offsets, values))[1:]:
            pairs = [
                (z * beside + x, ((z + dz) % groups) * beside + (x + dx) % beside)
                for z in range(groups)
                for x in range(beside)
            ]
            result.append(lax.ppermute(value, ("gz", "bx"), pairs))
        return result

    def from_sides(sibling, other):
        result = []
        for value, first in ((other, 1), (sibling, 0)):
            pairs = [(i, i + 1) for i in range(first, along - 1, 2)]
            result.append(lax.ppermute(value, "by", pairs + [(j, i) for i, j in pairs]))
        return result

    line = (1, psf_z.shape[0])
    psf_z, psf_x, psf_y = psf_z.reshape(line), psf_x.reshape(line), psf_y.reshape(line)
    order = pltpu.VMEM((2, columns, columns + 2 * radius), F32)
    block = sum(chunks)
    pieces = 4
    seen, sibling, other, *parcels = call(
        1.3,
        functools.partial(start_kernel, parts, radius, count),
        [shaped(columns, length), shaped(radius, length), shaped(radius, length)]
        + [shaped(block + sum(chunks[1:]), length)] * count,
        [SMEM, HBM, HBM],
        [order, pltpu.VMEM(line, F32), pltpu.VMEM((length, columns), F32), pltpu.SemaphoreType.DMA((pieces + 1,))],
    )(where, stays(psf_y), stays(observed.reshape(length, columns)))
    seen_sides = from_sides(sibling, other)
    parcels = exchanged(parcels)

    def left(rows, width):
        return jax.ShapeDtypeStruct((rows, 3 * width), BF16)

    def right(rows, width):
        return jax.ShapeDtypeStruct((3 * rows, width), BF16)

    span = 2 * radius // len(parts)
    across = LANES // rows * width
    first, back_early, back_late, ahead_early, ahead_late, end_early, end_late, *weights = call(
        0.8,
        functools.partial(weights_kernel, sizes, parts),
        [
            left(size_of(parts[0]), columns + 2 * radius),
            left(columns + 2 * radius, columns + 4 * radius - 2 * span),
            left(4 * radius, 2 * span),
            left(columns, columns - 2 * radius),
            left(columns, 4 * radius),
            left(columns, columns),
            left(2 * radius, 2 * radius),
            right(beside * LANES, across),
            right(across, beside * LANES),
            left(groups * planes, groups * planes),
            left(groups * planes, groups * planes),
        ],
        [SMEM] + [VMEM] * 3,
        [order],
    )(where, psf_z, psf_x, psf_y)
    outer = exchanged(
        call(
            0.8,
            first_y_kernel,
            [shaped(chunks[0], length)] * count,
            [SMEM] + [VMEM] * 4,
        )(where, first, seen, *seen_sides)
    )

    def through_planes(values, first, chunk, seen_values, seen_first=None):
        lines = groups * planes * chunk
        across = (width // LANES, lines, LANES)
        begins = seen_first is not None
        result = call(
            50,
            functools.partial(planes_kernel, sizes, first, seen_first),
            [shaped(chunk, length)] * count + [shaped(8, LANES)] + [shaped(*across)] * begins,
            [SMEM] + [VMEM] * (4 + len(values) + len(seen_values)),
            [
                pltpu.VMEM((beside, groups * (length // LANES) * chunk, LANES), F32),
                pltpu.VMEM(across, F32),
                pltpu.VMEM(across, F32),
            ],
        )(where, *weights, *values, *seen_values)
        return result[:count], result[count], result[count + 1 :] if begins else seen_values

    def sides_of(cost, values, span, mark):
        sides = call(
            cost,
            functools.partial(sides_kernel, count),
            [shaped(span, length)] * 2,
            [SMEM] + [VMEM] * count + [ANY],
        )(where, *values, mark)
        return from_sides(*sides)

    fields, across, sides = ([None] * len(parts) for _ in range(3))
    before = 0
    for k in reversed(range(len(parts))):
        values, first = (parcels, before + chunks[k]) if k else (outer, 0)
        fields[k], mark, across[k] = through_planes(values, first, chunks[k], parcels, before)
        fields[k] = exchanged(fields[k])
        before += chunks[k] * (2 if k else 1)
    for k in reversed(range(len(parts))):
        sides[k] = sides_of(50, fields[k], span, mark)
    partial = [shaped(4 * radius, length), shaped(columns - 2 * radius, length), shaped(columns, length)]
    partial = call(
        2.2,
        functools.partial(middle_early_kernel, parts, radius, count),
        partial,
        [SMEM] + [VMEM] * (1 + (count + 2) * len(parts)),
        [pltpu.VMEM((size_of(runs), length), F32) for runs in parts],
    )(where, back_early, ahead_early, *flat(fields), *flat(sides[1:]), seen)
    estimate, *parcels = call(
        1.3,
        functools.partial(middle_late_kernel, parts, radius, count),
        [shaped(columns, length)] + [shaped(chunk, length) for chunk in chunks for _ in range(count)],
        [SMEM] + [VMEM] * 10,
    )(where, back_late, ahead_late, *sides[0], *partial, seen, *seen_sides)
    for k in range(len(parts)):
        fields[k] = exchanged(parcels[k * count : (k + 1) * count])
    for k in range(len(parts)):
        values, mark, _ = through_planes(fields[k], 0, chunks[k], across[k])
        fields[k] = exchanged(values)
    sides = sides_of(0.6, fields[0], radius, mark)
    partial = call(
        50,
        functools.partial(last_early_kernel, parts, radius, count),
        [shaped(2 * radius, length), shaped(columns - 2 * radius, length)],
        [SMEM] + [VMEM] * (2 + count * len(parts)),
        [pltpu.VMEM((size_of(runs), length), F32) for runs in parts],
    )(where, end_early, estimate, *flat(fields))
    out = call(
        1.5,
        functools.partial(last_late_kernel, radius, count),
        shaped(length, columns),
        [SMEM] + [VMEM] * 6,
        [pltpu.VMEM((length, columns), F32), pltpu.SemaphoreType.DMA((pieces,))],
        HBM,
    )(where, end_late, *sides, *partial, estimate)
    return out.reshape(planes, rows, columns)


def solution(mesh):
    placed = (P("gz", "bx", "by"), P(), P(), P())
    return jax.shard_map(
        per_device, mesh=mesh, in_specs=placed, out_specs=P("gz", "bx", "by"), check_vma=False
    )
```

```python
import functools
import jax
import jax.numpy as jnp
from jax import lax
from jax.experimental import pallas as pl
from jax.experimental.pallas import tpu as pltpu
from jax.sharding import PartitionSpec as P

LANES = 128
RATE = 1150 * 1000 * 1000
STEP = 4 * LANES
F32 = jnp.float32
BF16 = jnp.bfloat16
VMEM = pl.BlockSpec(memory_space=pltpu.VMEM)
HBM = pl.BlockSpec(memory_space=pltpu.HBM)


def shaped(*shape):
    return jax.ShapeDtypeStruct(shape, F32)


def stays(value):
    return pltpu.with_memory_space_constraint(value, pltpu.HBM)


def call(cost, kernel, outs, specs, scratch=(), place=VMEM):
    return pl.pallas_call(
        lambda *refs: kernel(place_of_device(), *refs),
        out_shape=outs,
        in_specs=specs,
        out_specs=jax.tree.map(lambda _: place, outs),
        scratch_shapes=list(scratch),
        compiler_params=pltpu.CompilerParams(vmem_limit_bytes=40 * 1024 * 1024),
        cost_estimate=pl.CostEstimate(flops=int(cost * RATE), bytes_accessed=0, transcendentals=0),
    )


def parts_of(columns, radius, count):
    outer = [(0, radius), (columns - radius, radius)]
    inner = [(radius, columns - 2 * radius)]
    fits = columns >= 3 * radius and count % 2 == 0
    for runs in (outer, inner):
        fits = fits and sum(size for _, size in runs) % (8 * count) == 0
    return [outer, inner] if fits else [[(0, columns)]]


def flat(lists):
    return [value for values in lists for value in values]


def size_of(runs):
    return sum(size for _, size in runs)


def rows_of(value, runs):
    return jnp.concatenate([value[start : start + size] for start, size in runs], axis=0)


def place_of(runs, offset):
    place, before = runs[0][0] + offset, 0
    for (start, size), (after, _) in zip(runs, runs[1:]):
        before += size
        place = jnp.where(offset >= before, after - before + offset, place)
    return place


def offsets_of(groups, beside):
    offsets = [(dz, dx) for dz in range(groups) for dx in range(beside)]
    return offsets[:1] + sorted(offsets[1:], key=lambda offset: offset.count(0))


def place_of_device():
    groups, beside = lax.axis_size("gz"), lax.axis_size("bx")
    me_z, me_x = lax.axis_index("gz"), lax.axis_index("bx")
    offsets = offsets_of(groups, beside)
    ahead = [lax.rem(me_z + dz, groups) * beside + lax.rem(me_x + dx, beside) for dz, dx in offsets]
    behind = [
        lax.rem(me_z + groups - dz, groups) * beside + lax.rem(me_x + beside - dx, beside) for dz, dx in offsets
    ]
    return ahead + behind + [lax.rem(lax.axis_index("by"), 2), me_z, me_x]


def split(value):
    high = value.astype(BF16)
    return high, (value - high.astype(F32)).astype(BF16)


def dot(left, right):
    return lax.dot_general(left, right, (((1,), (0,)), ((), ())), preferred_element_type=F32)


def banded(taps, rows, width, start):
    room = (width + 2 * LANES - 1) // LANES * LANES
    base = jnp.concatenate([taps, jnp.zeros((1, room - LANES), F32)], axis=1)
    base = jnp.broadcast_to(base, (rows, room))
    return pltpu.roll(base, start % room, 1, stride=1, stride_axis=0)[:, :width]


def as_left(matrix):
    high, low = split(matrix)
    return jnp.concatenate([high, high, low], axis=1)


def left_product(matrix, value):
    high, low = split(value)
    return dot(matrix, jnp.concatenate([high, low, high], axis=0))


def as_right(matrix):
    high, low = split(matrix)
    return jnp.concatenate([high, high, low], axis=0)


def right_product(value, matrix):
    high, low = split(value)
    return dot(jnp.concatenate([high, low, high], axis=1), matrix)


def ordered_rows(matrix, where, order_ref, runs, count):
    size = size_of(runs)
    chunk = size // count
    width = matrix.shape[1]
    order_ref[0, :size, :width] = rows_of(matrix, runs)
    for slot in range(count):
        place = pl.multiple_of(where[slot] * chunk, chunk)
        order_ref[1, slot * chunk : (slot + 1) * chunk, :width] = order_ref[0, pl.ds(place, chunk), :width]
    return order_ref[1, :size, :width]


def columns_of(matrix, runs):
    return jnp.concatenate([matrix[:, start : start + size] for start, size in runs], axis=1)


def taps_of(psf_ref):
    count = psf_ref.shape[1]
    row = lax.broadcasted_iota(jnp.int32, (LANES, LANES), 0)
    lane = lax.broadcasted_iota(jnp.int32, (LANES, LANES), 1)
    taps = psf_ref[...] / jnp.sum(psf_ref[...], axis=1, keepdims=True)
    taps = jnp.concatenate([taps, jnp.zeros((1, LANES - count), F32)], axis=1)
    column = jnp.transpose(jnp.broadcast_to(taps, (LANES, LANES)))
    return taps, jnp.sum(jnp.where(row + lane == count - 1, column, 0.0), axis=0, keepdims=True)


def weights_kernel(
    sizes,
    parts,
    where,
    psf_z_ref,
    psf_x_ref,
    psf_y_ref,
    first_ref,
    back_early_ref,
    back_late_ref,
    ahead_early_ref,
    ahead_late_ref,
    end_early_ref,
    end_late_ref,
    rows_ahead_ref,
    rows_back_ref,
    planes_ahead_ref,
    planes_back_ref,
    order_ref,
):
    groups, beside, radius, depth, rows, columns = sizes
    count = groups * beside
    taps, turned = taps_of(psf_y_ref)
    wide = columns + 2 * radius
    span = 2 * radius // len(parts)
    edges = [(0, 2 * radius), (wide - 2 * radius, 2 * radius)]

    ahead = banded(taps, columns, wide, 0)
    ahead = jnp.concatenate([ordered_rows(ahead, where, order_ref, runs, count) for runs in parts], axis=0)
    first_ref[...] = as_left(ahead[: size_of(parts[0])])
    ahead_early_ref[...] = as_left(ahead[:, 2 * radius : columns])
    ahead_late_ref[...] = as_left(columns_of(ahead, edges))
    back = banded(turned, wide, wide + 2 * radius, 0)
    late = [(2 * radius - span, span), (columns + 2 * radius, span)]
    early = [(0, 2 * radius - span), (2 * radius, columns), (columns + 2 * radius + span, 2 * radius - span)]
    back_early_ref[...] = as_left(columns_of(back, [run for run in early if run[1]]))
    back_late_ref[...] = as_left(columns_of(rows_of(back, edges), late))
    back = banded(turned, columns, wide, 0)
    end_early_ref[...] = as_left(back[:, radius : radius + columns])
    edges = [(0, radius), (columns - radius, radius)]
    end_late_ref[...] = as_left(columns_of(rows_of(back, edges), [(0, radius), (columns + radius, radius)]))

    per = LANES // rows
    width = beside * rows
    taps, turned = taps_of(psf_x_ref)
    ahead = banded(turned, width, width, -radius)
    back = banded(taps, width, width, -radius)
    blocks = []
    for b in range(beside):
        for k in range(per):
            line = [jnp.zeros((rows, width), F32)] * per
            line[k] = ahead[b * rows : (b + 1) * rows]
            blocks.append(jnp.concatenate(line, axis=1))
    rows_ahead_ref[...] = as_right(jnp.concatenate(blocks, axis=0))
    for b in range(beside):
        blocks = []
        for k in range(per):
            line = [jnp.zeros((width, rows), F32)] * per
            line[k] = back[:, b * rows : (b + 1) * rows]
            blocks.append(jnp.concatenate(line, axis=1))
        slot = lax.rem(b + beside - where[2 * count + 2], beside)
        rows_back_ref[:, pl.ds(pl.multiple_of(slot * LANES, LANES), LANES)] = as_right(jnp.concatenate(blocks, axis=0))
    planes = groups * depth
    for ref, line in zip((planes_ahead_ref, planes_back_ref), taps_of(psf_z_ref)):
        ref[...] = as_left(banded(line, planes, planes, -radius))


def send_sides(where, count, value_ref, span, sibling_ref, other_ref):
    odd = where[2 * count]
    room = value_ref.shape[0] - span
    sibling_ref[...] = value_ref[pl.ds(pl.multiple_of((1 - odd) * room, 8), span), :]
    other_ref[...] = value_ref[pl.ds(pl.multiple_of(odd * room, 8), span), :]


def start_kernel(parts, radius, count, where, psf_hbm, block_hbm, *refs):
    own_ref, sibling_ref, other_ref = refs[:3]
    part_refs, (order_ref, psf_ref, block_ref, sems) = refs[3:-4], refs[-4:]
    length, columns = block_ref.shape
    pieces = sems.shape[0] - 1
    piece = length // pieces
    copies = [pltpu.make_async_copy(psf_hbm, psf_ref, sems.at[pieces])]
    for k in range(pieces):
        here = pl.ds(k * piece, piece)
        copies.append(pltpu.make_async_copy(block_hbm.at[here], block_ref.at[here], sems.at[k]))
    for copy in copies:
        copy.start()
    copies[0].wait()
    taps, _ = taps_of(psf_ref)
    matrices = [None]
    for runs in parts[1:]:
        matrix = banded(taps, columns, columns, -radius)
        matrices.append(as_left(ordered_rows(matrix, where, order_ref, runs, count)))
    for k in range(pieces):
        copies[k + 1].wait()
        for at in range(k * piece, (k + 1) * piece, LANES):
            own_ref[:, at : at + LANES] = jnp.transpose(block_ref[at : at + LANES, :])
    send_sides(where, count, own_ref, radius, sibling_ref, other_ref)
    before = 0
    for k, runs in reversed(list(enumerate(parts))):
        chunk = size_of(runs) // count
        for slot, part_ref in enumerate(part_refs):
            place = pl.multiple_of(place_of(runs, where[slot] * chunk), 8)
            part_ref[before : before + chunk, :] = own_ref[pl.ds(place, chunk), :]
        before += chunk
        if k:
            for at in range(0, length, STEP):
                here = slice(at, at + STEP)
                result = left_product(matrices[k], own_ref[:, here])
                for slot, part_ref in enumerate(part_refs):
                    part_ref[before : before + chunk, here] = result[slot * chunk : (slot + 1) * chunk]
            before += chunk


def first_y_kernel(where, matrix_ref, own_ref, other_ref, sibling_ref, *part_refs):
    columns, length = own_ref.shape
    count = len(part_refs)
    chunk = part_refs[0].shape[0]
    odd = where[2 * count] == 1
    for at in range(0, length, STEP):
        here = slice(at, at + STEP)
        field = assembled([[(0, columns)]], odd, [own_ref], [(other_ref, sibling_ref)], here)
        result = left_product(matrix_ref[...], field)
        for slot, part_ref in enumerate(part_refs):
            part_ref[:, here] = result[slot * chunk : (slot + 1) * chunk]


def put_parts(where, count, part_refs, own_refs):
    for k, own_ref in enumerate(own_refs):
        for slot, part_ref in enumerate(part_refs[k * count : (k + 1) * count]):
            chunk = part_ref.shape[0]
            place = pl.multiple_of(where[count + slot] * chunk, chunk)
            own_ref[pl.ds(place, chunk), :] = part_ref[...]


def sides_kernel(count, where, *refs):
    part_refs, (_, sibling_ref, other_ref) = refs[:count], refs[count:]
    span = sibling_ref.shape[0]
    chunk = part_refs[0].shape[0]
    odd = where[2 * count]
    for slot, part_ref in enumerate(part_refs):
        start = where[count + slot] * chunk
        for first, to_sibling in ((0, odd), (count * chunk - span, 1 - odd)):
            inside = (start >= first) & (start < first + span)

            def put(ref, start=start, first=first, part_ref=part_ref):
                ref[pl.ds(pl.multiple_of(start - first, 8), chunk), :] = part_ref[...]

            pl.when(inside & (to_sibling == 1))(functools.partial(put, sibling_ref))
            pl.when(inside & (to_sibling == 0))(functools.partial(put, other_ref))


def assembled(parts, odd, own_refs, side_refs, here):
    pieces = {}
    for runs, ref in zip(parts, own_refs):
        at = 0
        for start, size in runs:
            pieces[start] = ref[at : at + size] if isinstance(ref, jax.Array) else ref[at : at + size, here]
            at += size
    own = [pieces[start] for start in sorted(pieces)]
    low, high = [], []
    for other_ref, sibling_ref in side_refs:
        sibling, other = sibling_ref[:, here], other_ref[:, here]
        low.insert(0, jnp.where(odd, sibling, other))
        high.append(jnp.where(odd, other, sibling))
    return jnp.concatenate(low + own + high, axis=0)


def middle_early_kernel(parts, radius, count, where, back_ref, ahead_ref, *refs):
    kinds = len(parts)
    own_refs, refs = refs[-kinds:], refs[:-kinds]
    put_parts(where, count, refs, own_refs)
    refs = refs[kinds * count :]
    side_refs = [refs[2 * k : 2 * k + 2] for k in range(kinds - 1)]
    seen_ref, outer_ref, inner_ref, result_ref = refs[2 * kinds - 2 :]
    columns, length = seen_ref.shape
    wide = columns + 2 * radius
    edges = [(0, 2 * radius), (wide - 2 * radius, 2 * radius)]
    odd = where[2 * count] == 1
    for at in range(0, length, STEP):
        here = slice(at, at + STEP)
        blurred = left_product(back_ref[...], assembled(parts, odd, own_refs, side_refs, here))
        outer_ref[:, here] = rows_of(blurred, edges)
        inner = seen_ref[radius : columns - radius, here] * blurred[2 * radius : columns]
        inner_ref[:, here] = inner
        result_ref[:, here] = left_product(ahead_ref[...], inner)


def middle_late_kernel(parts, radius, count, where, back_ref, ahead_ref, *refs):
    (other_ref, sibling_ref, outer_ref, inner_ref, result_ref), refs = refs[:5], refs[5:]
    seen_ref, seen_other_ref, seen_sibling_ref, estimate_ref, *part_refs = refs
    columns, length = seen_ref.shape
    wide = columns + 2 * radius
    edges = [(0, 2 * radius), (wide - 2 * radius, 2 * radius)]
    odd = where[2 * count] == 1
    for at in range(0, length, STEP):
        here = slice(at, at + STEP)
        sides = assembled([], odd, [], [(other_ref, sibling_ref)], here)
        seen = assembled([[(0, columns)]], odd, [seen_ref], [(seen_other_ref, seen_sibling_ref)], here)
        outer = rows_of(seen, edges) * (outer_ref[:, here] + left_product(back_ref[...], sides))
        estimate_ref[:, here] = jnp.concatenate(
            [outer[radius : 2 * radius], inner_ref[:, here], outer[2 * radius : 3 * radius]], axis=0
        )
        result = result_ref[:, here] + left_product(ahead_ref[...], outer)
        place = 0
        for part_ref in part_refs:
            chunk = part_ref.shape[0]
            part_ref[:, here] = result[place : place + chunk]
            place += chunk


def last_early_kernel(parts, radius, count, where, back_ref, estimate_ref, *refs):
    outer_ref, inner_ref, *own_refs = refs[len(parts) * count :]
    put_parts(where, count, refs, own_refs)
    columns, length = estimate_ref.shape
    edges = [(0, radius), (columns - radius, radius)]
    for at in range(0, length, STEP):
        here = slice(at, at + STEP)
        blurred = left_product(back_ref[...], assembled(parts, None, own_refs, [], here))
        outer_ref[:, here] = rows_of(blurred, edges)
        inner_ref[:, here] = estimate_ref[radius : columns - radius, here] * blurred[radius : columns - radius]


def last_late_kernel(
    radius, count, where, back_ref, other_ref, sibling_ref, outer_ref, inner_ref, estimate_ref, out_hbm, out_ref, sems
):
    columns, length = estimate_ref.shape
    odd = where[2 * count] == 1
    edges = [(0, radius), (columns - radius, radius)]
    pieces = sems.shape[0]
    piece = length // pieces
    copies = []
    for at in range(0, length, STEP):
        here = slice(at, at + STEP)
        sides = assembled([], odd, [], [(other_ref, sibling_ref)], here)
        outer = rows_of(estimate_ref[:, here], edges) * (outer_ref[:, here] + left_product(back_ref[...], sides))
        estimate = jnp.concatenate([outer[:radius], inner_ref[:, here], outer[radius:]], axis=0)
        for tile in range(0, STEP, LANES):
            out_ref[at + tile : at + tile + LANES, :] = jnp.transpose(estimate[:, tile : tile + LANES])
            if (at + tile + LANES) % piece == 0:
                k = (at + tile) // piece
                lines = pl.ds(k * piece, piece)
                copies.append(pltpu.make_async_copy(out_ref.at[lines], out_hbm.at[lines], sems.at[k]))
                copies[-1].start()
    for copy in copies:
        copy.wait()


def put_lines(ref, lines, value):
    for tile in range(ref.shape[0]):
        ref[tile, lines, :] = value[:, tile * LANES : (tile + 1) * LANES]


def get_lines(ref, lines):
    return jnp.concatenate([ref[tile, lines, :] for tile in range(ref.shape[0])], axis=1)


def fill(sizes, where, part_refs, first, chunk, held_ref):
    groups, beside = sizes[:2]
    count = groups * beside
    tiles = part_refs[0].shape[1] // LANES
    for (dz, dx), part_ref in zip(offsets_of(groups, beside), part_refs):
        source_z = lax.rem(where[2 * count + 1] + groups - dz, groups)
        source_x = lax.rem(where[2 * count + 2] + beside - dx, beside)
        for t in range(tiles):
            place = pl.multiple_of((source_z * tiles + t) * chunk, chunk)
            held_ref[source_x, pl.ds(place, chunk), :] = part_ref[first : first + chunk, t * LANES : (t + 1) * LANES]


def planes_kernel(
    sizes, first, seen_first, where, rows_ahead_ref, rows_back_ref, planes_ahead_ref, planes_back_ref, *refs
):
    groups, beside, _, _, rows, _ = sizes
    count = groups * beside
    part_refs, refs = refs[:count], refs[count:]
    begins = seen_first is not None
    if begins:
        seen_refs, refs = refs[:count], refs[count:]
        out_refs, (seen_ref, held_ref, field_ref, other_ref) = refs[:count], refs[count:]
    else:
        seen_ref, out_refs, (held_ref, field_ref, other_ref) = refs[0], refs[1 : count + 1], refs[count + 1 :]
    chunk, length = out_refs[0].shape
    tiles = length // LANES
    per = LANES // rows
    width = beside * rows
    planes = groups * tiles * per
    if begins:
        fill(sizes, where, seen_refs, seen_first, chunk, held_ref)
        for at in range(groups * tiles):
            for k in range(per):
                lines = slice(at * chunk, (at + 1) * chunk)
                pieces = [held_ref[b, lines, k * rows : (k + 1) * rows] for b in range(beside)]
                place = (at * per + k) * chunk
                put_lines(seen_ref, slice(place, place + chunk), jnp.concatenate(pieces, axis=1))
    fill(sizes, where, part_refs, first, chunk, held_ref)

    group = min(tiles, max(1, 4 * LANES // chunk))
    for at in range(0, groups * tiles, group):
        here = slice(at * chunk, (at + group) * chunk)
        left = jnp.concatenate([held_ref[b, here, :] for b in range(beside)], axis=1)
        result = right_product(left, rows_ahead_ref[...])
        for g in range(group):
            for k in range(per):
                place = ((at + g) * per + k) * chunk
                part = result[g * chunk : (g + 1) * chunk, k * width : (k + 1) * width]
                put_lines(field_ref, slice(place, place + chunk), part)

    for y in range(0, chunk, 2):
        lines = [pl.ds(y + k, planes, stride=chunk) for k in range(2)]
        value = jnp.concatenate([get_lines(field_ref, line) for line in lines], axis=1)
        seen = jnp.concatenate([get_lines(seen_ref, line) for line in lines], axis=1)
        value = left_product(planes_back_ref[...], seen / left_product(planes_ahead_ref[...], value))
        for k, line in enumerate(lines):
            put_lines(other_ref, line, value[:, k * width : (k + 1) * width])

    offsets = offsets_of(groups, beside)
    for dz in range(groups):
        target_z = lax.rem(where[2 * count + 1] + dz, groups)
        for at in range(0, tiles, group):
            pieces = []
            for g in range(group):
                line = []
                for k in range(per):
                    place = pl.multiple_of(((target_z * tiles + at + g) * per + k) * chunk, chunk)
                    line.append(get_lines(other_ref, pl.ds(place, chunk)))
                pieces.append(jnp.concatenate(line, axis=1))
            left = jnp.concatenate(pieces, axis=0)
            result = right_product(left, rows_back_ref[...])
            for dx in range(beside):
                for g in range(group):
                    out_refs[offsets.index((dz, dx))][:, (at + g) * LANES : (at + g + 1) * LANES] = result[
                        g * chunk : (g + 1) * chunk, dx * LANES : (dx + 1) * LANES
                    ]


def per_device(observed, psf_z, psf_x, psf_y):
    groups, beside, along = (lax.axis_size(axis) for axis in ("gz", "bx", "by"))
    count = groups * beside
    planes, rows, columns = observed.shape
    length = planes * rows
    radius = psf_z.shape[0] // 2
    sizes = (groups, beside, radius, planes, rows, columns)
    width = beside * rows
    parts = parts_of(columns, radius, count)
    chunks = [size_of(runs) // count for runs in parts]

    offsets = offsets_of(groups, beside)

    def exchanged(values):
        result = [values[0]]
        for (dz, dx), value in list(zip(offsets, values))[1:]:
            pairs = [
                (z * beside + x, ((z + dz) % groups) * beside + (x + dx) % beside)
                for z in range(groups)
                for x in range(beside)
            ]
            result.append(lax.ppermute(value, ("gz", "bx"), pairs))
        return result

    def from_sides(sibling, other):
        result = []
        for value, first in ((other, 1), (sibling, 0)):
            pairs = [(i, i + 1) for i in range(first, along - 1, 2)]
            result.append(lax.ppermute(value, "by", pairs + [(j, i) for i, j in pairs]))
        return result

    line = (1, psf_z.shape[0])
    psf_z, psf_x, psf_y = psf_z.reshape(line), psf_x.reshape(line), psf_y.reshape(line)
    order = pltpu.VMEM((2, columns, columns + 2 * radius), F32)
    block = sum(chunks)
    pieces = 4
    seen, sibling, other, *parcels = call(
        1.3,
        functools.partial(start_kernel, parts, radius, count),
        [shaped(columns, length), shaped(radius, length), shaped(radius, length)]
        + [shaped(block + sum(chunks[1:]), length)] * count,
        [HBM, HBM],
        [order, pltpu.VMEM(line, F32), pltpu.VMEM((length, columns), F32), pltpu.SemaphoreType.DMA((pieces + 1,))],
    )(stays(psf_y), stays(observed.reshape(length, columns)))
    seen_sides = from_sides(sibling, other)
    parcels = exchanged(parcels)

    def left(rows, width):
        return jax.ShapeDtypeStruct((rows, 3 * width), BF16)

    def right(rows, width):
        return jax.ShapeDtypeStruct((3 * rows, width), BF16)

    span = 2 * radius // len(parts)
    across = LANES // rows * width
    first, back_early, back_late, ahead_early, ahead_late, end_early, end_late, *weights = call(
        0.8,
        functools.partial(weights_kernel, sizes, parts),
        [
            left(size_of(parts[0]), columns + 2 * radius),
            left(columns + 2 * radius, columns + 4 * radius - 2 * span),
            left(4 * radius, 2 * span),
            left(columns, columns - 2 * radius),
            left(columns, 4 * radius),
            left(columns, columns),
            left(2 * radius, 2 * radius),
            right(beside * LANES, across),
            right(across, beside * LANES),
            left(groups * planes, groups * planes),
            left(groups * planes, groups * planes),
        ],
        [VMEM] * 3,
        [order],
    )(psf_z, psf_x, psf_y)
    outer = exchanged(
        call(
            0.8,
            first_y_kernel,
            [shaped(chunks[0], length)] * count,
            [VMEM] * 4,
        )(first, seen, *seen_sides)
    )

    def through_planes(values, first, chunk, seen_values, seen_first=None):
        lines = groups * planes * chunk
        across = (width // LANES, lines, LANES)
        begins = seen_first is not None
        result = call(
            50,
            functools.partial(planes_kernel, sizes, first, seen_first),
            [shaped(chunk, length)] * count + [shaped(*across)] * begins,
            [VMEM] * (4 + len(values) + len(seen_values)),
            [
                pltpu.VMEM((beside, groups * (length // LANES) * chunk, LANES), F32),
                pltpu.VMEM(across, F32),
                pltpu.VMEM(across, F32),
            ],
        )(*weights, *values, *seen_values)
        return result[:count], result[count:] if begins else seen_values

    def sides_of(cost, values, span, after):
        sides = call(
            cost,
            functools.partial(sides_kernel, count),
            [shaped(span, length)] * 2,
            [VMEM] * (count + 1),
        )(*values, after)
        return from_sides(*sides)

    fields, across, sides = ([None] * len(parts) for _ in range(3))
    before = 0
    for k in reversed(range(len(parts))):
        values, first = (parcels, before + chunks[k]) if k else (outer, 0)
        fields[k], across[k] = through_planes(values, first, chunks[k], parcels, before)
        fields[k] = exchanged(fields[k])
        before += chunks[k] * (2 if k else 1)
    for k in reversed(range(len(parts))):
        sides[k] = sides_of(50, fields[k], span, fields[0][0])
    partial = [shaped(4 * radius, length), shaped(columns - 2 * radius, length), shaped(columns, length)]
    partial = call(
        2.2,
        functools.partial(middle_early_kernel, parts, radius, count),
        partial,
        [VMEM] * (1 + (count + 2) * len(parts)),
        [pltpu.VMEM((size_of(runs), length), F32) for runs in parts],
    )(back_early, ahead_early, *flat(fields), *flat(sides[1:]), seen)
    estimate, *parcels = call(
        1.3,
        functools.partial(middle_late_kernel, parts, radius, count),
        [shaped(columns, length)] + [shaped(chunk, length) for chunk in chunks for _ in range(count)],
        [VMEM] * 10,
    )(back_late, ahead_late, *sides[0], *partial, seen, *seen_sides)
    for k in range(len(parts)):
        fields[k] = exchanged(parcels[k * count : (k + 1) * count])
    for k in range(len(parts)):
        values, _ = through_planes(fields[k], 0, chunks[k], across[k])
        fields[k] = exchanged(values)
    sides = sides_of(0.6, fields[0], radius, fields[-1][0])
    partial = call(
        50,
        functools.partial(last_early_kernel, parts, radius, count),
        [shaped(2 * radius, length), shaped(columns - 2 * radius, length)],
        [VMEM] * (2 + count * len(parts)),
        [pltpu.VMEM((size_of(runs), length), F32) for runs in parts],
    )(end_early, estimate, *flat(fields))
    out = call(
        1.5,
        functools.partial(last_late_kernel, radius, count),
        shaped(length, columns),
        [VMEM] * 6,
        [pltpu.VMEM((length, columns), F32), pltpu.SemaphoreType.DMA((pieces,))],
        HBM,
    )(end_late, *sides, *partial, estimate)
    return out.reshape(planes, rows, columns)


def solution(mesh):
    placed = (P("gz", "bx", "by"), P(), P(), P())
    return jax.shard_map(
        per_device, mesh=mesh, in_specs=placed, out_specs=P("gz", "bx", "by"), check_vma=False
    )
```

```python
import functools
import jax
import jax.numpy as jnp
from jax import lax
from jax.experimental import pallas as pl
from jax.experimental.pallas import tpu as pltpu
from jax.sharding import PartitionSpec as P

LANES = 128
RATE = 1150 * 1000 * 1000
STEP = 4 * LANES
F32 = jnp.float32
BF16 = jnp.bfloat16
VMEM = pl.BlockSpec(memory_space=pltpu.VMEM)
HBM = pl.BlockSpec(memory_space=pltpu.HBM)


def shaped(*shape):
    return jax.ShapeDtypeStruct(shape, F32)


def stays(value):
    return pltpu.with_memory_space_constraint(value, pltpu.HBM)


def call(cost, kernel, outs, specs, scratch=(), place=VMEM):
    return pl.pallas_call(
        lambda *refs: kernel(place_of_device(), *refs),
        out_shape=outs,
        in_specs=specs,
        out_specs=jax.tree.map(lambda _: place, outs),
        scratch_shapes=list(scratch),
        compiler_params=pltpu.CompilerParams(vmem_limit_bytes=16 * 1024 * 1024),
        cost_estimate=pl.CostEstimate(flops=int(cost * RATE), bytes_accessed=0, transcendentals=0),
    )


def parts_of(columns, radius, count):
    outer = [(0, radius), (columns - radius, radius)]
    inner = [(radius, columns - 2 * radius)]
    fits = columns >= 3 * radius and count % 2 == 0
    for runs in (outer, inner):
        fits = fits and sum(size for _, size in runs) % (8 * count) == 0
    return [outer, inner] if fits else [[(0, columns)]]


def flat(lists):
    return [value for values in lists for value in values]


def size_of(runs):
    return sum(size for _, size in runs)


def rows_of(value, runs):
    return jnp.concatenate([value[start : start + size] for start, size in runs], axis=0)


def place_of(runs, offset):
    place, before = runs[0][0] + offset, 0
    for (start, size), (after, _) in zip(runs, runs[1:]):
        before += size
        place = jnp.where(offset >= before, after - before + offset, place)
    return place


def offsets_of(groups, beside):
    offsets = [(dz, dx) for dz in range(groups) for dx in range(beside)]
    return offsets[:1] + sorted(offsets[1:], key=lambda offset: offset.count(0))


def place_of_device():
    groups, beside = lax.axis_size("gz"), lax.axis_size("bx")
    me_z, me_x = lax.axis_index("gz"), lax.axis_index("bx")
    offsets = offsets_of(groups, beside)
    ahead = [lax.rem(me_z + dz, groups) * beside + lax.rem(me_x + dx, beside) for dz, dx in offsets]
    behind = [
        lax.rem(me_z + groups - dz, groups) * beside + lax.rem(me_x + beside - dx, beside) for dz, dx in offsets
    ]
    return ahead + behind + [lax.rem(lax.axis_index("by"), 2), me_z, me_x]


def split(value):
    high = value.astype(BF16)
    return high, (value - high.astype(F32)).astype(BF16)


def dot(left, right):
    return lax.dot_general(left, right, (((1,), (0,)), ((), ())), preferred_element_type=F32)


def banded(taps, rows, width, start):
    room = (width + 2 * LANES - 1) // LANES * LANES
    base = jnp.concatenate([taps, jnp.zeros((1, room - LANES), F32)], axis=1)
    base = jnp.broadcast_to(base, (rows, room))
    return pltpu.roll(base, start % room, 1, stride=1, stride_axis=0)[:, :width]


def as_left(matrix):
    high, low = split(matrix)
    return jnp.concatenate([high, high, low], axis=1)


def left_product(matrix, value):
    high, low = split(value)
    return dot(matrix, jnp.concatenate([high, low, high], axis=0))


def as_right(matrix):
    high, low = split(matrix)
    return jnp.concatenate([high, high, low], axis=0)


def right_product(value, matrix):
    high, low = split(value)
    return dot(jnp.concatenate([high, low, high], axis=1), matrix)


def ordered_rows(matrix, where, order_ref, runs, count):
    size = size_of(runs)
    chunk = size // count
    width = matrix.shape[1]
    order_ref[0, :size, :width] = rows_of(matrix, runs)
    for slot in range(count):
        place = pl.multiple_of(where[slot] * chunk, chunk)
        order_ref[1, slot * chunk : (slot + 1) * chunk, :width] = order_ref[0, pl.ds(place, chunk), :width]
    return order_ref[1, :size, :width]


def columns_of(matrix, runs):
    return jnp.concatenate([matrix[:, start : start + size] for start, size in runs], axis=1)


def taps_of(psf_ref):
    count = psf_ref.shape[1]
    row = lax.broadcasted_iota(jnp.int32, (LANES, LANES), 0)
    lane = lax.broadcasted_iota(jnp.int32, (LANES, LANES), 1)
    taps = psf_ref[...] / jnp.sum(psf_ref[...], axis=1, keepdims=True)
    taps = jnp.concatenate([taps, jnp.zeros((1, LANES - count), F32)], axis=1)
    column = jnp.transpose(jnp.broadcast_to(taps, (LANES, LANES)))
    return taps, jnp.sum(jnp.where(row + lane == count - 1, column, 0.0), axis=0, keepdims=True)


def weights_kernel(
    sizes,
    parts,
    where,
    psf_z_ref,
    psf_x_ref,
    psf_y_ref,
    first_ref,
    back_early_ref,
    back_late_ref,
    ahead_early_ref,
    ahead_late_ref,
    ahead_rest_ref,
    end_early_ref,
    end_late_ref,
    rows_ahead_ref,
    rows_back_ref,
    planes_ahead_ref,
    planes_back_ref,
    order_ref,
):
    groups, beside, radius, depth, rows, columns = sizes
    count = groups * beside
    taps, turned = taps_of(psf_y_ref)
    wide = columns + 2 * radius
    span = 2 * radius // len(parts)
    edges = [(0, 2 * radius), (wide - 2 * radius, 2 * radius)]
    rest_rows = ahead_rest_ref.shape[0]

    ahead = banded(taps, columns, wide, 0)
    ahead = jnp.concatenate([ordered_rows(ahead, where, order_ref, runs, count) for runs in parts], axis=0)
    first_ref[...] = as_left(ahead[: size_of(parts[0])])
    ahead_early_ref[...] = as_left(ahead[:, 2 * radius : columns])
    ahead = columns_of(ahead, edges)
    ahead_late_ref[...] = as_left(ahead[: size_of(parts[0])])
    ahead_rest_ref[...] = as_left(ahead[-rest_rows:])
    back = banded(turned, wide, wide + 2 * radius, 0)
    late = [(2 * radius - span, span), (columns + 2 * radius, span)]
    early = [(0, 2 * radius - span), (2 * radius, columns), (columns + 2 * radius + span, 2 * radius - span)]
    back_early_ref[...] = as_left(columns_of(back, [run for run in early if run[1]]))
    back_late_ref[...] = as_left(columns_of(rows_of(back, edges), late))
    back = banded(turned, columns, wide, 0)
    end_early_ref[...] = as_left(back[:, radius : radius + columns])
    edges = [(0, radius), (columns - radius, radius)]
    end_late_ref[...] = as_left(columns_of(rows_of(back, edges), [(0, radius), (columns + radius, radius)]))

    per = LANES // rows
    width = beside * rows
    taps, turned = taps_of(psf_x_ref)
    ahead = banded(turned, width, width, -radius)
    back = banded(taps, width, width, -radius)
    blocks = []
    for b in range(beside):
        for k in range(per):
            line = [jnp.zeros((rows, width), F32)] * per
            line[k] = ahead[b * rows : (b + 1) * rows]
            blocks.append(jnp.concatenate(line, axis=1))
    rows_ahead_ref[...] = as_right(jnp.concatenate(blocks, axis=0))
    for b in range(beside):
        blocks = []
        for k in range(per):
            line = [jnp.zeros((width, rows), F32)] * per
            line[k] = back[:, b * rows : (b + 1) * rows]
            blocks.append(jnp.concatenate(line, axis=1))
        slot = lax.rem(b + beside - where[2 * count + 2], beside)
        rows_back_ref[:, pl.ds(pl.multiple_of(slot * LANES, LANES), LANES)] = as_right(jnp.concatenate(blocks, axis=0))
    planes = groups * depth
    for ref, line in zip((planes_ahead_ref, planes_back_ref), taps_of(psf_z_ref)):
        ref[...] = as_left(banded(line, planes, planes, -radius))


def send_sides(where, count, value_ref, span, sibling_ref, other_ref):
    odd = where[2 * count]
    room = value_ref.shape[0] - span
    sibling_ref[...] = value_ref[pl.ds(pl.multiple_of((1 - odd) * room, 8), span), :]
    other_ref[...] = value_ref[pl.ds(pl.multiple_of(odd * room, 8), span), :]


def start_kernel(parts, radius, count, where, psf_hbm, block_hbm, *refs):
    own_ref, sibling_ref, other_ref = refs[:3]
    part_refs, (order_ref, psf_ref, block_ref, sems) = refs[3:-4], refs[-4:]
    length, columns = block_ref.shape
    pieces = sems.shape[0] - 1
    piece = length // pieces
    copies = [pltpu.make_async_copy(psf_hbm, psf_ref, sems.at[pieces])]
    for k in range(pieces):
        here = pl.ds(k * piece, piece)
        copies.append(pltpu.make_async_copy(block_hbm.at[here], block_ref.at[here], sems.at[k]))
    for copy in copies:
        copy.start()
    copies[0].wait()
    taps, _ = taps_of(psf_ref)
    matrices = [None]
    for runs in parts[1:]:
        matrix = banded(taps, columns, columns, -radius)
        matrices.append(as_left(ordered_rows(matrix, where, order_ref, runs, count)))
    for k in range(pieces):
        copies[k + 1].wait()
        for at in range(k * piece, (k + 1) * piece, LANES):
            own_ref[:, at : at + LANES] = jnp.transpose(block_ref[at : at + LANES, :])
    send_sides(where, count, own_ref, radius, sibling_ref, other_ref)
    before = 0
    for k, runs in reversed(list(enumerate(parts))):
        chunk = size_of(runs) // count
        for slot, part_ref in enumerate(part_refs):
            place = pl.multiple_of(place_of(runs, where[slot] * chunk), 8)
            part_ref[before : before + chunk, :] = own_ref[pl.ds(place, chunk), :]
        before += chunk
        if k:
            for at in range(0, length, STEP):
                here = slice(at, at + STEP)
                result = left_product(matrices[k], own_ref[:, here])
                for slot, part_ref in enumerate(part_refs):
                    part_ref[before : before + chunk, here] = result[slot * chunk : (slot + 1) * chunk]
            before += chunk


def first_y_kernel(where, matrix_ref, own_ref, other_ref, sibling_ref, *part_refs):
    columns, length = own_ref.shape
    count = len(part_refs)
    chunk = part_refs[0].shape[0]
    odd = where[2 * count] == 1
    for at in range(0, length, STEP):
        here = slice(at, at + STEP)
        field = assembled([[(0, columns)]], odd, [own_ref], [(other_ref, sibling_ref)], here)
        result = left_product(matrix_ref[...], field)
        for slot, part_ref in enumerate(part_refs):
            part_ref[:, here] = result[slot * chunk : (slot + 1) * chunk]


def put_parts(where, count, part_refs, own_refs):
    for k, own_ref in enumerate(own_refs):
        for slot, part_ref in enumerate(part_refs[k * count : (k + 1) * count]):
            chunk = part_ref.shape[0]
            place = pl.multiple_of(where[count + slot] * chunk, chunk)
            own_ref[pl.ds(place, chunk), :] = part_ref[...]


def sides_kernel(count, where, *refs):
    part_refs, (_, sibling_ref, other_ref) = refs[:count], refs[count:]
    span = sibling_ref.shape[0]
    chunk = part_refs[0].shape[0]
    odd = where[2 * count]
    for slot, part_ref in enumerate(part_refs):
        start = where[count + slot] * chunk
        for first, to_sibling in ((0, odd), (count * chunk - span, 1 - odd)):
            inside = (start >= first) & (start < first + span)

            def put(ref, start=start, first=first, part_ref=part_ref):
                ref[pl.ds(pl.multiple_of(start - first, 8), chunk), :] = part_ref[...]

            pl.when(inside & (to_sibling == 1))(functools.partial(put, sibling_ref))
            pl.when(inside & (to_sibling == 0))(functools.partial(put, other_ref))


def assembled(parts, odd, own_refs, side_refs, here):
    pieces = {}
    for runs, ref in zip(parts, own_refs):
        at = 0
        for start, size in runs:
            pieces[start] = ref[at : at + size] if isinstance(ref, jax.Array) else ref[at : at + size, here]
            at += size
    own = [pieces[start] for start in sorted(pieces)]
    low, high = [], []
    for other_ref, sibling_ref in side_refs:
        sibling, other = sibling_ref[:, here], other_ref[:, here]
        low.insert(0, jnp.where(odd, sibling, other))
        high.append(jnp.where(odd, other, sibling))
    return jnp.concatenate(low + own + high, axis=0)


def middle_early_kernel(parts, radius, count, where, back_ref, ahead_ref, *refs):
    kinds = len(parts)
    own_refs, refs = refs[-kinds:], refs[:-kinds]
    put_parts(where, count, refs, own_refs)
    refs = refs[kinds * count :]
    side_refs = [refs[2 * k : 2 * k + 2] for k in range(kinds - 1)]
    seen_ref, outer_ref, inner_ref, result_ref = refs[2 * kinds - 2 :]
    columns, length = seen_ref.shape
    wide = columns + 2 * radius
    edges = [(0, 2 * radius), (wide - 2 * radius, 2 * radius)]
    odd = where[2 * count] == 1
    for at in range(0, length, STEP):
        here = slice(at, at + STEP)
        blurred = left_product(back_ref[...], assembled(parts, odd, own_refs, side_refs, here))
        outer_ref[:, here] = rows_of(blurred, edges)
        inner = seen_ref[radius : columns - radius, here] * blurred[2 * radius : columns]
        inner_ref[:, here] = inner
        result_ref[:, here] = left_product(ahead_ref[...], inner)


def middle_late_kernel(parts, radius, count, where, back_ref, ahead_ref, *refs):
    (other_ref, sibling_ref, outer_ref, result_ref), refs = refs[:4], refs[4:]
    seen_ref, seen_other_ref, seen_sibling_ref, estimate_ref, *part_refs = refs
    columns, length = seen_ref.shape
    wide = columns + 2 * radius
    edges = [(0, 2 * radius), (wide - 2 * radius, 2 * radius)]
    odd = where[2 * count] == 1
    rows = size_of(parts[0])
    for at in range(0, length, STEP):
        here = slice(at, at + STEP)
        sides = assembled([], odd, [], [(other_ref, sibling_ref)], here)
        seen = assembled([[(0, columns)]], odd, [seen_ref], [(seen_other_ref, seen_sibling_ref)], here)
        outer = rows_of(seen, edges) * (outer_ref[:, here] + left_product(back_ref[...], sides))
        estimate_ref[:, here] = outer
        result = result_ref[:rows, here] + left_product(ahead_ref[...], outer)
        place = 0
        for part_ref in part_refs:
            chunk = part_ref.shape[0]
            part_ref[:, here] = result[place : place + chunk]
            place += chunk


def middle_rest_kernel(parts, radius, where, ahead_ref, outer_ref, inner_ref, result_ref, _, estimate_ref, *part_refs):
    length = outer_ref.shape[1]
    rows = size_of(parts[0])
    for at in range(0, length, STEP):
        here = slice(at, at + STEP)
        outer = outer_ref[:, here]
        estimate_ref[:, here] = jnp.concatenate(
            [outer[radius : 2 * radius], inner_ref[:, here], outer[2 * radius : 3 * radius]], axis=0
        )
        if part_refs:
            result = result_ref[rows:, here] + left_product(ahead_ref[...], outer)
        place = 0
        for part_ref in part_refs:
            chunk = part_ref.shape[0]
            part_ref[:, here] = result[place : place + chunk]
            place += chunk


def last_early_kernel(parts, radius, count, where, back_ref, estimate_ref, *refs):
    outer_ref, inner_ref, *own_refs = refs[len(parts) * count :]
    put_parts(where, count, refs, own_refs)
    columns, length = estimate_ref.shape
    edges = [(0, radius), (columns - radius, radius)]
    for at in range(0, length, STEP):
        here = slice(at, at + STEP)
        blurred = left_product(back_ref[...], assembled(parts, None, own_refs, [], here))
        outer_ref[:, here] = rows_of(blurred, edges)
        inner_ref[:, here] = estimate_ref[radius : columns - radius, here] * blurred[radius : columns - radius]


def last_late_kernel(
    radius, count, where, back_ref, other_ref, sibling_ref, outer_ref, inner_ref, estimate_ref, out_hbm, out_ref, sems
):
    columns, length = estimate_ref.shape
    odd = where[2 * count] == 1
    edges = [(0, radius), (columns - radius, radius)]
    pieces = sems.shape[0]
    piece = length // pieces
    copies = []
    for at in range(0, length, STEP):
        here = slice(at, at + STEP)
        sides = assembled([], odd, [], [(other_ref, sibling_ref)], here)
        outer = rows_of(estimate_ref[:, here], edges) * (outer_ref[:, here] + left_product(back_ref[...], sides))
        estimate = jnp.concatenate([outer[:radius], inner_ref[:, here], outer[radius:]], axis=0)
        for tile in range(0, STEP, LANES):
            out_ref[at + tile : at + tile + LANES, :] = jnp.transpose(estimate[:, tile : tile + LANES])
            if (at + tile + LANES) % piece == 0:
                k = (at + tile) // piece
                lines = pl.ds(k * piece, piece)
                copies.append(pltpu.make_async_copy(out_ref.at[lines], out_hbm.at[lines], sems.at[k]))
                copies[-1].start()
    for copy in copies:
        copy.wait()


def put_lines(ref, lines, value):
    for tile in range(ref.shape[0]):
        ref[tile, lines, :] = value[:, tile * LANES : (tile + 1) * LANES]


def get_lines(ref, lines):
    return jnp.concatenate([ref[tile, lines, :] for tile in range(ref.shape[0])], axis=1)


def fill(sizes, where, part_refs, first, chunk, held_ref):
    groups, beside = sizes[:2]
    count = groups * beside
    tiles = part_refs[0].shape[1] // LANES
    for (dz, dx), part_ref in zip(offsets_of(groups, beside), part_refs):
        source_z = lax.rem(where[2 * count + 1] + groups - dz, groups)
        source_x = lax.rem(where[2 * count + 2] + beside - dx, beside)
        for t in range(tiles):
            place = pl.multiple_of((source_z * tiles + t) * chunk, chunk)
            held_ref[source_x, pl.ds(place, chunk), :] = part_ref[first : first + chunk, t * LANES : (t + 1) * LANES]


def planes_kernel(
    sizes, first, seen_first, where, rows_ahead_ref, rows_back_ref, planes_ahead_ref, planes_back_ref, *refs
):
    groups, beside, _, _, rows, _ = sizes
    count = groups * beside
    part_refs, refs = refs[:count], refs[count:]
    begins = seen_first is not None
    if begins:
        seen_refs, refs = refs[:count], refs[count:]
        out_refs, (seen_ref, held_ref, field_ref, other_ref) = refs[:count], refs[count:]
    else:
        seen_ref, out_refs, (held_ref, field_ref, other_ref) = refs[0], refs[1 : count + 1], refs[count + 1 :]
    chunk, length = out_refs[0].shape
    tiles = length // LANES
    per = LANES // rows
    width = beside * rows
    planes = groups * tiles * per
    if begins:
        fill(sizes, where, seen_refs, seen_first, chunk, held_ref)
        for at in range(groups * tiles):
            for k in range(per):
                lines = slice(at * chunk, (at + 1) * chunk)
                pieces = [held_ref[b, lines, k * rows : (k + 1) * rows] for b in range(beside)]
                place = (at * per + k) * chunk
                put_lines(seen_ref, slice(place, place + chunk), jnp.concatenate(pieces, axis=1))
    fill(sizes, where, part_refs, first, chunk, held_ref)

    group = min(tiles, max(1, 4 * LANES // chunk))
    for at in range(0, groups * tiles, group):
        here = slice(at * chunk, (at + group) * chunk)
        left = jnp.concatenate([held_ref[b, here, :] for b in range(beside)], axis=1)
        result = right_product(left, rows_ahead_ref[...])
        for g in range(group):
            for k in range(per):
                place = ((at + g) * per + k) * chunk
                part = result[g * chunk : (g + 1) * chunk, k * width : (k + 1) * width]
                put_lines(field_ref, slice(place, place + chunk), part)

    for y in range(0, chunk, 2):
        lines = [pl.ds(y + k, planes, stride=chunk) for k in range(2)]
        value = jnp.concatenate([get_lines(field_ref, line) for line in lines], axis=1)
        seen = jnp.concatenate([get_lines(seen_ref, line) for line in lines], axis=1)
        value = left_product(planes_back_ref[...], seen / left_product(planes_ahead_ref[...], value))
        for k, line in enumerate(lines):
            put_lines(other_ref, line, value[:, k * width : (k + 1) * width])

    offsets = offsets_of(groups, beside)
    for dz in range(groups):
        target_z = lax.rem(where[2 * count + 1] + dz, groups)
        for at in range(0, tiles, group):
            pieces = []
            for g in range(group):
                line = []
                for k in range(per):
                    place = pl.multiple_of(((target_z * tiles + at + g) * per + k) * chunk, chunk)
                    line.append(get_lines(other_ref, pl.ds(place, chunk)))
                pieces.append(jnp.concatenate(line, axis=1))
            left = jnp.concatenate(pieces, axis=0)
            result = right_product(left, rows_back_ref[...])
            for dx in range(beside):
                for g in range(group):
                    out_refs[offsets.index((dz, dx))][:, (at + g) * LANES : (at + g + 1) * LANES] = result[
                        g * chunk : (g + 1) * chunk, dx * LANES : (dx + 1) * LANES
                    ]


def per_device(observed, psf_z, psf_x, psf_y):
    groups, beside, along = (lax.axis_size(axis) for axis in ("gz", "bx", "by"))
    count = groups * beside
    planes, rows, columns = observed.shape
    length = planes * rows
    radius = psf_z.shape[0] // 2
    sizes = (groups, beside, radius, planes, rows, columns)
    width = beside * rows
    parts = parts_of(columns, radius, count)
    chunks = [size_of(runs) // count for runs in parts]

    offsets = offsets_of(groups, beside)

    def exchanged(values):
        result = [values[0]]
        for (dz, dx), value in list(zip(offsets, values))[1:]:
            pairs = [
                (z * beside + x, ((z + dz) % groups) * beside + (x + dx) % beside)
                for z in range(groups)
                for x in range(beside)
            ]
            result.append(lax.ppermute(value, ("gz", "bx"), pairs))
        return result

    def from_sides(sibling, other):
        result = []
        for value, first in ((other, 1), (sibling, 0)):
            pairs = [(i, i + 1) for i in range(first, along - 1, 2)]
            result.append(lax.ppermute(value, "by", pairs + [(j, i) for i, j in pairs]))
        return result

    line = (1, psf_z.shape[0])
    psf_z, psf_x, psf_y = psf_z.reshape(line), psf_x.reshape(line), psf_y.reshape(line)
    order = pltpu.VMEM((2, columns, columns + 2 * radius), F32)
    block = sum(chunks)
    pieces = 4
    seen, sibling, other, *parcels = call(
        1.3,
        functools.partial(start_kernel, parts, radius, count),
        [shaped(columns, length), shaped(radius, length), shaped(radius, length)]
        + [shaped(block + sum(chunks[1:]), length)] * count,
        [HBM, HBM],
        [order, pltpu.VMEM(line, F32), pltpu.VMEM((length, columns), F32), pltpu.SemaphoreType.DMA((pieces + 1,))],
    )(stays(psf_y), stays(observed.reshape(length, columns)))
    seen_sides = from_sides(sibling, other)
    parcels = exchanged(parcels)

    def left(rows, width):
        return jax.ShapeDtypeStruct((rows, 3 * width), BF16)

    def right(rows, width):
        return jax.ShapeDtypeStruct((3 * rows, width), BF16)

    span = 2 * radius // len(parts)
    across = LANES // rows * width
    first, back_early, back_late, ahead_early, ahead_late, ahead_rest, end_early, end_late, *weights = call(
        0.8,
        functools.partial(weights_kernel, sizes, parts),
        [
            left(size_of(parts[0]), columns + 2 * radius),
            left(columns + 2 * radius, columns + 4 * radius - 2 * span),
            left(4 * radius, 2 * span),
            left(columns, columns - 2 * radius),
            left(size_of(parts[0]), 4 * radius),
            left(size_of(parts[-1]), 4 * radius),
            left(columns, columns),
            left(2 * radius, 2 * radius),
            right(beside * LANES, across),
            right(across, beside * LANES),
            left(groups * planes, groups * planes),
            left(groups * planes, groups * planes),
        ],
        [VMEM] * 3,
        [order],
    )(psf_z, psf_x, psf_y)
    outer = exchanged(
        call(
            0.8,
            first_y_kernel,
            [shaped(chunks[0], length)] * count,
            [VMEM] * 4,
        )(first, seen, *seen_sides)
    )

    def through_planes(values, first, chunk, seen_values, seen_first=None):
        lines = groups * planes * chunk
        across = (width // LANES, lines, LANES)
        begins = seen_first is not None
        result = call(
            50,
            functools.partial(planes_kernel, sizes, first, seen_first),
            [shaped(chunk, length)] * count + [shaped(*across)] * begins,
            [VMEM] * (4 + len(values) + len(seen_values)),
            [
                pltpu.VMEM((beside, groups * (length // LANES) * chunk, LANES), F32),
                pltpu.VMEM(across, F32),
                pltpu.VMEM(across, F32),
            ],
        )(*weights, *values, *seen_values)
        return result[:count], result[count:] if begins else seen_values

    def sides_of(cost, values, span, after):
        sides = call(
            cost,
            functools.partial(sides_kernel, count),
            [shaped(span, length)] * 2,
            [VMEM] * (count + 1),
        )(*values, after)
        return from_sides(*sides)

    fields, across, sides = ([None] * len(parts) for _ in range(3))
    before = 0
    for k in reversed(range(len(parts))):
        values, first = (parcels, before + chunks[k]) if k else (outer, 0)
        fields[k], across[k] = through_planes(values, first, chunks[k], parcels, before)
        fields[k] = exchanged(fields[k])
        before += chunks[k] * (2 if k else 1)
    for k in reversed(range(len(parts))):
        sides[k] = sides_of(50, fields[k], span, fields[0][0])
    partial = [shaped(4 * radius, length), shaped(columns - 2 * radius, length), shaped(columns, length)]
    partial = call(
        2.2,
        functools.partial(middle_early_kernel, parts, radius, count),
        partial,
        [VMEM] * (1 + (count + 2) * len(parts)),
        [pltpu.VMEM((size_of(runs), length), F32) for runs in parts],
    )(back_early, ahead_early, *flat(fields), *flat(sides[1:]), seen)
    estimate, *values = call(
        0.8,
        functools.partial(middle_late_kernel, parts, radius, count),
        [shaped(4 * radius, length)] + [shaped(chunks[0], length)] * count,
        [VMEM] * 9,
    )(back_late, ahead_late, *sides[0], partial[0], partial[2], seen, *seen_sides)
    fields[0] = exchanged(values)
    estimate, *values = call(
        50,
        functools.partial(middle_rest_kernel, parts, radius),
        [shaped(columns, length)] + [shaped(chunk, length) for chunk in chunks[1:] for _ in range(count)],
        [VMEM] * 5,
    )(ahead_rest, estimate, *partial[1:], fields[0][0])
    if len(parts) > 1:
        fields[1] = exchanged(values)
    for k in range(len(parts)):
        values, _ = through_planes(fields[k], 0, chunks[k], across[k])
        fields[k] = exchanged(values)
    sides = sides_of(0.6, fields[0], radius, fields[-1][0])
    partial = call(
        50,
        functools.partial(last_early_kernel, parts, radius, count),
        [shaped(2 * radius, length), shaped(columns - 2 * radius, length)],
        [VMEM] * (2 + count * len(parts)),
        [pltpu.VMEM((size_of(runs), length), F32) for runs in parts],
    )(end_early, estimate, *flat(fields))
    out = call(
        1.5,
        functools.partial(last_late_kernel, radius, count),
        shaped(length, columns),
        [VMEM] * 6,
        [pltpu.VMEM((length, columns), F32), pltpu.SemaphoreType.DMA((pieces,))],
        HBM,
    )(end_late, *sides, *partial, estimate)
    return out.reshape(planes, rows, columns)


def solution(mesh):
    placed = (P("gz", "bx", "by"), P(), P(), P())
    return jax.shard_map(
        per_device, mesh=mesh, in_specs=placed, out_specs=P("gz", "bx", "by"), check_vma=False
    )
```

```python
import functools
import jax
import jax.numpy as jnp
from jax import lax
from jax.experimental import pallas as pl
from jax.experimental.pallas import tpu as pltpu
from jax.sharding import PartitionSpec as P

LANES = 128
RATE = 1150 * 1000 * 1000
STEP = 4 * LANES
F32 = jnp.float32
BF16 = jnp.bfloat16
VMEM = pl.BlockSpec(memory_space=pltpu.VMEM)
HBM = pl.BlockSpec(memory_space=pltpu.HBM)


def shaped(*shape):
    return jax.ShapeDtypeStruct(shape, F32)


def stays(value):
    return pltpu.with_memory_space_constraint(value, pltpu.HBM)


def call(cost, kernel, outs, specs, scratch=(), place=VMEM):
    return pl.pallas_call(
        lambda *refs: kernel(place_of_device(), *refs),
        out_shape=outs,
        in_specs=specs,
        out_specs=jax.tree.map(lambda _: place, outs),
        scratch_shapes=list(scratch),
        compiler_params=pltpu.CompilerParams(vmem_limit_bytes=16 * 1024 * 1024),
        cost_estimate=pl.CostEstimate(flops=int(cost * RATE), bytes_accessed=0, transcendentals=0),
    )


def parts_of(columns, radius, count):
    outer = [(0, radius), (columns - radius, radius)]
    inner = [(radius, columns - 2 * radius)]
    fits = columns >= 3 * radius and count % 2 == 0
    for runs in (outer, inner):
        fits = fits and sum(size for _, size in runs) % (8 * count) == 0
    return [outer, inner] if fits else [[(0, columns)]]


def flat(lists):
    return [value for values in lists for value in values]


def size_of(runs):
    return sum(size for _, size in runs)


def rows_of(value, runs):
    return jnp.concatenate([value[start : start + size] for start, size in runs], axis=0)


def place_of(runs, offset):
    place, before = runs[0][0] + offset, 0
    for (start, size), (after, _) in zip(runs, runs[1:]):
        before += size
        place = jnp.where(offset >= before, after - before + offset, place)
    return place


def offsets_of(groups, beside):
    offsets = [(dz, dx) for dz in range(groups) for dx in range(beside)]
    return offsets[:1] + sorted(offsets[1:], key=lambda offset: offset.count(0))


def place_of_device():
    groups, beside = lax.axis_size("gz"), lax.axis_size("bx")
    me_z, me_x = lax.axis_index("gz"), lax.axis_index("bx")
    offsets = offsets_of(groups, beside)
    ahead = [lax.rem(me_z + dz, groups) * beside + lax.rem(me_x + dx, beside) for dz, dx in offsets]
    behind = [
        lax.rem(me_z + groups - dz, groups) * beside + lax.rem(me_x + beside - dx, beside) for dz, dx in offsets
    ]
    me_y, odd = lax.axis_index("by"), lax.rem(lax.axis_index("by"), 2)
    other = me_y + 2 * odd - 1
    alone = jnp.where((other < 0) | (other >= lax.axis_size("by")), 1, 0)
    return ahead + behind + [odd, me_z, me_x, alone]


def split(value):
    high = value.astype(BF16)
    return high, (value - high.astype(F32)).astype(BF16)


def dot(left, right):
    return lax.dot_general(left, right, (((1,), (0,)), ((), ())), preferred_element_type=F32)


def banded(taps, rows, width, start):
    room = (width + 2 * LANES - 1) // LANES * LANES
    base = jnp.concatenate([taps, jnp.zeros((1, room - LANES), F32)], axis=1)
    base = jnp.broadcast_to(base, (rows, room))
    return pltpu.roll(base, start % room, 1, stride=1, stride_axis=0)[:, :width]


def as_left(matrix):
    high, low = split(matrix)
    return jnp.concatenate([high, high, low], axis=1)


def left_product(matrix, value):
    high, low = split(value)
    return dot(matrix, jnp.concatenate([high, low, high], axis=0))


def as_right(matrix):
    high, low = split(matrix)
    return jnp.concatenate([high, high, low], axis=0)


def right_product(value, matrix):
    high, low = split(value)
    return dot(jnp.concatenate([high, low, high], axis=1), matrix)


def ordered_rows(matrix, where, order_ref, runs, count):
    size = size_of(runs)
    chunk = size // count
    width = matrix.shape[1]
    order_ref[0, :size, :width] = rows_of(matrix, runs)
    for slot in range(count):
        place = pl.multiple_of(where[slot] * chunk, chunk)
        order_ref[1, slot * chunk : (slot + 1) * chunk, :width] = order_ref[0, pl.ds(place, chunk), :width]
    return order_ref[1, :size, :width]


def columns_of(matrix, runs):
    return jnp.concatenate([matrix[:, start : start + size] for start, size in runs], axis=1)


def taps_of(psf_ref):
    count = psf_ref.shape[1]
    row = lax.broadcasted_iota(jnp.int32, (LANES, LANES), 0)
    lane = lax.broadcasted_iota(jnp.int32, (LANES, LANES), 1)
    taps = psf_ref[...] / jnp.sum(psf_ref[...], axis=1, keepdims=True)
    taps = jnp.concatenate([taps, jnp.zeros((1, LANES - count), F32)], axis=1)
    column = jnp.transpose(jnp.broadcast_to(taps, (LANES, LANES)))
    return taps, jnp.sum(jnp.where(row + lane == count - 1, column, 0.0), axis=0, keepdims=True)


def weights_kernel(
    sizes,
    parts,
    where,
    psf_z_ref,
    psf_x_ref,
    psf_y_ref,
    first_ref,
    back_early_ref,
    back_late_ref,
    ahead_early_ref,
    ahead_late_ref,
    ahead_rest_ref,
    end_early_ref,
    end_late_ref,
    rows_ahead_ref,
    rows_back_ref,
    planes_ahead_ref,
    planes_back_ref,
    order_ref,
):
    groups, beside, radius, depth, rows, columns = sizes
    count = groups * beside
    taps, turned = taps_of(psf_y_ref)
    wide = columns + 2 * radius
    span = 2 * radius // len(parts)
    edges = [(0, 2 * radius), (wide - 2 * radius, 2 * radius)]
    rest_rows = ahead_rest_ref.shape[0]

    ahead = banded(taps, columns, wide, 0)
    ahead = jnp.concatenate([ordered_rows(ahead, where, order_ref, runs, count) for runs in parts], axis=0)
    first_ref[...] = as_left(ahead[: size_of(parts[0])])
    ahead_early_ref[...] = as_left(ahead[:, 2 * radius : columns])
    ahead = columns_of(ahead, edges)
    ahead_late_ref[...] = as_left(ahead[: size_of(parts[0])])
    ahead_rest_ref[...] = as_left(ahead[-rest_rows:])
    back = banded(turned, wide, wide + 2 * radius, 0)
    late = [(2 * radius - span, span), (columns + 2 * radius, span)]
    early = [(0, 2 * radius - span), (2 * radius, columns), (columns + 2 * radius + span, 2 * radius - span)]
    back_early_ref[...] = as_left(columns_of(back, [run for run in early if run[1]]))
    back_late_ref[...] = as_left(columns_of(rows_of(back, edges), late))
    back = banded(turned, columns, wide, 0)
    end_early_ref[...] = as_left(back[:, radius : radius + columns])
    edges = [(0, radius), (columns - radius, radius)]
    end_late_ref[...] = as_left(columns_of(rows_of(back, edges), [(0, radius), (columns + radius, radius)]))

    per = LANES // rows
    width = beside * rows
    taps, turned = taps_of(psf_x_ref)
    ahead = banded(turned, width, width, -radius)
    back = banded(taps, width, width, -radius)
    blocks = []
    for b in range(beside):
        for k in range(per):
            line = [jnp.zeros((rows, width), F32)] * per
            line[k] = ahead[b * rows : (b + 1) * rows]
            blocks.append(jnp.concatenate(line, axis=1))
    rows_ahead_ref[...] = as_right(jnp.concatenate(blocks, axis=0))
    for b in range(beside):
        blocks = []
        for k in range(per):
            line = [jnp.zeros((width, rows), F32)] * per
            line[k] = back[:, b * rows : (b + 1) * rows]
            blocks.append(jnp.concatenate(line, axis=1))
        slot = lax.rem(b + beside - where[2 * count + 2], beside)
        rows_back_ref[:, pl.ds(pl.multiple_of(slot * LANES, LANES), LANES)] = as_right(jnp.concatenate(blocks, axis=0))
    planes = groups * depth
    for ref, line in zip((planes_ahead_ref, planes_back_ref), taps_of(psf_z_ref)):
        ref[...] = as_left(banded(line, planes, planes, -radius))


def send_sides(where, count, value_ref, span, sibling_ref, other_ref):
    odd = where[2 * count]
    room = value_ref.shape[0] - span
    sibling_ref[...] = value_ref[pl.ds(pl.multiple_of((1 - odd) * room, 8), span), :]
    other_ref[...] = value_ref[pl.ds(pl.multiple_of(odd * room, 8), span), :]


def start_kernel(parts, radius, count, where, psf_hbm, block_hbm, *refs):
    own_ref, sibling_ref, other_ref = refs[:3]
    part_refs, (order_ref, psf_ref, block_ref, sems) = refs[3:-4], refs[-4:]
    length, columns = block_ref.shape
    pieces = sems.shape[0] - 1
    piece = length // pieces
    copies = [pltpu.make_async_copy(psf_hbm, psf_ref, sems.at[pieces])]
    for k in range(pieces):
        here = pl.ds(k * piece, piece)
        copies.append(pltpu.make_async_copy(block_hbm.at[here], block_ref.at[here], sems.at[k]))
    for copy in copies:
        copy.start()
    copies[0].wait()
    taps, _ = taps_of(psf_ref)
    matrices = [None]
    for runs in parts[1:]:
        matrix = banded(taps, columns, columns, -radius)
        matrices.append(as_left(ordered_rows(matrix, where, order_ref, runs, count)))
    for k in range(pieces):
        copies[k + 1].wait()
        for at in range(k * piece, (k + 1) * piece, LANES):
            own_ref[:, at : at + LANES] = jnp.transpose(block_ref[at : at + LANES, :])
    send_sides(where, count, own_ref, radius, sibling_ref, other_ref)
    before = 0
    for k, runs in reversed(list(enumerate(parts))):
        chunk = size_of(runs) // count
        for slot, part_ref in enumerate(part_refs):
            place = pl.multiple_of(place_of(runs, where[slot] * chunk), 8)
            part_ref[before : before + chunk, :] = own_ref[pl.ds(place, chunk), :]
        before += chunk
        if k:
            for at in range(0, length, STEP):
                here = slice(at, at + STEP)
                result = left_product(matrices[k], own_ref[:, here])
                for slot, part_ref in enumerate(part_refs):
                    part_ref[before : before + chunk, here] = result[slot * chunk : (slot + 1) * chunk]
            before += chunk


def first_y_kernel(where, matrix_ref, own_ref, other_ref, sibling_ref, *part_refs):
    columns, length = own_ref.shape
    count = len(part_refs)
    chunk = part_refs[0].shape[0]
    odd = where[2 * count] == 1, where[2 * count + 3] == 1
    for at in range(0, length, STEP):
        here = slice(at, at + STEP)
        field = assembled([[(0, columns)]], odd, [own_ref], [(other_ref, sibling_ref)], here)
        result = left_product(matrix_ref[...], field)
        for slot, part_ref in enumerate(part_refs):
            part_ref[:, here] = result[slot * chunk : (slot + 1) * chunk]


def put_parts(where, count, part_refs, own_refs):
    for k, own_ref in enumerate(own_refs):
        for slot, part_ref in enumerate(part_refs[k * count : (k + 1) * count]):
            chunk = part_ref.shape[0]
            place = pl.multiple_of(where[count + slot] * chunk, chunk)
            own_ref[pl.ds(place, chunk), :] = part_ref[...]


def sides_kernel(count, where, *refs):
    part_refs, (_, sibling_ref, other_ref) = refs[:count], refs[count:]
    span = sibling_ref.shape[0]
    chunk = part_refs[0].shape[0]
    odd = where[2 * count]
    for slot, part_ref in enumerate(part_refs):
        start = where[count + slot] * chunk
        for first, to_sibling in ((0, odd), (count * chunk - span, 1 - odd)):
            inside = (start >= first) & (start < first + span)

            def put(ref, start=start, first=first, part_ref=part_ref):
                ref[pl.ds(pl.multiple_of(start - first, 8), chunk), :] = part_ref[...]

            pl.when(inside & (to_sibling == 1))(functools.partial(put, sibling_ref))
            pl.when(inside & (to_sibling == 0))(functools.partial(put, other_ref))


def assembled(parts, odd, own_refs, side_refs, here):
    pieces = {}
    for runs, ref in zip(parts, own_refs):
        at = 0
        for start, size in runs:
            pieces[start] = ref[at : at + size] if isinstance(ref, jax.Array) else ref[at : at + size, here]
            at += size
    own = [pieces[start] for start in sorted(pieces)]
    low, high = [], []
    odd, alone = odd or (None, None)
    for other_ref, sibling_ref in side_refs:
        sibling, other = sibling_ref[:, here], jnp.where(alone, 0.0, other_ref[:, here])
        low.insert(0, jnp.where(odd, sibling, other))
        high.append(jnp.where(odd, other, sibling))
    return jnp.concatenate(low + own + high, axis=0)


def middle_early_kernel(parts, radius, count, where, back_ref, ahead_ref, *refs):
    kinds = len(parts)
    own_refs, refs = refs[-kinds:], refs[:-kinds]
    put_parts(where, count, refs, own_refs)
    refs = refs[kinds * count :]
    side_refs = [refs[2 * k : 2 * k + 2] for k in range(kinds - 1)]
    seen_ref, outer_ref, inner_ref, result_ref = refs[2 * kinds - 2 :]
    columns, length = seen_ref.shape
    wide = columns + 2 * radius
    edges = [(0, 2 * radius), (wide - 2 * radius, 2 * radius)]
    odd = where[2 * count] == 1, where[2 * count + 3] == 1
    for at in range(0, length, STEP):
        here = slice(at, at + STEP)
        blurred = left_product(back_ref[...], assembled(parts, odd, own_refs, side_refs, here))
        outer_ref[:, here] = rows_of(blurred, edges)
        inner = seen_ref[radius : columns - radius, here] * blurred[2 * radius : columns]
        inner_ref[:, here] = inner
        result_ref[:, here] = left_product(ahead_ref[...], inner)


def middle_late_kernel(parts, radius, count, where, back_ref, ahead_ref, *refs):
    (other_ref, sibling_ref, outer_ref, result_ref), refs = refs[:4], refs[4:]
    seen_ref, seen_other_ref, seen_sibling_ref, estimate_ref, *part_refs = refs
    columns, length = seen_ref.shape
    wide = columns + 2 * radius
    edges = [(0, 2 * radius), (wide - 2 * radius, 2 * radius)]
    odd = where[2 * count] == 1, where[2 * count + 3] == 1
    rows = size_of(parts[0])
    for at in range(0, length, STEP):
        here = slice(at, at + STEP)
        sides = assembled([], odd, [], [(other_ref, sibling_ref)], here)
        seen = assembled([[(0, columns)]], odd, [seen_ref], [(seen_other_ref, seen_sibling_ref)], here)
        outer = rows_of(seen, edges) * (outer_ref[:, here] + left_product(back_ref[...], sides))
        estimate_ref[:, here] = outer
        result = result_ref[:rows, here] + left_product(ahead_ref[...], outer)
        place = 0
        for part_ref in part_refs:
            chunk = part_ref.shape[0]
            part_ref[:, here] = result[place : place + chunk]
            place += chunk


def middle_rest_kernel(parts, radius, where, ahead_ref, outer_ref, inner_ref, result_ref, _, estimate_ref, *part_refs):
    length = outer_ref.shape[1]
    rows = size_of(parts[0])
    for at in range(0, length, STEP):
        here = slice(at, at + STEP)
        outer = outer_ref[:, here]
        estimate_ref[:, here] = jnp.concatenate(
            [outer[radius : 2 * radius], inner_ref[:, here], outer[2 * radius : 3 * radius]], axis=0
        )
        if part_refs:
            result = result_ref[rows:, here] + left_product(ahead_ref[...], outer)
        place = 0
        for part_ref in part_refs:
            chunk = part_ref.shape[0]
            part_ref[:, here] = result[place : place + chunk]
            place += chunk


def last_early_kernel(parts, radius, count, where, back_ref, estimate_ref, *refs):
    outer_ref, inner_ref, *own_refs = refs[len(parts) * count :]
    put_parts(where, count, refs, own_refs)
    columns, length = estimate_ref.shape
    edges = [(0, radius), (columns - radius, radius)]
    for at in range(0, length, STEP):
        here = slice(at, at + STEP)
        blurred = left_product(back_ref[...], assembled(parts, None, own_refs, [], here))
        outer_ref[:, here] = rows_of(blurred, edges)
        inner_ref[:, here] = estimate_ref[radius : columns - radius, here] * blurred[radius : columns - radius]


def last_late_kernel(
    radius, count, where, back_ref, other_ref, sibling_ref, outer_ref, inner_ref, estimate_ref, out_hbm, out_ref, sems
):
    columns, length = estimate_ref.shape
    odd = where[2 * count] == 1, where[2 * count + 3] == 1
    edges = [(0, radius), (columns - radius, radius)]
    pieces = sems.shape[0]
    piece = length // pieces
    copies = []
    for at in range(0, length, STEP):
        here = slice(at, at + STEP)
        sides = assembled([], odd, [], [(other_ref, sibling_ref)], here)
        outer = rows_of(estimate_ref[:, here], edges) * (outer_ref[:, here] + left_product(back_ref[...], sides))
        estimate = jnp.concatenate([outer[:radius], inner_ref[:, here], outer[radius:]], axis=0)
        for tile in range(0, STEP, LANES):
            out_ref[at + tile : at + tile + LANES, :] = jnp.transpose(estimate[:, tile : tile + LANES])
            if (at + tile + LANES) % piece == 0:
                k = (at + tile) // piece
                lines = pl.ds(k * piece, piece)
                copies.append(pltpu.make_async_copy(out_ref.at[lines], out_hbm.at[lines], sems.at[k]))
                copies[-1].start()
    for copy in copies:
        copy.wait()


def put_lines(ref, lines, value):
    for tile in range(ref.shape[0]):
        ref[tile, lines, :] = value[:, tile * LANES : (tile + 1) * LANES]


def get_lines(ref, lines):
    return jnp.concatenate([ref[tile, lines, :] for tile in range(ref.shape[0])], axis=1)


def fill(sizes, where, part_refs, first, chunk, held_ref):
    groups, beside = sizes[:2]
    count = groups * beside
    tiles = part_refs[0].shape[1] // LANES
    for (dz, dx), part_ref in zip(offsets_of(groups, beside), part_refs):
        source_z = lax.rem(where[2 * count + 1] + groups - dz, groups)
        source_x = lax.rem(where[2 * count + 2] + beside - dx, beside)
        for t in range(tiles):
            place = pl.multiple_of((source_z * tiles + t) * chunk, chunk)
            held_ref[source_x, pl.ds(place, chunk), :] = part_ref[first : first + chunk, t * LANES : (t + 1) * LANES]


def planes_kernel(
    sizes, first, seen_first, where, rows_ahead_ref, rows_back_ref, planes_ahead_ref, planes_back_ref, *refs
):
    groups, beside, _, _, rows, _ = sizes
    count = groups * beside
    part_refs, refs = refs[:count], refs[count:]
    begins = seen_first is not None
    if begins:
        seen_refs, refs = refs[:count], refs[count:]
        out_refs, (seen_ref, held_ref, field_ref, other_ref) = refs[:count], refs[count:]
    else:
        seen_ref, out_refs, (held_ref, field_ref, other_ref) = refs[0], refs[1 : count + 1], refs[count + 1 :]
    chunk, length = out_refs[0].shape
    tiles = length // LANES
    per = LANES // rows
    width = beside * rows
    planes = groups * tiles * per
    if begins:
        fill(sizes, where, seen_refs, seen_first, chunk, held_ref)
        for at in range(groups * tiles):
            for k in range(per):
                lines = slice(at * chunk, (at + 1) * chunk)
                pieces = [held_ref[b, lines, k * rows : (k + 1) * rows] for b in range(beside)]
                place = (at * per + k) * chunk
                put_lines(seen_ref, slice(place, place + chunk), jnp.concatenate(pieces, axis=1))
    fill(sizes, where, part_refs, first, chunk, held_ref)

    group = min(tiles, max(1, 4 * LANES // chunk))
    for at in range(0, groups * tiles, group):
        here = slice(at * chunk, (at + group) * chunk)
        left = jnp.concatenate([held_ref[b, here, :] for b in range(beside)], axis=1)
        result = right_product(left, rows_ahead_ref[...])
        for g in range(group):
            for k in range(per):
                place = ((at + g) * per + k) * chunk
                part = result[g * chunk : (g + 1) * chunk, k * width : (k + 1) * width]
                put_lines(field_ref, slice(place, place + chunk), part)

    for y in range(0, chunk, 2):
        lines = [pl.ds(y + k, planes, stride=chunk) for k in range(2)]
        value = jnp.concatenate([get_lines(field_ref, line) for line in lines], axis=1)
        seen = jnp.concatenate([get_lines(seen_ref, line) for line in lines], axis=1)
        value = left_product(planes_back_ref[...], seen / left_product(planes_ahead_ref[...], value))
        for k, line in enumerate(lines):
            put_lines(other_ref, line, value[:, k * width : (k + 1) * width])

    offsets = offsets_of(groups, beside)
    for dz in range(groups):
        target_z = lax.rem(where[2 * count + 1] + dz, groups)
        for at in range(0, tiles, group):
            pieces = []
            for g in range(group):
                line = []
                for k in range(per):
                    place = pl.multiple_of(((target_z * tiles + at + g) * per + k) * chunk, chunk)
                    line.append(get_lines(other_ref, pl.ds(place, chunk)))
                pieces.append(jnp.concatenate(line, axis=1))
            left = jnp.concatenate(pieces, axis=0)
            result = right_product(left, rows_back_ref[...])
            for dx in range(beside):
                for g in range(group):
                    out_refs[offsets.index((dz, dx))][:, (at + g) * LANES : (at + g + 1) * LANES] = result[
                        g * chunk : (g + 1) * chunk, dx * LANES : (dx + 1) * LANES
                    ]


def per_device(observed, psf_z, psf_x, psf_y):
    groups, beside, along = (lax.axis_size(axis) for axis in ("gz", "bx", "by"))
    count = groups * beside
    planes, rows, columns = observed.shape
    length = planes * rows
    radius = psf_z.shape[0] // 2
    sizes = (groups, beside, radius, planes, rows, columns)
    width = beside * rows
    parts = parts_of(columns, radius, count)
    chunks = [size_of(runs) // count for runs in parts]

    offsets = offsets_of(groups, beside)

    def exchanged(values):
        result = [values[0]]
        for (dz, dx), value in list(zip(offsets, values))[1:]:
            pairs = [
                (z * beside + x, ((z + dz) % groups) * beside + (x + dx) % beside)
                for z in range(groups)
                for x in range(beside)
            ]
            result.append(lax.ppermute(value, ("gz", "bx"), pairs))
        return result

    def from_sides(sibling, other, paced=False):
        result = []
        for value, first in ((other, 1), (sibling, 0)):
            pairs = []
            for place in range(count):
                line = [place * along + i for i in range(along)]
                pairs += [(line[i], line[i + 1]) for i in range(first, along - 1, 2)]
                if paced and first and place + beside < count and place // beside % 2 == 0:
                    ends = [0] + [along - 1] * (along % 2 == 0)
                    pairs += [(line[i], line[i] + beside * along) for i in ends]
            result.append(lax.ppermute(value, ("gz", "bx", "by"), pairs + [(j, i) for i, j in pairs]))
        return result

    line = (1, psf_z.shape[0])
    psf_z, psf_x, psf_y = psf_z.reshape(line), psf_x.reshape(line), psf_y.reshape(line)
    order = pltpu.VMEM((2, columns, columns + 2 * radius), F32)
    block = sum(chunks)
    pieces = 4
    seen, sibling, other, *parcels = call(
        1.3,
        functools.partial(start_kernel, parts, radius, count),
        [shaped(columns, length), shaped(radius, length), shaped(radius, length)]
        + [shaped(block + sum(chunks[1:]), length)] * count,
        [HBM, HBM],
        [order, pltpu.VMEM(line, F32), pltpu.VMEM((length, columns), F32), pltpu.SemaphoreType.DMA((pieces + 1,))],
    )(stays(psf_y), stays(observed.reshape(length, columns)))
    seen_sides = from_sides(sibling, other)
    parcels = exchanged(parcels)

    def left(rows, width):
        return jax.ShapeDtypeStruct((rows, 3 * width), BF16)

    def right(rows, width):
        return jax.ShapeDtypeStruct((3 * rows, width), BF16)

    span = 2 * radius // len(parts)
    across = LANES // rows * width
    first, back_early, back_late, ahead_early, ahead_late, ahead_rest, end_early, end_late, *weights = call(
        0.8,
        functools.partial(weights_kernel, sizes, parts),
        [
            left(size_of(parts[0]), columns + 2 * radius),
            left(columns + 2 * radius, columns + 4 * radius - 2 * span),
            left(4 * radius, 2 * span),
            left(columns, columns - 2 * radius),
            left(size_of(parts[0]), 4 * radius),
            left(size_of(parts[-1]), 4 * radius),
            left(columns, columns),
            left(2 * radius, 2 * radius),
            right(beside * LANES, across),
            right(across, beside * LANES),
            left(groups * planes, groups * planes),
            left(groups * planes, groups * planes),
        ],
        [VMEM] * 3,
        [order],
    )(psf_z, psf_x, psf_y)
    outer = exchanged(
        call(
            0.8,
            first_y_kernel,
            [shaped(chunks[0], length)] * count,
            [VMEM] * 4,
        )(first, seen, *seen_sides)
    )

    def through_planes(values, first, chunk, seen_values, seen_first=None):
        lines = groups * planes * chunk
        across = (width // LANES, lines, LANES)
        begins = seen_first is not None
        result = call(
            50,
            functools.partial(planes_kernel, sizes, first, seen_first),
            [shaped(chunk, length)] * count + [shaped(*across)] * begins,
            [VMEM] * (4 + len(values) + len(seen_values)),
            [
                pltpu.VMEM((beside, groups * (length // LANES) * chunk, LANES), F32),
                pltpu.VMEM(across, F32),
                pltpu.VMEM(across, F32),
            ],
        )(*weights, *values, *seen_values)
        return result[:count], result[count:] if begins else seen_values

    def sides_of(cost, values, span, after, paced=False):
        sides = call(
            cost,
            functools.partial(sides_kernel, count),
            [shaped(span, length)] * 2,
            [VMEM] * (count + 1),
        )(*values, after)
        return from_sides(*sides, paced)

    fields, across, sides = ([None] * len(parts) for _ in range(3))
    before = 0
    for k in reversed(range(len(parts))):
        values, first = (parcels, before + chunks[k]) if k else (outer, 0)
        fields[k], across[k] = through_planes(values, first, chunks[k], parcels, before)
        fields[k] = exchanged(fields[k])
        before += chunks[k] * (2 if k else 1)
    for k in reversed(range(len(parts))):
        sides[k] = sides_of(50, fields[k], span, fields[0][0], k == 0)
    partial = [shaped(4 * radius, length), shaped(columns - 2 * radius, length), shaped(columns, length)]
    partial = call(
        2.2,
        functools.partial(middle_early_kernel, parts, radius, count),
        partial,
        [VMEM] * (1 + (count + 2) * len(parts)),
        [pltpu.VMEM((size_of(runs), length), F32) for runs in parts],
    )(back_early, ahead_early, *flat(fields), *flat(sides[1:]), seen)
    estimate, *values = call(
        0.8,
        functools.partial(middle_late_kernel, parts, radius, count),
        [shaped(4 * radius, length)] + [shaped(chunks[0], length)] * count,
        [VMEM] * 9,
    )(back_late, ahead_late, *sides[0], partial[0], partial[2], seen, *seen_sides)
    fields[0] = exchanged(values)
    estimate, *values = call(
        50,
        functools.partial(middle_rest_kernel, parts, radius),
        [shaped(columns, length)] + [shaped(chunk, length) for chunk in chunks[1:] for _ in range(count)],
        [VMEM] * 5,
    )(ahead_rest, estimate, *partial[1:], fields[0][0])
    if len(parts) > 1:
        fields[1] = exchanged(values)
    for k in range(len(parts)):
        values, _ = through_planes(fields[k], 0, chunks[k], across[k])
        fields[k] = exchanged(values)
    sides = sides_of(0.6, fields[0], radius, fields[-1][0])
    partial = call(
        50,
        functools.partial(last_early_kernel, parts, radius, count),
        [shaped(2 * radius, length), shaped(columns - 2 * radius, length)],
        [VMEM] * (2 + count * len(parts)),
        [pltpu.VMEM((size_of(runs), length), F32) for runs in parts],
    )(end_early, estimate, *flat(fields))
    out = call(
        1.5,
        functools.partial(last_late_kernel, radius, count),
        shaped(length, columns),
        [VMEM] * 6,
        [pltpu.VMEM((length, columns), F32), pltpu.SemaphoreType.DMA((pieces,))],
        HBM,
    )(end_late, *sides, *partial, estimate)
    return out.reshape(planes, rows, columns)


def solution(mesh):
    placed = (P("gz", "bx", "by"), P(), P(), P())
    return jax.shard_map(
        per_device, mesh=mesh, in_specs=placed, out_specs=P("gz", "bx", "by"), check_vma=False
    )
```

```python
import functools
import jax
import jax.numpy as jnp
from jax import lax
from jax.experimental import pallas as pl
from jax.experimental.pallas import tpu as pltpu
from jax.sharding import PartitionSpec as P

LANES = 128
RATE = 1150 * 1000 * 1000
STEP = 4 * LANES
F32 = jnp.float32
BF16 = jnp.bfloat16
VMEM = pl.BlockSpec(memory_space=pltpu.VMEM)
HBM = pl.BlockSpec(memory_space=pltpu.HBM)


def shaped(*shape):
    return jax.ShapeDtypeStruct(shape, F32)


def stays(value):
    return pltpu.with_memory_space_constraint(value, pltpu.HBM)


def call(cost, kernel, outs, specs, scratch=(), place=VMEM):
    return pl.pallas_call(
        lambda *refs: kernel(place_of_device(), *refs),
        out_shape=outs,
        in_specs=specs,
        out_specs=jax.tree.map(lambda _: place, outs),
        scratch_shapes=list(scratch),
        compiler_params=pltpu.CompilerParams(vmem_limit_bytes=16 * 1024 * 1024),
        cost_estimate=pl.CostEstimate(flops=int(cost * RATE), bytes_accessed=0, transcendentals=0),
    )


def parts_of(columns, radius, count):
    outer = [(0, radius), (columns - radius, radius)]
    inner = [(radius, columns - 2 * radius)]
    fits = columns >= 3 * radius and count % 2 == 0
    for runs in (outer, inner):
        fits = fits and sum(size for _, size in runs) % (8 * count) == 0
    return [outer, inner] if fits else [[(0, columns)]]


def flat(lists):
    return [value for values in lists for value in values]


def size_of(runs):
    return sum(size for _, size in runs)


def rows_of(value, runs):
    return jnp.concatenate([value[start : start + size] for start, size in runs], axis=0)


def place_of(runs, offset):
    place, before = runs[0][0] + offset, 0
    for (start, size), (after, _) in zip(runs, runs[1:]):
        before += size
        place = jnp.where(offset >= before, after - before + offset, place)
    return place


def offsets_of(groups, beside):
    offsets = [(dz, dx) for dz in range(groups) for dx in range(beside)]
    return offsets[:1] + sorted(offsets[1:], key=lambda offset: offset.count(0))


def place_of_device():
    groups, beside = lax.axis_size("gz"), lax.axis_size("bx")
    me_z, me_x = lax.axis_index("gz"), lax.axis_index("bx")
    offsets = offsets_of(groups, beside)
    ahead = [lax.rem(me_z + dz, groups) * beside + lax.rem(me_x + dx, beside) for dz, dx in offsets]
    behind = [
        lax.rem(me_z + groups - dz, groups) * beside + lax.rem(me_x + beside - dx, beside) for dz, dx in offsets
    ]
    me_y, odd = lax.axis_index("by"), lax.rem(lax.axis_index("by"), 2)
    other = me_y + 2 * odd - 1
    alone = jnp.where((other < 0) | (other >= lax.axis_size("by")), 1, 0)
    return ahead + behind + [odd, me_z, me_x, alone]


def split(value):
    high = value.astype(BF16)
    return high, (value - high.astype(F32)).astype(BF16)


def dot(left, right):
    return lax.dot_general(left, right, (((1,), (0,)), ((), ())), preferred_element_type=F32)


def banded(taps, rows, width, start):
    room = (width + 2 * LANES - 1) // LANES * LANES
    base = jnp.concatenate([taps, jnp.zeros((1, room - LANES), F32)], axis=1)
    base = jnp.broadcast_to(base, (rows, room))
    return pltpu.roll(base, start % room, 1, stride=1, stride_axis=0)[:, :width]


def as_left(matrix):
    high, low = split(matrix)
    return jnp.concatenate([high, high, low], axis=1)


def left_product(matrix, value):
    high, low = split(value)
    return dot(matrix, jnp.concatenate([high, low, high], axis=0))


def as_right(matrix):
    high, low = split(matrix)
    return jnp.concatenate([high, high, low], axis=0)


def right_product(value, matrix):
    high, low = split(value)
    return dot(jnp.concatenate([high, low, high], axis=1), matrix)


def ordered_rows(matrix, where, order_ref, runs, count):
    size = size_of(runs)
    chunk = size // count
    width = matrix.shape[1]
    order_ref[0, :size, :width] = rows_of(matrix, runs)
    for slot in range(count):
        place = pl.multiple_of(where[slot] * chunk, chunk)
        order_ref[1, slot * chunk : (slot + 1) * chunk, :width] = order_ref[0, pl.ds(place, chunk), :width]
    return order_ref[1, :size, :width]


def columns_of(matrix, runs):
    return jnp.concatenate([matrix[:, start : start + size] for start, size in runs], axis=1)


def taps_of(psf_ref):
    count = psf_ref.shape[1]
    row = lax.broadcasted_iota(jnp.int32, (LANES, LANES), 0)
    lane = lax.broadcasted_iota(jnp.int32, (LANES, LANES), 1)
    taps = psf_ref[...] / jnp.sum(psf_ref[...], axis=1, keepdims=True)
    taps = jnp.concatenate([taps, jnp.zeros((1, LANES - count), F32)], axis=1)
    column = jnp.transpose(jnp.broadcast_to(taps, (LANES, LANES)))
    return taps, jnp.sum(jnp.where(row + lane == count - 1, column, 0.0), axis=0, keepdims=True)


def weights_kernel(
    sizes,
    parts,
    where,
    psf_z_ref,
    psf_x_ref,
    psf_y_ref,
    first_ref,
    back_early_ref,
    back_late_ref,
    ahead_early_ref,
    ahead_late_ref,
    ahead_rest_ref,
    end_early_ref,
    end_late_ref,
    rows_ahead_ref,
    rows_back_ref,
    planes_ahead_ref,
    planes_back_ref,
    order_ref,
):
    groups, beside, radius, depth, rows, columns = sizes
    count = groups * beside
    taps, turned = taps_of(psf_y_ref)
    wide = columns + 2 * radius
    span = 2 * radius // len(parts)
    edges = [(0, 2 * radius), (wide - 2 * radius, 2 * radius)]
    rest_rows = ahead_rest_ref.shape[0]

    ahead = banded(taps, columns, wide, 0)
    ahead = jnp.concatenate([ordered_rows(ahead, where, order_ref, runs, count) for runs in parts], axis=0)
    first_ref[...] = as_left(ahead[: size_of(parts[0])])
    ahead_early_ref[...] = as_left(ahead[:, 2 * radius : columns])
    ahead = columns_of(ahead, edges)
    ahead_late_ref[...] = as_left(ahead[: size_of(parts[0])])
    ahead_rest_ref[...] = as_left(ahead[-rest_rows:])
    back = banded(turned, wide, wide + 2 * radius, 0)
    late = [(2 * radius - span, span), (columns + 2 * radius, span)]
    early = [(0, 2 * radius - span), (2 * radius, columns), (columns + 2 * radius + span, 2 * radius - span)]
    back_early_ref[...] = as_left(columns_of(back, [run for run in early if run[1]]))
    back_late_ref[...] = as_left(columns_of(rows_of(back, edges), late))
    back = banded(turned, columns, wide, 0)
    end_early_ref[...] = as_left(back[:, radius : radius + columns])
    edges = [(0, radius), (columns - radius, radius)]
    end_late_ref[...] = as_left(columns_of(rows_of(back, edges), [(0, radius), (columns + radius, radius)]))

    per = LANES // rows
    width = beside * rows
    taps, turned = taps_of(psf_x_ref)
    ahead = banded(turned, width, width, -radius)
    back = banded(taps, width, width, -radius)
    blocks = []
    for b in range(beside):
        for k in range(per):
            line = [jnp.zeros((rows, width), F32)] * per
            line[k] = ahead[b * rows : (b + 1) * rows]
            blocks.append(jnp.concatenate(line, axis=1))
    rows_ahead_ref[...] = as_right(jnp.concatenate(blocks, axis=0))
    for b in range(beside):
        blocks = []
        for k in range(per):
            line = [jnp.zeros((width, rows), F32)] * per
            line[k] = back[:, b * rows : (b + 1) * rows]
            blocks.append(jnp.concatenate(line, axis=1))
        slot = lax.rem(b + beside - where[2 * count + 2], beside)
        rows_back_ref[:, pl.ds(pl.multiple_of(slot * LANES, LANES), LANES)] = as_right(jnp.concatenate(blocks, axis=0))
    planes = groups * depth
    for ref, line in zip((planes_ahead_ref, planes_back_ref), taps_of(psf_z_ref)):
        ref[...] = as_left(banded(line, planes, planes, -radius))


def send_sides(where, count, value_ref, span, sibling_ref, other_ref):
    odd = where[2 * count]
    room = value_ref.shape[0] - span
    sibling_ref[...] = value_ref[pl.ds(pl.multiple_of((1 - odd) * room, 8), span), :]
    other_ref[...] = value_ref[pl.ds(pl.multiple_of(odd * room, 8), span), :]


def start_kernel(parts, radius, count, where, psf_hbm, block_hbm, *refs):
    own_ref, sibling_ref, other_ref = refs[:3]
    part_refs, (order_ref, psf_ref, block_ref, sems) = refs[3:-4], refs[-4:]
    length, columns = block_ref.shape
    pieces = sems.shape[0] - 1
    piece = length // pieces
    copies = [pltpu.make_async_copy(psf_hbm, psf_ref, sems.at[pieces])]
    for k in range(pieces):
        here = pl.ds(k * piece, piece)
        copies.append(pltpu.make_async_copy(block_hbm.at[here], block_ref.at[here], sems.at[k]))
    for copy in copies:
        copy.start()
    copies[0].wait()
    taps, _ = taps_of(psf_ref)
    matrices = [None]
    for runs in parts[1:]:
        matrix = banded(taps, columns, columns, -radius)
        matrices.append(as_left(ordered_rows(matrix, where, order_ref, runs, count)))
    for k in range(pieces):
        copies[k + 1].wait()
        for at in range(k * piece, (k + 1) * piece, LANES):
            own_ref[:, at : at + LANES] = jnp.transpose(block_ref[at : at + LANES, :])
    send_sides(where, count, own_ref, radius, sibling_ref, other_ref)
    before = 0
    for k, runs in reversed(list(enumerate(parts))):
        chunk = size_of(runs) // count
        for slot, part_ref in enumerate(part_refs):
            place = pl.multiple_of(place_of(runs, where[slot] * chunk), 8)
            part_ref[before : before + chunk, :] = own_ref[pl.ds(place, chunk), :]
        before += chunk
        if k:
            for at in range(0, length, STEP):
                here = slice(at, at + STEP)
                result = left_product(matrices[k], own_ref[:, here])
                for slot, part_ref in enumerate(part_refs):
                    part_ref[before : before + chunk, here] = result[slot * chunk : (slot + 1) * chunk]
            before += chunk


def first_y_kernel(where, matrix_ref, own_ref, other_ref, sibling_ref, *part_refs):
    columns, length = own_ref.shape
    count = len(part_refs)
    chunk = part_refs[0].shape[0]
    odd = where[2 * count] == 1, where[2 * count + 3] == 1
    for at in range(0, length, STEP):
        here = slice(at, at + STEP)
        field = assembled([[(0, columns)]], odd, [own_ref], [(other_ref, sibling_ref)], here)
        result = left_product(matrix_ref[...], field)
        for slot, part_ref in enumerate(part_refs):
            part_ref[:, here] = result[slot * chunk : (slot + 1) * chunk]


def put_parts(where, count, part_refs, own_refs):
    for k, own_ref in enumerate(own_refs):
        for slot, part_ref in enumerate(part_refs[k * count : (k + 1) * count]):
            chunk = part_ref.shape[0]
            place = pl.multiple_of(where[count + slot] * chunk, chunk)
            own_ref[pl.ds(place, chunk), :] = part_ref[...]


def sides_kernel(count, where, *refs):
    part_refs, (_, sibling_ref, other_ref) = refs[:count], refs[count:]
    span = sibling_ref.shape[0]
    chunk = part_refs[0].shape[0]
    odd = where[2 * count]
    for slot, part_ref in enumerate(part_refs):
        start = where[count + slot] * chunk
        for first, to_sibling in ((0, odd), (count * chunk - span, 1 - odd)):
            inside = (start >= first) & (start < first + span)

            def put(ref, start=start, first=first, part_ref=part_ref):
                place = jnp.clip(start - first, 0, span - chunk)
                ref[pl.ds(pl.multiple_of(place, 8), chunk), :] = part_ref[...]

            pl.when(inside & (to_sibling == 1))(functools.partial(put, sibling_ref))
            pl.when(inside & (to_sibling == 0))(functools.partial(put, other_ref))


def assembled(parts, odd, own_refs, side_refs, here):
    pieces = {}
    for runs, ref in zip(parts, own_refs):
        at = 0
        for start, size in runs:
            pieces[start] = ref[at : at + size] if isinstance(ref, jax.Array) else ref[at : at + size, here]
            at += size
    own = [pieces[start] for start in sorted(pieces)]
    low, high = [], []
    odd, alone = odd or (None, None)
    for other_ref, sibling_ref in side_refs:
        sibling, other = sibling_ref[:, here], jnp.where(alone, 0.0, other_ref[:, here])
        low.insert(0, jnp.where(odd, sibling, other))
        high.append(jnp.where(odd, other, sibling))
    return jnp.concatenate(low + own + high, axis=0)


def middle_early_kernel(parts, radius, count, where, back_ref, ahead_ref, *refs):
    kinds = len(parts)
    own_refs, refs = refs[-kinds:], refs[:-kinds]
    put_parts(where, count, refs, own_refs)
    refs = refs[kinds * count :]
    side_refs = [refs[2 * k : 2 * k + 2] for k in range(kinds - 1)]
    seen_ref, outer_ref, inner_ref, result_ref = refs[2 * kinds - 2 :]
    columns, length = seen_ref.shape
    wide = columns + 2 * radius
    edges = [(0, 2 * radius), (wide - 2 * radius, 2 * radius)]
    odd = where[2 * count] == 1, where[2 * count + 3] == 1
    for at in range(0, length, STEP):
        here = slice(at, at + STEP)
        blurred = left_product(back_ref[...], assembled(parts, odd, own_refs, side_refs, here))
        outer_ref[:, here] = rows_of(blurred, edges)
        inner = seen_ref[radius : columns - radius, here] * blurred[2 * radius : columns]
        inner_ref[:, here] = inner
        result_ref[:, here] = left_product(ahead_ref[...], inner)


def middle_late_kernel(parts, radius, count, where, back_ref, ahead_ref, *refs):
    (other_ref, sibling_ref, outer_ref, result_ref), refs = refs[:4], refs[4:]
    seen_ref, seen_other_ref, seen_sibling_ref, estimate_ref, *part_refs = refs
    columns, length = seen_ref.shape
    wide = columns + 2 * radius
    edges = [(0, 2 * radius), (wide - 2 * radius, 2 * radius)]
    odd = where[2 * count] == 1, where[2 * count + 3] == 1
    rows = size_of(parts[0])
    for at in range(0, length, STEP):
        here = slice(at, at + STEP)
        sides = assembled([], odd, [], [(other_ref, sibling_ref)], here)
        seen = assembled([[(0, columns)]], odd, [seen_ref], [(seen_other_ref, seen_sibling_ref)], here)
        outer = rows_of(seen, edges) * (outer_ref[:, here] + left_product(back_ref[...], sides))
        estimate_ref[:, here] = outer
        result = result_ref[:rows, here] + left_product(ahead_ref[...], outer)
        place = 0
        for part_ref in part_refs:
            chunk = part_ref.shape[0]
            part_ref[:, here] = result[place : place + chunk]
            place += chunk


def middle_rest_kernel(parts, radius, where, ahead_ref, outer_ref, inner_ref, result_ref, _, estimate_ref, *part_refs):
    length = outer_ref.shape[1]
    rows = size_of(parts[0])
    for at in range(0, length, STEP):
        here = slice(at, at + STEP)
        outer = outer_ref[:, here]
        estimate_ref[:, here] = jnp.concatenate(
            [outer[radius : 2 * radius], inner_ref[:, here], outer[2 * radius : 3 * radius]], axis=0
        )
        if part_refs:
            result = result_ref[rows:, here] + left_product(ahead_ref[...], outer)
        place = 0
        for part_ref in part_refs:
            chunk = part_ref.shape[0]
            part_ref[:, here] = result[place : place + chunk]
            place += chunk


def last_early_kernel(parts, radius, count, where, back_ref, estimate_ref, *refs):
    outer_ref, inner_ref, *own_refs = refs[len(parts) * count :]
    put_parts(where, count, refs, own_refs)
    columns, length = estimate_ref.shape
    edges = [(0, radius), (columns - radius, radius)]
    for at in range(0, length, STEP):
        here = slice(at, at + STEP)
        blurred = left_product(back_ref[...], assembled(parts, None, own_refs, [], here))
        outer_ref[:, here] = rows_of(blurred, edges)
        inner_ref[:, here] = estimate_ref[radius : columns - radius, here] * blurred[radius : columns - radius]


def last_late_kernel(
    radius, count, where, back_ref, other_ref, sibling_ref, outer_ref, inner_ref, estimate_ref, out_hbm, out_ref, sems
):
    columns, length = estimate_ref.shape
    odd = where[2 * count] == 1, where[2 * count + 3] == 1
    edges = [(0, radius), (columns - radius, radius)]
    pieces = sems.shape[0]
    piece = length // pieces
    copies = []
    for at in range(0, length, STEP):
        here = slice(at, at + STEP)
        sides = assembled([], odd, [], [(other_ref, sibling_ref)], here)
        outer = rows_of(estimate_ref[:, here], edges) * (outer_ref[:, here] + left_product(back_ref[...], sides))
        estimate = jnp.concatenate([outer[:radius], inner_ref[:, here], outer[radius:]], axis=0)
        for tile in range(0, STEP, LANES):
            out_ref[at + tile : at + tile + LANES, :] = jnp.transpose(estimate[:, tile : tile + LANES])
            if (at + tile + LANES) % piece == 0:
                k = (at + tile) // piece
                lines = pl.ds(k * piece, piece)
                copies.append(pltpu.make_async_copy(out_ref.at[lines], out_hbm.at[lines], sems.at[k]))
                copies[-1].start()
    for copy in copies:
        copy.wait()


def put_lines(ref, lines, value):
    for tile in range(ref.shape[0]):
        ref[tile, lines, :] = value[:, tile * LANES : (tile + 1) * LANES]


def get_lines(ref, lines):
    return jnp.concatenate([ref[tile, lines, :] for tile in range(ref.shape[0])], axis=1)


def fill(sizes, where, part_refs, first, chunk, held_ref):
    groups, beside = sizes[:2]
    count = groups * beside
    tiles = part_refs[0].shape[1] // LANES
    for (dz, dx), part_ref in zip(offsets_of(groups, beside), part_refs):
        source_z = lax.rem(where[2 * count + 1] + groups - dz, groups)
        source_x = lax.rem(where[2 * count + 2] + beside - dx, beside)
        for t in range(tiles):
            place = pl.multiple_of((source_z * tiles + t) * chunk, chunk)
            held_ref[source_x, pl.ds(place, chunk), :] = part_ref[first : first + chunk, t * LANES : (t + 1) * LANES]


def planes_kernel(
    sizes, first, seen_first, where, rows_ahead_ref, rows_back_ref, planes_ahead_ref, planes_back_ref, *refs
):
    groups, beside, _, _, rows, _ = sizes
    count = groups * beside
    part_refs, refs = refs[:count], refs[count:]
    begins = seen_first is not None
    if begins:
        seen_refs, refs = refs[:count], refs[count:]
        out_refs, (seen_ref, held_ref, field_ref, other_ref) = refs[:count], refs[count:]
    else:
        seen_ref, out_refs, (held_ref, field_ref, other_ref) = refs[0], refs[1 : count + 1], refs[count + 1 :]
    chunk, length = out_refs[0].shape
    tiles = length // LANES
    per = LANES // rows
    width = beside * rows
    planes = groups * tiles * per
    if begins:
        fill(sizes, where, seen_refs, seen_first, chunk, held_ref)
        for at in range(groups * tiles):
            for k in range(per):
                lines = slice(at * chunk, (at + 1) * chunk)
                pieces = [held_ref[b, lines, k * rows : (k + 1) * rows] for b in range(beside)]
                place = (at * per + k) * chunk
                put_lines(seen_ref, slice(place, place + chunk), jnp.concatenate(pieces, axis=1))
    fill(sizes, where, part_refs, first, chunk, held_ref)

    group = min(tiles, max(1, 4 * LANES // chunk))
    for at in range(0, groups * tiles, group):
        here = slice(at * chunk, (at + group) * chunk)
        left = jnp.concatenate([held_ref[b, here, :] for b in range(beside)], axis=1)
        result = right_product(left, rows_ahead_ref[...])
        for g in range(group):
            for k in range(per):
                place = ((at + g) * per + k) * chunk
                part = result[g * chunk : (g + 1) * chunk, k * width : (k + 1) * width]
                put_lines(field_ref, slice(place, place + chunk), part)

    for y in range(0, chunk, 2):
        lines = [pl.ds(y + k, planes, stride=chunk) for k in range(2)]
        value = jnp.concatenate([get_lines(field_ref, line) for line in lines], axis=1)
        seen = jnp.concatenate([get_lines(seen_ref, line) for line in lines], axis=1)
        value = left_product(planes_back_ref[...], seen / left_product(planes_ahead_ref[...], value))
        for k, line in enumerate(lines):
            put_lines(other_ref, line, value[:, k * width : (k + 1) * width])

    offsets = offsets_of(groups, beside)
    for dz in range(groups):
        target_z = lax.rem(where[2 * count + 1] + dz, groups)
        for at in range(0, tiles, group):
            pieces = []
            for g in range(group):
                line = []
                for k in range(per):
                    place = pl.multiple_of(((target_z * tiles + at + g) * per + k) * chunk, chunk)
                    line.append(get_lines(other_ref, pl.ds(place, chunk)))
                pieces.append(jnp.concatenate(line, axis=1))
            left = jnp.concatenate(pieces, axis=0)
            result = right_product(left, rows_back_ref[...])
            for dx in range(beside):
                for g in range(group):
                    out_refs[offsets.index((dz, dx))][:, (at + g) * LANES : (at + g + 1) * LANES] = result[
                        g * chunk : (g + 1) * chunk, dx * LANES : (dx + 1) * LANES
                    ]


def per_device(observed, psf_z, psf_x, psf_y):
    groups, beside, along = (lax.axis_size(axis) for axis in ("gz", "bx", "by"))
    count = groups * beside
    planes, rows, columns = observed.shape
    length = planes * rows
    radius = psf_z.shape[0] // 2
    sizes = (groups, beside, radius, planes, rows, columns)
    width = beside * rows
    parts = parts_of(columns, radius, count)
    chunks = [size_of(runs) // count for runs in parts]

    offsets = offsets_of(groups, beside)

    def exchanged(values):
        result = [values[0]]
        for (dz, dx), value in list(zip(offsets, values))[1:]:
            pairs = [
                (z * beside + x, ((z + dz) % groups) * beside + (x + dx) % beside)
                for z in range(groups)
                for x in range(beside)
            ]
            result.append(lax.ppermute(value, ("gz", "bx"), pairs))
        return result

    def from_sides(sibling, other, paced=False):
        result = []
        for value, first in ((other, 1), (sibling, 0)):
            pairs = []
            for place in range(count):
                line = [place * along + i for i in range(along)]
                pairs += [(line[i], line[i + 1]) for i in range(first, along - 1, 2)]
                if paced and first and place + beside < count and place // beside % 2 == 0:
                    ends = [0] + [along - 1] * (along % 2 == 0)
                    pairs += [(line[i], line[i] + beside * along) for i in ends]
            result.append(lax.ppermute(value, ("gz", "bx", "by"), pairs + [(j, i) for i, j in pairs]))
        return result

    line = (1, psf_z.shape[0])
    psf_z, psf_x, psf_y = psf_z.reshape(line), psf_x.reshape(line), psf_y.reshape(line)
    order = pltpu.VMEM((2, columns, columns + 2 * radius), F32)
    block = sum(chunks)
    pieces = 4
    seen, sibling, other, *parcels = call(
        1.3,
        functools.partial(start_kernel, parts, radius, count),
        [shaped(columns, length), shaped(radius, length), shaped(radius, length)]
        + [shaped(block + sum(chunks[1:]), length)] * count,
        [HBM, HBM],
        [order, pltpu.VMEM(line, F32), pltpu.VMEM((length, columns), F32), pltpu.SemaphoreType.DMA((pieces + 1,))],
    )(stays(psf_y), stays(observed.reshape(length, columns)))
    seen_sides = from_sides(sibling, other)
    parcels = exchanged(parcels)

    def left(rows, width):
        return jax.ShapeDtypeStruct((rows, 3 * width), BF16)

    def right(rows, width):
        return jax.ShapeDtypeStruct((3 * rows, width), BF16)

    span = 2 * radius // len(parts)
    across = LANES // rows * width
    first, back_early, back_late, ahead_early, ahead_late, ahead_rest, end_early, end_late, *weights = call(
        0.8,
        functools.partial(weights_kernel, sizes, parts),
        [
            left(size_of(parts[0]), columns + 2 * radius),
            left(columns + 2 * radius, columns + 4 * radius - 2 * span),
            left(4 * radius, 2 * span),
            left(columns, columns - 2 * radius),
            left(size_of(parts[0]), 4 * radius),
            left(size_of(parts[-1]), 4 * radius),
            left(columns, columns),
            left(2 * radius, 2 * radius),
            right(beside * LANES, across),
            right(across, beside * LANES),
            left(groups * planes, groups * planes),
            left(groups * planes, groups * planes),
        ],
        [VMEM] * 3,
        [order],
    )(psf_z, psf_x, psf_y)
    outer = exchanged(
        call(
            0.8,
            first_y_kernel,
            [shaped(chunks[0], length)] * count,
            [VMEM] * 4,
        )(first, seen, *seen_sides)
    )

    def through_planes(values, first, chunk, seen_values, seen_first=None):
        lines = groups * planes * chunk
        across = (width // LANES, lines + chunk, LANES)
        begins = seen_first is not None
        result = call(
            50,
            functools.partial(planes_kernel, sizes, first, seen_first),
            [shaped(chunk, length)] * count + [shaped(*across)] * begins,
            [VMEM] * (4 + len(values) + len(seen_values)),
            [
                pltpu.VMEM((beside, groups * (length // LANES) * chunk, LANES), F32),
                pltpu.VMEM(across, F32),
                pltpu.VMEM(across, F32),
            ],
        )(*weights, *values, *seen_values)
        return result[:count], result[count:] if begins else seen_values

    def sides_of(cost, values, span, after, paced=False):
        sides = call(
            cost,
            functools.partial(sides_kernel, count),
            [shaped(span, length)] * 2,
            [VMEM] * (count + 1),
        )(*values, after)
        return from_sides(*sides, paced)

    fields, across, sides = ([None] * len(parts) for _ in range(3))
    before = 0
    for k in reversed(range(len(parts))):
        values, first = (parcels, before + chunks[k]) if k else (outer, 0)
        fields[k], across[k] = through_planes(values, first, chunks[k], parcels, before)
        fields[k] = exchanged(fields[k])
        before += chunks[k] * (2 if k else 1)
    for k in reversed(range(len(parts))):
        sides[k] = sides_of(50, fields[k], span, fields[0][0], k == 0)
    partial = [shaped(4 * radius, length), shaped(columns - 2 * radius, length), shaped(columns, length)]
    partial = call(
        2.2,
        functools.partial(middle_early_kernel, parts, radius, count),
        partial,
        [VMEM] * (1 + (count + 2) * len(parts)),
        [pltpu.VMEM((size_of(runs), length), F32) for runs in parts],
    )(back_early, ahead_early, *flat(fields), *flat(sides[1:]), seen)
    estimate, *values = call(
        0.8,
        functools.partial(middle_late_kernel, parts, radius, count),
        [shaped(4 * radius, length)] + [shaped(chunks[0], length)] * count,
        [VMEM] * 9,
    )(back_late, ahead_late, *sides[0], partial[0], partial[2], seen, *seen_sides)
    fields[0] = exchanged(values)
    estimate, *values = call(
        50,
        functools.partial(middle_rest_kernel, parts, radius),
        [shaped(columns, length)] + [shaped(chunk, length) for chunk in chunks[1:] for _ in range(count)],
        [VMEM] * 5,
    )(ahead_rest, estimate, *partial[1:], fields[0][0])
    if len(parts) > 1:
        fields[1] = exchanged(values)
    for k in range(len(parts)):
        values, _ = through_planes(fields[k], 0, chunks[k], across[k])
        fields[k] = exchanged(values)
    sides = sides_of(0.6, fields[0], radius, fields[-1][0])
    partial = call(
        50,
        functools.partial(last_early_kernel, parts, radius, count),
        [shaped(2 * radius, length), shaped(columns - 2 * radius, length)],
        [VMEM] * (2 + count * len(parts)),
        [pltpu.VMEM((size_of(runs), length), F32) for runs in parts],
    )(end_early, estimate, *flat(fields))
    out = call(
        1.5,
        functools.partial(last_late_kernel, radius, count),
        shaped(length, columns),
        [VMEM] * 6,
        [pltpu.VMEM((length, columns), F32), pltpu.SemaphoreType.DMA((pieces,))],
        HBM,
    )(end_late, *sides, *partial, estimate)
    return out.reshape(planes, rows, columns)


def solution(mesh):
    placed = (P("gz", "bx", "by"), P(), P(), P())
    return jax.shard_map(
        per_device, mesh=mesh, in_specs=placed, out_specs=P("gz", "bx", "by"), check_vma=False
    )
```

```python
import functools
import jax
import jax.numpy as jnp
from jax import lax
from jax.experimental import pallas as pl
from jax.experimental.pallas import tpu as pltpu
from jax.sharding import PartitionSpec as P

LANES = 128
RATE = 1150 * 1000 * 1000
STEP = 4 * LANES
F32 = jnp.float32
BF16 = jnp.bfloat16
VMEM = pl.BlockSpec(memory_space=pltpu.VMEM)
HBM = pl.BlockSpec(memory_space=pltpu.HBM)


def shaped(*shape):
    return jax.ShapeDtypeStruct(shape, F32)


def stays(value):
    return pltpu.with_memory_space_constraint(value, pltpu.HBM)


def call(cost, kernel, outs, specs, scratch=(), place=VMEM):
    return pl.pallas_call(
        lambda *refs: kernel(place_of_device(), *refs),
        out_shape=outs,
        in_specs=specs,
        out_specs=jax.tree.map(lambda _: place, outs),
        scratch_shapes=list(scratch),
        compiler_params=pltpu.CompilerParams(vmem_limit_bytes=16 * 1024 * 1024),
        cost_estimate=pl.CostEstimate(flops=int(cost * RATE), bytes_accessed=0, transcendentals=0),
    )


def parts_of(columns, radius, count):
    outer = [(0, radius), (columns - radius, radius)]
    inner = [(radius, columns - 2 * radius)]
    fits = columns >= 3 * radius and count % 2 == 0
    for runs in (outer, inner):
        fits = fits and sum(size for _, size in runs) % (8 * count) == 0
    return [outer, inner] if fits else [[(0, columns)]]


def flat(lists):
    return [value for values in lists for value in values]


def size_of(runs):
    return sum(size for _, size in runs)


def rows_of(value, runs):
    return jnp.concatenate([value[start : start + size] for start, size in runs], axis=0)


def place_of(runs, offset):
    place, before = runs[0][0] + offset, 0
    for (start, size), (after, _) in zip(runs, runs[1:]):
        before += size
        place = jnp.where(offset >= before, after - before + offset, place)
    return place


def offsets_of(groups, beside):
    offsets = [(dz, dx) for dz in range(groups) for dx in range(beside)]
    return offsets[:1] + sorted(offsets[1:], key=lambda offset: offset.count(0))


def place_of_device():
    groups, beside = lax.axis_size("gz"), lax.axis_size("bx")
    me_z, me_x = lax.axis_index("gz"), lax.axis_index("bx")
    offsets = offsets_of(groups, beside)
    ahead = [lax.rem(me_z + dz, groups) * beside + lax.rem(me_x + dx, beside) for dz, dx in offsets]
    behind = [
        lax.rem(me_z + groups - dz, groups) * beside + lax.rem(me_x + beside - dx, beside) for dz, dx in offsets
    ]
    me_y, odd = lax.axis_index("by"), lax.rem(lax.axis_index("by"), 2)
    other = me_y + 2 * odd - 1
    alone = jnp.where((other < 0) | (other >= lax.axis_size("by")), 1, 0)
    return ahead + behind + [odd, me_z, me_x, alone]


def split(value):
    high = value.astype(BF16)
    return high, (value - high.astype(F32)).astype(BF16)


def dot(left, right):
    return lax.dot_general(left, right, (((1,), (0,)), ((), ())), preferred_element_type=F32)


def banded(taps, rows, width, start):
    room = (width + 2 * LANES - 1) // LANES * LANES
    base = jnp.concatenate([taps, jnp.zeros((1, room - LANES), F32)], axis=1)
    base = jnp.broadcast_to(base, (rows, room))
    return pltpu.roll(base, start % room, 1, stride=1, stride_axis=0)[:, :width]


def as_left(matrix):
    high, low = split(matrix)
    return jnp.concatenate([high, high, low], axis=1)


def left_product(matrix, value):
    high, low = split(value)
    return dot(matrix, jnp.concatenate([high, low, high], axis=0))


def as_right(matrix):
    high, low = split(matrix)
    return jnp.concatenate([high, high, low], axis=0)


def right_product(value, matrix):
    high, low = split(value)
    return dot(jnp.concatenate([high, low, high], axis=1), matrix)


def ordered_rows(matrix, where, order_ref, runs, count):
    size = size_of(runs)
    chunk = size // count
    width = matrix.shape[1]
    order_ref[0, :size, :width] = rows_of(matrix, runs)
    for slot in range(count):
        place = pl.multiple_of(where[slot] * chunk, chunk)
        order_ref[1, slot * chunk : (slot + 1) * chunk, :width] = order_ref[0, pl.ds(place, chunk), :width]
    return order_ref[1, :size, :width]


def columns_of(matrix, runs):
    return jnp.concatenate([matrix[:, start : start + size] for start, size in runs], axis=1)


def taps_of(psf_ref):
    count = psf_ref.shape[1]
    row = lax.broadcasted_iota(jnp.int32, (LANES, LANES), 0)
    lane = lax.broadcasted_iota(jnp.int32, (LANES, LANES), 1)
    taps = psf_ref[...] / jnp.sum(psf_ref[...], axis=1, keepdims=True)
    taps = jnp.concatenate([taps, jnp.zeros((1, LANES - count), F32)], axis=1)
    column = jnp.transpose(jnp.broadcast_to(taps, (LANES, LANES)))
    return taps, jnp.sum(jnp.where(row + lane == count - 1, column, 0.0), axis=0, keepdims=True)


def weights_kernel(
    sizes,
    parts,
    where,
    psf_z_ref,
    psf_x_ref,
    psf_y_ref,
    first_ref,
    back_early_ref,
    back_late_ref,
    ahead_early_ref,
    ahead_late_ref,
    ahead_rest_ref,
    end_early_ref,
    end_late_ref,
    rows_ahead_ref,
    rows_back_ref,
    planes_ahead_ref,
    planes_back_ref,
    order_ref,
):
    groups, beside, radius, depth, rows, columns = sizes
    count = groups * beside
    taps, turned = taps_of(psf_y_ref)
    wide = columns + 2 * radius
    span = 2 * radius // len(parts)
    edges = [(0, 2 * radius), (wide - 2 * radius, 2 * radius)]
    rest_rows = ahead_rest_ref.shape[0]

    ahead = banded(taps, columns, wide, 0)
    ahead = jnp.concatenate([ordered_rows(ahead, where, order_ref, runs, count) for runs in parts], axis=0)
    first_ref[...] = as_left(ahead[: size_of(parts[0])])
    ahead_early_ref[...] = as_left(ahead[:, 2 * radius : columns])
    ahead = columns_of(ahead, edges)
    ahead_late_ref[...] = as_left(ahead[: size_of(parts[0])])
    ahead_rest_ref[...] = as_left(ahead[-rest_rows:])
    back = banded(turned, wide, wide + 2 * radius, 0)
    late = [(2 * radius - span, span), (columns + 2 * radius, span)]
    early = [(0, 2 * radius - span), (2 * radius, columns), (columns + 2 * radius + span, 2 * radius - span)]
    back_early_ref[...] = as_left(columns_of(back, [run for run in early if run[1]]))
    back_late_ref[...] = as_left(columns_of(rows_of(back, edges), late))
    back = banded(turned, columns, wide, 0)
    end_early_ref[...] = as_left(back[:, radius : radius + columns])
    edges = [(0, radius), (columns - radius, radius)]
    end_late_ref[...] = as_left(columns_of(rows_of(back, edges), [(0, radius), (columns + radius, radius)]))

    per = LANES // rows
    width = beside * rows
    taps, turned = taps_of(psf_x_ref)
    ahead = banded(turned, width, width, -radius)
    back = banded(taps, width, width, -radius)
    blocks = []
    for b in range(beside):
        for k in range(per):
            line = [jnp.zeros((rows, width), F32)] * per
            line[k] = ahead[b * rows : (b + 1) * rows]
            blocks.append(jnp.concatenate(line, axis=1))
    rows_ahead_ref[...] = as_right(jnp.concatenate(blocks, axis=0))
    for b in range(beside):
        blocks = []
        for k in range(per):
            line = [jnp.zeros((width, rows), F32)] * per
            line[k] = back[:, b * rows : (b + 1) * rows]
            blocks.append(jnp.concatenate(line, axis=1))
        slot = lax.rem(b + beside - where[2 * count + 2], beside)
        rows_back_ref[:, pl.ds(pl.multiple_of(slot * LANES, LANES), LANES)] = as_right(jnp.concatenate(blocks, axis=0))
    planes = groups * depth
    for ref, line in zip((planes_ahead_ref, planes_back_ref), taps_of(psf_z_ref)):
        ref[...] = as_left(banded(line, planes, planes, -radius))


def send_sides(where, count, value_ref, span, sibling_ref, other_ref):
    odd = where[2 * count]
    room = value_ref.shape[0] - span
    sibling_ref[...] = value_ref[pl.ds(pl.multiple_of((1 - odd) * room, 8), span), :]
    other_ref[...] = value_ref[pl.ds(pl.multiple_of(odd * room, 8), span), :]


def start_kernel(parts, radius, count, where, psf_hbm, block_hbm, *refs):
    own_ref, sibling_ref, other_ref = refs[:3]
    part_refs, (order_ref, psf_ref, block_ref, sems) = refs[3:-4], refs[-4:]
    length, columns = block_ref.shape
    pieces = sems.shape[0] - 1
    piece = length // pieces
    copies = [pltpu.make_async_copy(psf_hbm, psf_ref, sems.at[pieces])]
    for k in range(pieces):
        here = pl.ds(k * piece, piece)
        copies.append(pltpu.make_async_copy(block_hbm.at[here], block_ref.at[here], sems.at[k]))
    for copy in copies:
        copy.start()
    copies[0].wait()
    taps, _ = taps_of(psf_ref)
    matrices = [None]
    for runs in parts[1:]:
        matrix = banded(taps, columns, columns, -radius)
        matrices.append(as_left(ordered_rows(matrix, where, order_ref, runs, count)))
    for k in range(pieces):
        copies[k + 1].wait()
        for at in range(k * piece, (k + 1) * piece, LANES):
            own_ref[:, at : at + LANES] = jnp.transpose(block_ref[at : at + LANES, :])
    send_sides(where, count, own_ref, radius, sibling_ref, other_ref)
    before = 0
    for k, runs in reversed(list(enumerate(parts))):
        chunk = size_of(runs) // count
        for slot, part_ref in enumerate(part_refs):
            place = pl.multiple_of(place_of(runs, where[slot] * chunk), 8)
            part_ref[before : before + chunk, :] = own_ref[pl.ds(place, chunk), :]
        before += chunk
        if k:
            for at in range(0, length, STEP):
                here = slice(at, at + STEP)
                result = left_product(matrices[k], own_ref[:, here])
                for slot, part_ref in enumerate(part_refs):
                    part_ref[before : before + chunk, here] = result[slot * chunk : (slot + 1) * chunk]
            before += chunk


def first_y_kernel(where, matrix_ref, own_ref, other_ref, sibling_ref, *part_refs):
    columns, length = own_ref.shape
    count = len(part_refs)
    chunk = part_refs[0].shape[0]
    odd = where[2 * count] == 1, where[2 * count + 3] == 1
    for at in range(0, length, STEP):
        here = slice(at, at + STEP)
        field = assembled([[(0, columns)]], odd, [own_ref], [(other_ref, sibling_ref)], here)
        result = left_product(matrix_ref[...], field)
        for slot, part_ref in enumerate(part_refs):
            part_ref[:, here] = result[slot * chunk : (slot + 1) * chunk]


def put_parts(where, count, part_refs, own_refs):
    for k, own_ref in enumerate(own_refs):
        for slot, part_ref in enumerate(part_refs[k * count : (k + 1) * count]):
            chunk = part_ref.shape[0]
            place = pl.multiple_of(where[count + slot] * chunk, chunk)
            own_ref[pl.ds(place, chunk), :] = part_ref[...]


def sides_kernel(count, where, *refs):
    part_refs, (_, sibling_ref, other_ref) = refs[:count], refs[count:]
    span = sibling_ref.shape[0]
    chunk = part_refs[0].shape[0]
    odd = where[2 * count]
    for slot, part_ref in enumerate(part_refs):
        start = where[count + slot] * chunk
        for first, to_sibling in ((0, odd), (count * chunk - span, 1 - odd)):
            inside = (start >= first) & (start < first + span)

            def put(ref, start=start, first=first, part_ref=part_ref):
                place = jnp.clip(start - first, 0, span - chunk)
                ref[pl.ds(pl.multiple_of(place, 8), chunk), :] = part_ref[...]

            pl.when(inside & (to_sibling == 1))(functools.partial(put, sibling_ref))
            pl.when(inside & (to_sibling == 0))(functools.partial(put, other_ref))


def assembled(parts, odd, own_refs, side_refs, here):
    pieces = {}
    for runs, ref in zip(parts, own_refs):
        at = 0
        for start, size in runs:
            pieces[start] = ref[at : at + size] if isinstance(ref, jax.Array) else ref[at : at + size, here]
            at += size
    own = [pieces[start] for start in sorted(pieces)]
    low, high = [], []
    odd, alone = odd or (None, None)
    for other_ref, sibling_ref in side_refs:
        sibling, other = sibling_ref[:, here], jnp.where(alone, 0.0, other_ref[:, here])
        low.insert(0, jnp.where(odd, sibling, other))
        high.append(jnp.where(odd, other, sibling))
    return jnp.concatenate(low + own + high, axis=0)


def middle_early_kernel(parts, radius, count, where, back_ref, ahead_ref, *refs):
    kinds = len(parts)
    own_refs, refs = refs[-kinds:], refs[:-kinds]
    put_parts(where, count, refs, own_refs)
    refs = refs[kinds * count :]
    side_refs = [refs[2 * k : 2 * k + 2] for k in range(kinds - 1)]
    seen_ref, outer_ref, inner_ref, result_ref = refs[2 * kinds - 2 :]
    columns, length = seen_ref.shape
    wide = columns + 2 * radius
    edges = [(0, 2 * radius), (wide - 2 * radius, 2 * radius)]
    odd = where[2 * count] == 1, where[2 * count + 3] == 1
    for at in range(0, length, STEP):
        here = slice(at, at + STEP)
        blurred = left_product(back_ref[...], assembled(parts, odd, own_refs, side_refs, here))
        outer_ref[:, here] = rows_of(blurred, edges)
        inner = seen_ref[radius : columns - radius, here] * blurred[2 * radius : columns]
        inner_ref[:, here] = inner
        result_ref[:, here] = left_product(ahead_ref[...], inner)


def middle_late_kernel(parts, radius, count, where, back_ref, ahead_ref, *refs):
    (other_ref, sibling_ref, outer_ref, result_ref), refs = refs[:4], refs[4:]
    seen_ref, seen_other_ref, seen_sibling_ref, estimate_ref, *part_refs = refs
    columns, length = seen_ref.shape
    wide = columns + 2 * radius
    edges = [(0, 2 * radius), (wide - 2 * radius, 2 * radius)]
    odd = where[2 * count] == 1, where[2 * count + 3] == 1
    rows = size_of(parts[0])
    for at in range(0, length, STEP):
        here = slice(at, at + STEP)
        sides = assembled([], odd, [], [(other_ref, sibling_ref)], here)
        seen = assembled([[(0, columns)]], odd, [seen_ref], [(seen_other_ref, seen_sibling_ref)], here)
        outer = rows_of(seen, edges) * (outer_ref[:, here] + left_product(back_ref[...], sides))
        estimate_ref[:, here] = outer
        result = result_ref[:rows, here] + left_product(ahead_ref[...], outer)
        place = 0
        for part_ref in part_refs:
            chunk = part_ref.shape[0]
            part_ref[:, here] = result[place : place + chunk]
            place += chunk


def middle_rest_kernel(parts, radius, where, ahead_ref, outer_ref, inner_ref, result_ref, _, estimate_ref, *part_refs):
    length = outer_ref.shape[1]
    rows = size_of(parts[0])
    for at in range(0, length, STEP):
        here = slice(at, at + STEP)
        outer = outer_ref[:, here]
        estimate_ref[:, here] = jnp.concatenate(
            [outer[radius : 2 * radius], inner_ref[:, here], outer[2 * radius : 3 * radius]], axis=0
        )
        if part_refs:
            result = result_ref[rows:, here] + left_product(ahead_ref[...], outer)
        place = 0
        for part_ref in part_refs:
            chunk = part_ref.shape[0]
            part_ref[:, here] = result[place : place + chunk]
            place += chunk


def last_early_kernel(parts, radius, count, where, back_ref, estimate_ref, *refs):
    outer_ref, inner_ref, *own_refs = refs[len(parts) * count :]
    put_parts(where, count, refs, own_refs)
    columns, length = estimate_ref.shape
    edges = [(0, radius), (columns - radius, radius)]
    for at in range(0, length, STEP):
        here = slice(at, at + STEP)
        blurred = left_product(back_ref[...], assembled(parts, None, own_refs, [], here))
        outer_ref[:, here] = rows_of(blurred, edges)
        inner_ref[:, here] = estimate_ref[radius : columns - radius, here] * blurred[radius : columns - radius]


def last_late_kernel(
    radius, count, where, back_ref, other_ref, sibling_ref, outer_ref, inner_ref, estimate_ref, out_hbm, out_ref, sems
):
    columns, length = estimate_ref.shape
    odd = where[2 * count] == 1, where[2 * count + 3] == 1
    edges = [(0, radius), (columns - radius, radius)]
    pieces = sems.shape[0]
    piece = length // pieces
    copies = []
    for at in range(0, length, STEP // 2):
        here = slice(at, at + STEP // 2)
        sides = assembled([], odd, [], [(other_ref, sibling_ref)], here)
        outer = rows_of(estimate_ref[:, here], edges) * (outer_ref[:, here] + left_product(back_ref[...], sides))
        estimate = jnp.concatenate([outer[:radius], inner_ref[:, here], outer[radius:]], axis=0)
        for tile in range(0, STEP // 2, LANES):
            out_ref[at + tile : at + tile + LANES, :] = jnp.transpose(estimate[:, tile : tile + LANES])
            if (at + tile + LANES) % piece == 0:
                k = (at + tile) // piece
                lines = pl.ds(k * piece, piece)
                copies.append(pltpu.make_async_copy(out_ref.at[lines], out_hbm.at[lines], sems.at[k]))
                copies[-1].start()
    for copy in copies:
        copy.wait()


def put_lines(ref, lines, value):
    for tile in range(ref.shape[0]):
        ref[tile, lines, :] = value[:, tile * LANES : (tile + 1) * LANES]


def get_lines(ref, lines):
    return jnp.concatenate([ref[tile, lines, :] for tile in range(ref.shape[0])], axis=1)


def fill(sizes, where, part_refs, first, chunk, held_ref):
    groups, beside = sizes[:2]
    count = groups * beside
    tiles = part_refs[0].shape[1] // LANES
    for (dz, dx), part_ref in zip(offsets_of(groups, beside), part_refs):
        source_z = lax.rem(where[2 * count + 1] + groups - dz, groups)
        source_x = lax.rem(where[2 * count + 2] + beside - dx, beside)
        for t in range(tiles):
            place = pl.multiple_of((source_z * tiles + t) * chunk, chunk)
            held_ref[source_x, pl.ds(place, chunk), :] = part_ref[first : first + chunk, t * LANES : (t + 1) * LANES]


def planes_kernel(
    sizes, first, seen_first, where, rows_ahead_ref, rows_back_ref, planes_ahead_ref, planes_back_ref, *refs
):
    groups, beside, _, _, rows, _ = sizes
    count = groups * beside
    part_refs, refs = refs[:count], refs[count:]
    begins = seen_first is not None
    if begins:
        seen_refs, refs = refs[:count], refs[count:]
        out_refs, (seen_ref, held_ref, field_ref, other_ref) = refs[:count], refs[count:]
    else:
        seen_ref, out_refs, (held_ref, field_ref, other_ref) = refs[0], refs[1 : count + 1], refs[count + 1 :]
    chunk, length = out_refs[0].shape
    tiles = length // LANES
    per = LANES // rows
    width = beside * rows
    planes = groups * tiles * per
    if begins:
        fill(sizes, where, seen_refs, seen_first, chunk, held_ref)
        for at in range(groups * tiles):
            for k in range(per):
                lines = slice(at * chunk, (at + 1) * chunk)
                pieces = [held_ref[b, lines, k * rows : (k + 1) * rows] for b in range(beside)]
                place = (at * per + k) * chunk
                put_lines(seen_ref, slice(place, place + chunk), jnp.concatenate(pieces, axis=1))
    fill(sizes, where, part_refs, first, chunk, held_ref)

    group = min(tiles, max(1, 4 * LANES // chunk))
    for at in range(0, groups * tiles, group):
        here = slice(at * chunk, (at + group) * chunk)
        left = jnp.concatenate([held_ref[b, here, :] for b in range(beside)], axis=1)
        result = right_product(left, rows_ahead_ref[...])
        for g in range(group):
            for k in range(per):
                place = ((at + g) * per + k) * chunk
                part = result[g * chunk : (g + 1) * chunk, k * width : (k + 1) * width]
                put_lines(field_ref, slice(place, place + chunk), part)

    for y in range(0, chunk, 2):
        lines = [pl.ds(y + k, planes, stride=chunk) for k in range(2)]
        value = jnp.concatenate([get_lines(field_ref, line) for line in lines], axis=1)
        seen = jnp.concatenate([get_lines(seen_ref, line) for line in lines], axis=1)
        value = left_product(planes_back_ref[...], seen / left_product(planes_ahead_ref[...], value))
        for k, line in enumerate(lines):
            put_lines(other_ref, line, value[:, k * width : (k + 1) * width])

    offsets = offsets_of(groups, beside)
    for dz in range(groups):
        target_z = lax.rem(where[2 * count + 1] + dz, groups)
        for at in range(0, tiles, group):
            pieces = []
            for g in range(group):
                line = []
                for k in range(per):
                    place = pl.multiple_of(((target_z * tiles + at + g) * per + k) * chunk, chunk)
                    line.append(get_lines(other_ref, pl.ds(place, chunk)))
                pieces.append(jnp.concatenate(line, axis=1))
            left = jnp.concatenate(pieces, axis=0)
            result = right_product(left, rows_back_ref[...])
            for dx in range(beside):
                for g in range(group):
                    out_refs[offsets.index((dz, dx))][:, (at + g) * LANES : (at + g + 1) * LANES] = result[
                        g * chunk : (g + 1) * chunk, dx * LANES : (dx + 1) * LANES
                    ]


def per_device(observed, psf_z, psf_x, psf_y):
    groups, beside, along = (lax.axis_size(axis) for axis in ("gz", "bx", "by"))
    count = groups * beside
    planes, rows, columns = observed.shape
    length = planes * rows
    radius = psf_z.shape[0] // 2
    sizes = (groups, beside, radius, planes, rows, columns)
    width = beside * rows
    parts = parts_of(columns, radius, count)
    chunks = [size_of(runs) // count for runs in parts]

    offsets = offsets_of(groups, beside)

    def exchanged(values):
        result = [values[0]]
        for (dz, dx), value in list(zip(offsets, values))[1:]:
            pairs = [
                (z * beside + x, ((z + dz) % groups) * beside + (x + dx) % beside)
                for z in range(groups)
                for x in range(beside)
            ]
            result.append(lax.ppermute(value, ("gz", "bx"), pairs))
        return result

    def from_sides(sibling, other, paced=False):
        result = []
        for value, first in ((other, 1), (sibling, 0)):
            pairs = []
            for place in range(count):
                line = [place * along + i for i in range(along)]
                pairs += [(line[i], line[i + 1]) for i in range(first, along - 1, 2)]
                if paced and first and place + beside < count and place // beside % 2 == 0:
                    ends = [0] + [along - 1] * (along % 2 == 0)
                    pairs += [(line[i], line[i] + beside * along) for i in ends]
            result.append(lax.ppermute(value, ("gz", "bx", "by"), pairs + [(j, i) for i, j in pairs]))
        return result

    line = (1, psf_z.shape[0])
    psf_z, psf_x, psf_y = psf_z.reshape(line), psf_x.reshape(line), psf_y.reshape(line)
    order = pltpu.VMEM((2, columns, columns + 2 * radius), F32)
    block = sum(chunks)
    pieces = 4
    seen, sibling, other, *parcels = call(
        1.3,
        functools.partial(start_kernel, parts, radius, count),
        [shaped(columns, length), shaped(radius, length), shaped(radius, length)]
        + [shaped(block + sum(chunks[1:]), length)] * count,
        [HBM, HBM],
        [order, pltpu.VMEM(line, F32), pltpu.VMEM((length, columns), F32), pltpu.SemaphoreType.DMA((pieces + 1,))],
    )(stays(psf_y), stays(observed.reshape(length, columns)))
    seen_sides = from_sides(sibling, other)
    parcels = exchanged(parcels)

    def left(rows, width):
        return jax.ShapeDtypeStruct((rows, 3 * width), BF16)

    def right(rows, width):
        return jax.ShapeDtypeStruct((3 * rows, width), BF16)

    span = 2 * radius // len(parts)
    across = LANES // rows * width
    first, back_early, back_late, ahead_early, ahead_late, ahead_rest, end_early, end_late, *weights = call(
        0.8,
        functools.partial(weights_kernel, sizes, parts),
        [
            left(size_of(parts[0]), columns + 2 * radius),
            left(columns + 2 * radius, columns + 4 * radius - 2 * span),
            left(4 * radius, 2 * span),
            left(columns, columns - 2 * radius),
            left(size_of(parts[0]), 4 * radius),
            left(size_of(parts[-1]), 4 * radius),
            left(columns, columns),
            left(2 * radius, 2 * radius),
            right(beside * LANES, across),
            right(across, beside * LANES),
            left(groups * planes, groups * planes),
            left(groups * planes, groups * planes),
        ],
        [VMEM] * 3,
        [order],
    )(psf_z, psf_x, psf_y)
    outer = exchanged(
        call(
            0.8,
            first_y_kernel,
            [shaped(chunks[0], length)] * count,
            [VMEM] * 4,
        )(first, seen, *seen_sides)
    )

    def through_planes(values, first, chunk, seen_values, seen_first=None):
        lines = groups * planes * chunk
        across = (width // LANES, lines + chunk, LANES)
        begins = seen_first is not None
        result = call(
            50,
            functools.partial(planes_kernel, sizes, first, seen_first),
            [shaped(chunk, length)] * count + [shaped(*across)] * begins,
            [VMEM] * (4 + len(values) + len(seen_values)),
            [
                pltpu.VMEM((beside, groups * (length // LANES) * chunk, LANES), F32),
                pltpu.VMEM(across, F32),
                pltpu.VMEM(across, F32),
            ],
        )(*weights, *values, *seen_values)
        return result[:count], result[count:] if begins else seen_values

    def sides_of(cost, values, span, after, paced=False):
        sides = call(
            cost,
            functools.partial(sides_kernel, count),
            [shaped(span, length)] * 2,
            [VMEM] * (count + 1),
        )(*values, after)
        return from_sides(*sides, paced)

    fields, across, sides = ([None] * len(parts) for _ in range(3))
    before = 0
    for k in reversed(range(len(parts))):
        values, first = (parcels, before + chunks[k]) if k else (outer, 0)
        fields[k], across[k] = through_planes(values, first, chunks[k], parcels, before)
        fields[k] = exchanged(fields[k])
        before += chunks[k] * (2 if k else 1)
    for k in reversed(range(len(parts))):
        sides[k] = sides_of(50, fields[k], span, fields[0][0], k == 0)
    partial = [shaped(4 * radius, length), shaped(columns - 2 * radius, length), shaped(columns, length)]
    partial = call(
        2.2,
        functools.partial(middle_early_kernel, parts, radius, count),
        partial,
        [VMEM] * (1 + (count + 2) * len(parts)),
        [pltpu.VMEM((size_of(runs), length), F32) for runs in parts],
    )(back_early, ahead_early, *flat(fields), *flat(sides[1:]), seen)
    estimate, *values = call(
        0.8,
        functools.partial(middle_late_kernel, parts, radius, count),
        [shaped(4 * radius, length)] + [shaped(chunks[0], length)] * count,
        [VMEM] * 9,
    )(back_late, ahead_late, *sides[0], partial[0], partial[2], seen, *seen_sides)
    fields[0] = exchanged(values)
    estimate, *values = call(
        50,
        functools.partial(middle_rest_kernel, parts, radius),
        [shaped(columns, length)] + [shaped(chunk, length) for chunk in chunks[1:] for _ in range(count)],
        [VMEM] * 5,
    )(ahead_rest, estimate, *partial[1:], fields[0][0])
    if len(parts) > 1:
        fields[1] = exchanged(values)
    for k in range(len(parts)):
        values, _ = through_planes(fields[k], 0, chunks[k], across[k])
        fields[k] = exchanged(values)
    sides = sides_of(0.6, fields[0], radius, fields[-1][0])
    partial = call(
        50,
        functools.partial(last_early_kernel, parts, radius, count),
        [shaped(2 * radius, length), shaped(columns - 2 * radius, length)],
        [VMEM] * (2 + count * len(parts)),
        [pltpu.VMEM((size_of(runs), length), F32) for runs in parts],
    )(end_early, estimate, *flat(fields))
    out = call(
        1.5,
        functools.partial(last_late_kernel, radius, count),
        shaped(length, columns),
        [VMEM] * 6,
        [pltpu.VMEM((length, columns), F32), pltpu.SemaphoreType.DMA((2 * pieces,))],
        HBM,
    )(end_late, *sides, *partial, estimate)
    return out.reshape(planes, rows, columns)


def solution(mesh):
    placed = (P("gz", "bx", "by"), P(), P(), P())
    return jax.shard_map(
        per_device, mesh=mesh, in_specs=placed, out_specs=P("gz", "bx", "by"), check_vma=False
    )
```
